256 devices in a mesh: dp: 32 (over z, x_hi, core), tensor: 8 (over x_lo, y).
Axes of the slice: x: 4 (x_hi: 2, x_lo: 2; x = x_hi * 2 + x_lo), y: 4, z: 8, core: 2. Of those that a mesh axis runs over, the one named last changes fastest.
Arguments:
- tokens: bfloat16 [32768, 4096], P(('dp', 'tensor')), may hold values from -6 to 6
- norm_gain: float32 [4096], replicated, may hold values from 0.25 to 1.75
- norm_bias: float32 [4096], replicated, may hold values from -3 to 3
- qkv_weight: bfloat16 [4096, 6144], P('dp', 'tensor'), may hold values from -8 to 8
- out_weight: bfloat16 [2048, 4096], P('tensor', 'dp'), may hold values from -0.125 to 0.125
- match_weight: bfloat16 [4096, 512], P('dp'), may hold values from -0.09375 to 0.09375
- matcher_qkv: bfloat16 [512, 1536], replicated, may hold values from -12 to 12
- matcher_out: bfloat16 [512, 512], replicated, may hold values from -0.25 to 0.25
Outputs:
- features: bfloat16 [32768, 4096], P(('dp', 'tensor'))
- matched: bfloat16 [32768, 512], P(('dp', 'tensor'))
The draws below stay inside these ranges and needn't reach their ends.
All inputs are finite; a program needn't handle non-finite values.
Results may differ from the reference program's by a relative error of at most 0.014.
Values may be sent and summed in bfloat16 or wider, within the bound.
No kernel may reach another device: no remote copies, remote signals or barrier semaphores. Data moves between devices by JAX's collectives and lax.ppermute only.
A program may use at most 128 MiB of HBM per device.

```python
import math
import jax
import jax.numpy as jnp
from jax import lax

D = 4096
HEADS = 16
HEAD_DIM = 128
IMAGE_PATCHES = 1024
MATCH_WIDTH = 512
MATCH_HEADS = 8
MATCH_HEAD_SIZE = 64
IMAGES = 32
TOKENS = 32768
N_DP = 32


def draw_tokens(key, part):
    key = jax.random.fold_in(key, 11)
    stacked = jnp.clip(jax.random.normal(key, (IMAGES, IMAGE_PATCHES, D), jnp.float32), -6.0, 6.0)
    return stacked.reshape(TOKENS, D).astype(jnp.bfloat16)


def draw_qkv_weight(key, part):
    key = jax.random.fold_in(key, 23)
    random_base_key = jax.random.fold_in(key, 0)
    weight_matrix = jnp.clip(jax.random.normal(random_base_key, (D, HEADS, 3, HEAD_DIM), jnp.float32), -6.0, 6.0) / math.sqrt(D)
    return weight_matrix.reshape(D, 3 * HEADS * HEAD_DIM).astype(jnp.bfloat16)


def draw_matcher_qkv(key, part):
    key = jax.random.fold_in(key, 37)
    random_base_key = jax.random.fold_in(key, 0)
    weight_matrix = jnp.clip(jax.random.normal(random_base_key, (MATCH_WIDTH, 3, MATCH_HEADS, MATCH_HEAD_SIZE), jnp.float32), -6.0, 6.0) / math.sqrt(MATCH_WIDTH)
    return weight_matrix.reshape(MATCH_WIDTH, 3 * MATCH_WIDTH).astype(jnp.bfloat16)


def level_of(key, dims, shards, smallest, high):
    loudness = 1.0
    for position, blocks in shards:
        steps = jax.random.uniform(jax.random.fold_in(jax.random.fold_in(key, 6), position), (blocks,), jnp.float32, smallest / len(shards), high / len(shards))
        loudness = loudness * jnp.repeat(jnp.exp(steps), dims[position] // blocks).reshape((-1,) + (1,) * (len(dims) - 1 - position))
    return loudness


def bell_draw(key, shape, deviation, most, cuts=(), kind=jnp.bfloat16):
    drawn = deviation * jax.random.normal(key, shape, jnp.float32)
    if cuts:
        drawn = drawn * level_of(key, shape, cuts, -0.22, 0.18)
    return jnp.clip(drawn, -most, most).astype(kind)


def setup_inputs(seed: int = 0) -> dict:
    splits = jax.random.split(jax.random.key(seed), 9)
    tokens = draw_tokens(jax.random.fold_in(splits[8], 71), 0)
    norm_gain = jnp.clip(1.0 + 0.15 * jax.random.normal(splits[1], (D,), jnp.float32), 0.25, 1.75)
    norm_bias = bell_draw(splits[2], (D,), 0.5, 3.0, (), jnp.float32)
    qkv_weight = draw_qkv_weight(jax.random.fold_in(splits[8], 71), 0)
    out_weight = bell_draw(splits[4], (HEADS * HEAD_DIM, D), (HEADS * HEAD_DIM) ** -0.5, 0.125, ((0, 8), (1, 32)))
    match_weight = bell_draw(splits[5], (D, MATCH_WIDTH), D ** -0.5, 0.09375, ((0, 32),))
    matcher_qkv = draw_matcher_qkv(jax.random.fold_in(splits[8], 71), 0)
    matcher_out = bell_draw(splits[7], (MATCH_WIDTH, MATCH_WIDTH), MATCH_WIDTH ** -0.5, 0.25)
    return {"tokens": tokens, "norm_gain": norm_gain, "norm_bias": norm_bias, "qkv_weight": qkv_weight, "out_weight": out_weight, "match_weight": match_weight, "matcher_qkv": matcher_qkv, "matcher_out": matcher_out}


def layer_norm(rows_in, norm_gain, norm_bias):
    values = rows_in.astype(jnp.float32)
    center = lax.optimization_barrier(jnp.mean(values, axis=-1, keepdims=True))
    spread = lax.optimization_barrier(jnp.mean((values - center) ** 2, axis=-1, keepdims=True))
    return ((values - center) * lax.rsqrt(spread + 1e-06) * norm_gain + norm_bias).astype(jnp.bfloat16)

def attend_tokens(queries, keys, values, score_scale):
    scores = jnp.einsum('qhd,khd->hqk', queries.astype(jnp.float32), keys.astype(jnp.float32)) * score_scale
    probs = jax.nn.softmax(scores, axis=-1).astype(jnp.bfloat16)
    mixed_output = jnp.einsum('hqk,khd->qhd', probs.astype(jnp.float32), values.astype(jnp.float32))
    return mixed_output.astype(jnp.bfloat16)

def reference(tokens, norm_gain, norm_bias, qkv_weight, out_weight, match_weight, matcher_qkv, matcher_out):
    images = tokens.reshape(N_DP, IMAGE_PATCHES, D)

    def backbone(image_rows):
        normed = layer_norm(image_rows, norm_gain, norm_bias)
        projected = jnp.dot(normed, qkv_weight, preferred_element_type=jnp.float32).astype(jnp.bfloat16)
        projected = projected.reshape(IMAGE_PATCHES, HEADS, 3, HEAD_DIM)
        attended = attend_tokens(projected[:, :, 0], projected[:, :, 1], projected[:, :, 2], 1.0 / math.sqrt(HEAD_DIM))
        attended = attended.reshape(IMAGE_PATCHES, HEADS * HEAD_DIM)
        summed = jnp.dot(attended, out_weight, preferred_element_type=jnp.float32)
        features = (image_rows.astype(jnp.float32) + summed).astype(jnp.bfloat16)
        descriptor = jnp.dot(features, match_weight, preferred_element_type=jnp.float32).astype(jnp.bfloat16)
        return (features, descriptor)
    features, descriptors = lax.map(backbone, images)
    partners = jnp.roll(descriptors, N_DP // 2, axis=0)

    def matcher(pair):
        own_rows, other_rows = pair
        matcher_queries = jnp.dot(own_rows, matcher_qkv[:, :MATCH_WIDTH], preferred_element_type=jnp.float32).astype(jnp.bfloat16)
        matcher_keys = jnp.dot(other_rows, matcher_qkv[:, MATCH_WIDTH:2 * MATCH_WIDTH], preferred_element_type=jnp.float32).astype(jnp.bfloat16)
        matcher_values = jnp.dot(other_rows, matcher_qkv[:, 2 * MATCH_WIDTH:], preferred_element_type=jnp.float32).astype(jnp.bfloat16)
        mixed_output = attend_tokens(matcher_queries.reshape(IMAGE_PATCHES, MATCH_HEADS, MATCH_HEAD_SIZE), matcher_keys.reshape(IMAGE_PATCHES, MATCH_HEADS, MATCH_HEAD_SIZE), matcher_values.reshape(IMAGE_PATCHES, MATCH_HEADS, MATCH_HEAD_SIZE), 1.0 / math.sqrt(MATCH_HEAD_SIZE))
        mixed_output = mixed_output.reshape(IMAGE_PATCHES, MATCH_WIDTH)
        result = own_rows.astype(jnp.float32) + jnp.dot(mixed_output, matcher_out, preferred_element_type=jnp.float32)
        return result.astype(jnp.bfloat16)
    matched = lax.map(matcher, (descriptors, partners))
    return (features.reshape(TOKENS, D), matched.reshape(TOKENS, MATCH_WIDTH))
```

```python
import itertools
import math

import jax
import jax.numpy as jnp
from jax import lax
from jax.sharding import Mesh
from jax.sharding import PartitionSpec as P

HEAD_DIM = 128
MATCH_HEADS = 8
AXES = ("z", "xh", "core", "xl", "y")
SIZES = (8, 2, 2, 2, 4)


def moved(block, target):
    def index(place):
        at = 0
        for axis, size in zip(AXES, SIZES):
            at = at * size + place[axis]
        return at

    route = []
    for values in itertools.product(*[range(size) for size in SIZES]):
        place = dict(zip(AXES, values))
        route.append((index(place), index({**place, **target(place)})))
    return lax.ppermute(block, AXES, route)


def along_y(k):
    return lambda p: {"y": (p["y"] + k) % 4}


def along_z(k):
    return lambda p: {"z": (p["z"] + k) % 8}


def along_x(k):
    def target(p):
        x = (p["xh"] * 2 + p["xl"] + k) % 4
        return {"xh": x // 2, "xl": x % 2}

    return target


def other_core(p):
    return {"core": 1 - p["core"]}


def swapped_roles(block):
    return moved(block, lambda p: {"core": p["xl"], "xl": p["core"]})


def ring(block, step, count):
    half = block.shape[0] // 2
    up = down = block
    found = [(0, 0, block)]
    for s in range(1, count // 2):
        up, down = moved(up, step(1)), moved(down, step(-1))
        found += [(-s, 0, up), (s, 0, down)]
    found.append((-(count // 2), 0, moved(up[:half], step(1))))
    found.append((count // 2, half, moved(down[half:], step(-1))))
    return found


def layer_norm(rows_in, norm_gain, norm_bias):
    values = rows_in.astype(jnp.float32)
    center = jnp.mean(values, axis=-1, keepdims=True)
    spread = jnp.mean((values - center) ** 2, axis=-1, keepdims=True)
    return ((values - center) * lax.rsqrt(spread + 1e-06) * norm_gain + norm_bias).astype(
        jnp.bfloat16
    )


def attend_tokens(queries, keys, values, score_scale):
    scores = (
        jnp.einsum("qhd,khd->hqk", queries, keys, preferred_element_type=jnp.float32) * score_scale
    )
    probs = jax.nn.softmax(scores, axis=-1).astype(jnp.bfloat16)
    mixed_output = jnp.einsum("hqk,khd->qhd", probs, values, preferred_element_type=jnp.float32)
    return mixed_output.astype(jnp.bfloat16)


def per_device(
    tokens, norm_gain, norm_bias, qkv_weight, out_weight, match_weight, matcher_qkv, matcher_out
):
    bf16, f32 = jnp.bfloat16, jnp.float32
    z, y, core = lax.axis_index("z"), lax.axis_index("y"), lax.axis_index("core")
    x = lax.axis_index("xh") * 2 + lax.axis_index("xl")
    width = matcher_out.shape[0]
    rows, features_width = tokens.shape

    tokens = swapped_roles(tokens)
    qkv_weight = swapped_roles(qkv_weight)
    out_weight = swapped_roles(out_weight)

    normed = layer_norm(tokens, norm_gain, norm_bias)
    all_normed = lax.all_gather(normed, ("core", "y"), axis=0, tiled=True)

    block = qkv_weight.shape[0]
    columns = qkv_weight.shape[1]
    half = columns // 2
    weights = jnp.zeros((8, 4, block, columns), bf16)
    by_x = jnp.zeros((4, block, half), bf16)
    for dx, first, part in ring(qkv_weight[:, :half], along_x, 4):
        by_x = lax.dynamic_update_slice(by_x, part[None], ((x + dx) % 4, first, 0))
    by_z = jnp.zeros((8, block, half), bf16)
    for dz, first, part in ring(qkv_weight[:, half:], along_z, 8):
        by_z = lax.dynamic_update_slice(by_z, part[None], ((z + dz) % 8, first, 0))
    for dz, first, part in ring(by_x, along_z, 8):
        weights = lax.dynamic_update_slice(weights, part[None], ((z + dz) % 8, first, 0, 0))
    for dx, first, part in ring(by_z, along_x, 4):
        weights = lax.dynamic_update_slice(
            weights, part[:, None], (first, (x + dx) % 4, 0, half)
        )
    weights = weights.reshape(32 * block, columns)

    projected = jnp.dot(all_normed, weights, preferred_element_type=f32).astype(bf16)
    local_heads = columns // (3 * HEAD_DIM)
    patch_count = projected.shape[0]
    projected = projected.reshape(patch_count, local_heads, 3, HEAD_DIM)
    attended = attend_tokens(
        projected[:, :, 0], projected[:, :, 1], projected[:, :, 2], 1.0 / math.sqrt(HEAD_DIM)
    )
    attended = attended.reshape(2, patch_count // 2, local_heads * HEAD_DIM)

    out_z = jnp.zeros((8, 1, out_weight.shape[0], out_weight.shape[1]), bf16)
    for dz, first, part in ring(out_weight, along_z, 8):
        out_z = lax.dynamic_update_slice(out_z, part[None, None], ((z + dz) % 8, 0, first, 0))
    out_own = jnp.zeros((8, 4, out_weight.shape[0], out_weight.shape[1]), bf16)
    for dx, first, part in ring(out_z, along_x, 4):
        out_own = lax.dynamic_update_slice(out_own, part, (first, (x + dx) % 4, 0, 0))
    out_own = out_own.reshape(32, out_weight.shape[0], out_weight.shape[1])
    out_own = out_own.transpose(1, 0, 2).reshape(out_weight.shape[0], features_width)
    out_both = jnp.concatenate([out_own, moved(out_own, other_core)], axis=0)

    mine = lax.dynamic_index_in_dim(attended, core, 0, keepdims=False)
    theirs = lax.dynamic_index_in_dim(attended, 1 - core, 0, keepdims=False)
    both = jnp.concatenate([mine, moved(theirs, other_core)], axis=1)

    def term(dy):
        start = ((y + dy) % 4) * rows
        picked = lax.dynamic_slice_in_dim(both, start, rows, axis=0)
        return jnp.dot(picked, out_both, preferred_element_type=f32)

    far = term(2).astype(bf16)
    mid = rows // 2
    far_up = moved(far[:mid], along_y(1))
    far_down = moved(far[mid:], along_y(-1))
    near_up, near_down = term(1), term(-1)
    near_up = jnp.concatenate([near_up[:mid] + far_up.astype(f32), near_up[mid:]], axis=0)
    near_down = jnp.concatenate([near_down[:mid], near_down[mid:] + far_down.astype(f32)], axis=0)
    from_below = moved(near_up.astype(bf16), along_y(1))
    from_above = moved(near_down.astype(bf16), along_y(-1))
    summed = term(0) + from_below.astype(f32) + from_above.astype(f32)
    features = (tokens.astype(f32) + summed).astype(bf16)

    other_half = moved(
        match_weight, lambda p: {"xh": 1 - p["xh"], "xl": 1 - p["xl"]}
    )
    xh = lax.axis_index("xh")
    match_pair = jnp.where(
        xh == 0,
        jnp.concatenate([match_weight, other_half], axis=0),
        jnp.concatenate([other_half, match_weight], axis=0),
    ).reshape(2, 1, match_weight.shape[0], width)
    match_all = lax.all_gather(match_pair, ("z", "core"), axis=0, tiled=False)
    match_all = match_all.reshape(8, 2, 2, match_weight.shape[0], width)
    match_all = match_all.transpose(0, 2, 1, 3, 4).reshape(features_width, width)

    descriptor = jnp.dot(features, match_all, preferred_element_type=f32).astype(bf16)
    partner = moved(descriptor, along_z(4))
    matcher_queries = jnp.dot(
        descriptor, matcher_qkv[:, :width], preferred_element_type=f32
    ).astype(bf16)
    quarter = jnp.concatenate([partner] + [moved(partner, along_y(k)) for k in (1, 2, 3)], axis=0)
    partner_rows = jnp.concatenate([quarter, moved(quarter, other_core)], axis=0)
    key_values = jnp.dot(partner_rows, matcher_qkv[:, width:], preferred_element_type=f32).astype(
        bf16
    )
    key_count = key_values.shape[0]
    head_width = width // MATCH_HEADS
    mixed_output = attend_tokens(
        matcher_queries.reshape(rows, MATCH_HEADS, head_width),
        key_values[:, :width].reshape(key_count, MATCH_HEADS, head_width),
        key_values[:, width:].reshape(key_count, MATCH_HEADS, head_width),
        1.0 / math.sqrt(head_width),
    )
    mixed_output = mixed_output.reshape(rows, width)
    matched = descriptor.astype(f32) + jnp.dot(
        mixed_output, matcher_out, preferred_element_type=f32
    )
    return (swapped_roles(features), swapped_roles(matched.astype(bf16)))


def solution(mesh):
    fine = Mesh(mesh.devices.reshape(SIZES), AXES)
    dp, tensor = ("z", "xh", "core"), ("xl", "y")
    return jax.shard_map(
        per_device,
        mesh=fine,
        in_specs=(
            P(AXES, None),
            P(),
            P(),
            P(dp, tensor),
            P(tensor, dp),
            P(dp, None),
            P(),
            P(),
        ),
        out_specs=(P(AXES, None), P(AXES, None)),
        check_vma=False,
    )
```

```python
import itertools
import math

import jax
import jax.numpy as jnp
from jax import lax
from jax.sharding import Mesh
from jax.sharding import PartitionSpec as P

HEAD_DIM = 128
MATCH_HEADS = 8
AXES = ("z", "xh", "core", "xl", "y")
SIZES = (8, 2, 2, 2, 4)


def moved(block, target):
    def index(place):
        at = 0
        for axis, size in zip(AXES, SIZES):
            at = at * size + place[axis]
        return at

    route = []
    for values in itertools.product(*[range(size) for size in SIZES]):
        place = dict(zip(AXES, values))
        route.append((index(place), index({**place, **target(place)})))
    return lax.ppermute(block, AXES, route)


def along_y(k):
    return lambda p: {"y": (p["y"] + k) % 4}


def along_z(k):
    return lambda p: {"z": (p["z"] + k) % 8}


def two_along_z(p):
    return {"z": (p["z"] + 2 - 4 * (p["z"] % 2)) % 8}


def along_x(k):
    def target(p):
        x = (p["xh"] * 2 + p["xl"] + k) % 4
        return {"xh": x // 2, "xl": x % 2}

    return target


def other_core(p):
    return {"core": 1 - p["core"]}


def swapped_roles(block):
    return moved(block, lambda p: {"core": p["xl"], "xl": p["core"]})


def gathered_z(block, z):
    pair = jnp.stack([block, moved(block, along_z(4))])
    pairs = [pair, moved(pair, along_z(1)), moved(pair, along_z(-1)), moved(pair, two_along_z)]
    sign = 1 - 2 * (z % 2)
    whole = jnp.zeros((2, 4) + block.shape, block.dtype)
    rest = (0,) * block.ndim
    for k, pair in zip((0, 1, -1, 2 * sign), pairs):
        owner = (z - k) % 8
        low = jnp.where(owner < 4, pair, pair[::-1])
        whole = lax.dynamic_update_slice(whole, low[:, None], (0, owner % 4) + rest)
    return whole.reshape((8,) + block.shape)


def gathered_x(block, x, axis):
    whole = jnp.zeros(block.shape[:axis] + (4,) + block.shape[axis:], block.dtype)
    for k, part in [(0, block)] + [(k, moved(block, along_x(k))) for k in (1, -1, 2)]:
        at = [0] * whole.ndim
        at[axis] = (x - k) % 4
        whole = lax.dynamic_update_slice(whole, jnp.expand_dims(part, axis), at)
    return whole


def layer_norm(rows_in, norm_gain, norm_bias):
    values = rows_in.astype(jnp.float32)
    center = jnp.mean(values, axis=-1, keepdims=True)
    spread = jnp.mean((values - center) ** 2, axis=-1, keepdims=True)
    return ((values - center) * lax.rsqrt(spread + 1e-06) * norm_gain + norm_bias).astype(
        jnp.bfloat16
    )


def attend_tokens(queries, keys, values, score_scale):
    scores = (
        jnp.einsum("qhd,khd->hqk", queries, keys, preferred_element_type=jnp.float32) * score_scale
    )
    probs = jax.nn.softmax(scores, axis=-1).astype(jnp.bfloat16)
    mixed_output = jnp.einsum("hqk,khd->qhd", probs, values, preferred_element_type=jnp.float32)
    return mixed_output.astype(jnp.bfloat16)


def per_device(
    tokens, norm_gain, norm_bias, qkv_weight, out_weight, match_weight, matcher_qkv, matcher_out
):
    bf16, f32 = jnp.bfloat16, jnp.float32
    z, core = lax.axis_index("z"), lax.axis_index("core")
    x = lax.axis_index("xh") * 2 + lax.axis_index("xl")
    width = matcher_out.shape[0]
    rows, features_width = tokens.shape

    tokens = swapped_roles(tokens)
    qkv_weight = swapped_roles(qkv_weight)
    out_weight = swapped_roles(out_weight)

    normed = layer_norm(tokens, norm_gain, norm_bias)
    mid = rows // 2
    below, above = moved(normed, along_y(1)), moved(normed, along_y(-1))
    opposite = [moved(below[:mid], along_y(1)), moved(above[mid:], along_y(-1))]
    near = jnp.concatenate([normed, below, above], axis=0)
    far = jnp.concatenate(opposite, axis=0)
    own_half = [near, far]
    other_half = [moved(near, other_core), moved(far, other_core)]
    all_normed = jnp.concatenate(own_half + other_half, axis=0)

    block, columns = qkv_weight.shape
    half = columns // 2
    wide = out_weight.shape[1]
    first = qkv_weight[:, :half].reshape(block, half // wide, wide).transpose(1, 0, 2)
    packed = jnp.concatenate([first.reshape(-1, wide), out_weight], axis=0)
    packed = gathered_x(packed, x, 0)
    first = packed[:, : first.shape[0] * block].reshape(4, half // wide, block, wide)
    first = first.transpose(0, 2, 1, 3).reshape(4 * block, half)
    first = lax.all_gather(first, "z", axis=0, tiled=True)
    second = gathered_x(gathered_z(qkv_weight[:, half:], z), x, 1).reshape(32 * block, half)

    def head(weight):
        projected = jnp.dot(all_normed, weight, preferred_element_type=f32).astype(bf16)
        parts = projected.reshape(projected.shape[0], 1, 3, HEAD_DIM)
        return attend_tokens(parts[:, :, 0], parts[:, :, 1], parts[:, :, 2], 1 / math.sqrt(HEAD_DIM))

    attended = jnp.concatenate([head(first), head(second)], axis=1)
    patch_count = attended.shape[0]
    attended = attended.reshape(2, patch_count // 2, -1)

    out_own = gathered_z(packed[:, -out_weight.shape[0] :], z)
    out_own = out_own.reshape(32, out_weight.shape[0], out_weight.shape[1])
    out_own = out_own.transpose(1, 0, 2).reshape(out_weight.shape[0], features_width)
    out_both = jnp.concatenate([out_own, moved(out_own, other_core)], axis=0)

    both = jnp.concatenate([attended[0], moved(attended[1], other_core)], axis=1)
    places = {0: 0, -1: rows, 1: 2 * rows, 2: 3 * rows}

    def term(dy):
        picked = both[places[dy] : places[dy] + rows]
        return jnp.dot(picked, out_both, preferred_element_type=f32)

    far = term(2).astype(bf16)
    far_up = moved(far[:mid], along_y(1))
    far_down = moved(far[mid:], along_y(-1))
    near_up, near_down = term(1), term(-1)
    near_up = jnp.concatenate([near_up[:mid] + far_up.astype(f32), near_up[mid:]], axis=0)
    near_down = jnp.concatenate([near_down[:mid], near_down[mid:] + far_down.astype(f32)], axis=0)
    from_below = moved(near_up.astype(bf16), along_y(1))
    from_above = moved(near_down.astype(bf16), along_y(-1))
    summed = term(0) + from_below.astype(f32) + from_above.astype(f32)
    features = (tokens.astype(f32) + summed).astype(bf16)

    other_half = moved(
        match_weight, lambda p: {"xh": 1 - p["xh"], "xl": 1 - p["xl"]}
    )
    xh = lax.axis_index("xh")
    match_pair = jnp.where(
        xh == 0,
        jnp.concatenate([match_weight, other_half], axis=0),
        jnp.concatenate([other_half, match_weight], axis=0),
    ).reshape(2, 1, match_weight.shape[0], width)
    match_own = lax.all_gather(match_pair, "z", axis=0, tiled=False)
    match_own = match_own.reshape(16, match_weight.shape[0], width)
    match_other = moved(match_own, other_core)
    match_all = jnp.where(
        core == 0,
        jnp.stack([match_own, match_other], axis=1),
        jnp.stack([match_other, match_own], axis=1),
    ).reshape(features_width, width)

    descriptor = jnp.dot(features, match_all, preferred_element_type=f32).astype(bf16)
    partner = moved(descriptor, along_z(4))
    matcher_queries = jnp.dot(
        descriptor, matcher_qkv[:, :width], preferred_element_type=f32
    ).astype(bf16)
    quarter = jnp.concatenate([partner] + [moved(partner, along_y(k)) for k in (1, 2, 3)], axis=0)
    partner_rows = jnp.concatenate([quarter, moved(quarter, other_core)], axis=0)
    key_values = jnp.dot(partner_rows, matcher_qkv[:, width:], preferred_element_type=f32).astype(
        bf16
    )
    key_count = key_values.shape[0]
    head_width = width // MATCH_HEADS
    mixed_output = attend_tokens(
        matcher_queries.reshape(rows, MATCH_HEADS, head_width),
        key_values[:, :width].reshape(key_count, MATCH_HEADS, head_width),
        key_values[:, width:].reshape(key_count, MATCH_HEADS, head_width),
        1.0 / math.sqrt(head_width),
    )
    mixed_output = mixed_output.reshape(rows, width)
    matched = descriptor.astype(f32) + jnp.dot(
        mixed_output, matcher_out, preferred_element_type=f32
    )
    return (swapped_roles(features), swapped_roles(matched.astype(bf16)))


def solution(mesh):
    fine = Mesh(mesh.devices.reshape(SIZES), AXES)
    dp, tensor = ("z", "xh", "core"), ("xl", "y")
    return jax.shard_map(
        per_device,
        mesh=fine,
        in_specs=(
            P(AXES, None),
            P(),
            P(),
            P(dp, tensor),
            P(tensor, dp),
            P(dp, None),
            P(),
            P(),
        ),
        out_specs=(P(AXES, None), P(AXES, None)),
        check_vma=False,
    )
```

```python
import itertools
import math

import jax
import jax.numpy as jnp
from jax import lax
from jax.experimental import pallas as pl
from jax.experimental.pallas import tpu as pltpu
from jax.sharding import Mesh
from jax.sharding import PartitionSpec as P

HEAD_DIM = 128
MATCH_HEADS = 8
AXES = ("z", "xh", "core", "xl", "y")
SIZES = (8, 2, 2, 2, 4)


def moved(block, target):
    def index(place):
        at = 0
        for axis, size in zip(AXES, SIZES):
            at = at * size + place[axis]
        return at

    route = []
    for values in itertools.product(*[range(size) for size in SIZES]):
        place = dict(zip(AXES, values))
        route.append((index(place), index({**place, **target(place)})))
    return lax.ppermute(block, AXES, route)


def along_y(k):
    return lambda p: {"y": (p["y"] + k) % 4}


def along_z(k):
    return lambda p: {"z": (p["z"] + k) % 8}


def two_along_z(p):
    return {"z": (p["z"] + 2 - 4 * (p["z"] % 2)) % 8}


def along_x(k):
    def target(p):
        x = (p["xh"] * 2 + p["xl"] + k) % 4
        return {"xh": x // 2, "xl": x % 2}

    return target


def other_core(p):
    return {"core": 1 - p["core"]}


def swapped_roles(block):
    return moved(block, lambda p: {"core": p["xl"], "xl": p["core"]})


def gathered_z(block, z):
    pair = jnp.stack([block, moved(block, along_z(4))])
    pairs = [pair, moved(pair, along_z(1)), moved(pair, along_z(-1)), moved(pair, two_along_z)]
    sign = 1 - 2 * (z % 2)
    whole = jnp.zeros((2, 4) + block.shape, block.dtype)
    rest = (0,) * block.ndim
    for k, pair in zip((0, 1, -1, 2 * sign), pairs):
        owner = (z - k) % 8
        low = jnp.where(owner < 4, pair, pair[::-1])
        whole = lax.dynamic_update_slice(whole, low[:, None], (0, owner % 4) + rest)
    return whole.reshape((8,) + block.shape)


def gathered_x(block, x, axis):
    whole = jnp.zeros(block.shape[:axis] + (4,) + block.shape[axis:], block.dtype)
    for k, part in [(0, block)] + [(k, moved(block, along_x(k))) for k in (1, -1, 2)]:
        at = [0] * whole.ndim
        at[axis] = (x - k) % 4
        whole = lax.dynamic_update_slice(whole, jnp.expand_dims(part, axis), at)
    return whole


def layer_norm(rows_in, norm_gain, norm_bias):
    values = rows_in.astype(jnp.float32)
    center = jnp.mean(values, axis=-1, keepdims=True)
    spread = jnp.mean((values - center) ** 2, axis=-1, keepdims=True)
    return ((values - center) * lax.rsqrt(spread + 1e-06) * norm_gain + norm_bias).astype(
        jnp.bfloat16
    )


def local(kernel, out_shape, **kwargs):
    return pl.pallas_call(
        kernel,
        out_shape=out_shape,
        compiler_params=pltpu.CompilerParams(vmem_limit_bytes=48 << 20),
        **kwargs,
    )


def softmax_rows(scores):
    raised = jnp.exp(scores - jnp.max(scores, axis=-1, keepdims=True))
    return (raised * (1.0 / jnp.sum(raised, axis=-1, keepdims=True))).astype(jnp.bfloat16)


def dot(left, right):
    return jnp.dot(left, right, preferred_element_type=jnp.float32)


def dot_transposed(left, right):
    return lax.dot_general(
        left, right, (((1,), (1,)), ((), ())), preferred_element_type=jnp.float32
    )


PARTS = 4


def attention_kernel(*refs):
    pieces, (weight, own, other, held, held_weight, total, projected, sems) = refs[:-8], refs[-8:]
    depth = held.shape[1] // PARTS
    copies = []
    for part in range(PARTS):
        span = pl.ds(part * depth, depth)
        starting = [pltpu.make_async_copy(weight.at[span], held_weight.at[span], sems.at[part, 0])]
        at = 0
        for i, piece in enumerate(pieces):
            count = piece.shape[0]
            starting.append(
                pltpu.make_async_copy(
                    piece.at[:, span], held.at[pl.ds(at, count), span], sems.at[part, i + 1]
                )
            )
            at += count
        for copy in starting:
            copy.start()
        copies.append(starting)
    step = 256
    for part in range(PARTS):
        for copy in copies[part]:
            copy.wait()
        span = pl.ds(part * depth, depth)

        @pl.loop(0, held.shape[0], step=step)
        def _(row, part=part, span=span):
            rows = pl.ds(pl.multiple_of(row, step), step)
            term = dot(held[rows, span], held_weight[span, :])
            if part:
                term = total[rows, :] + term
            if part < PARTS - 1:
                total[rows, :] = term
            else:
                projected[rows, :] = term.astype(jnp.bfloat16)

    for head in range(2):
        at = head * 3 * HEAD_DIM
        for half, out in enumerate((own, other)):

            @pl.loop(0, out.shape[0], step=step)
            def _(row, at=at, half=half, out=out, head=head):
                rows = pl.ds(pl.multiple_of(half * out.shape[0] + row, step), step)
                scores = dot_transposed(
                    projected[rows, at : at + HEAD_DIM],
                    projected[:, at + HEAD_DIM : at + 2 * HEAD_DIM],
                ) * (1.0 / math.sqrt(HEAD_DIM))
                mixed = dot(
                    softmax_rows(scores), projected[:, at + 2 * HEAD_DIM : at + 3 * HEAD_DIM]
                )
                out[pl.ds(pl.multiple_of(row, step), step), pl.ds(head * HEAD_DIM, HEAD_DIM)] = (
                    mixed.astype(jnp.bfloat16)
                )


def attention(pieces, weight):
    count = sum(piece.shape[0] for piece in pieces)
    depth, columns = weight.shape
    result = jax.ShapeDtypeStruct((count // 2, columns // 3), jnp.bfloat16)
    return local(
        attention_kernel,
        (result, result),
        in_specs=[pl.BlockSpec(memory_space=pl.ANY)] * (len(pieces) + 1),
        out_specs=(pl.BlockSpec(memory_space=pltpu.VMEM),) * 2,
        scratch_shapes=[
            pltpu.VMEM((count, depth), jnp.bfloat16),
            pltpu.VMEM((depth, columns), jnp.bfloat16),
            pltpu.VMEM((count, columns), jnp.float32),
            pltpu.VMEM((count, columns), jnp.bfloat16),
            pltpu.SemaphoreType.DMA((PARTS, len(pieces) + 1)),
        ],
    )(*pieces, weight)


def out_kernel(mine, theirs, weight, other_weight, own, *others):
    blocks = range(weight.shape[0])
    matrix = jnp.concatenate(
        [jnp.concatenate([w[i] for i in blocks], axis=1) for w in (weight, other_weight)], axis=0
    )
    both = jnp.concatenate([mine[...], theirs[...]], axis=1)
    terms = dot(both, matrix)
    at = own.shape[0]
    own[...] = terms[:at]
    for out in others:
        out[...] = terms[at : at + out.shape[0]].astype(jnp.bfloat16)
        at += out.shape[0]


def out_projection(mine, theirs, weight, other_weight):
    count, wide = weight.shape[0], weight.shape[2]
    at_once = 4
    rows = mine.shape[0] // 4
    columns = at_once * wide
    width = count * wide
    own = jax.ShapeDtypeStruct((rows, width), jnp.float32)
    half = jax.ShapeDtypeStruct((rows // 2, width), jnp.bfloat16)
    whole = pl.BlockSpec(mine.shape, lambda i: (0, 0))
    weights = pl.BlockSpec((at_once,) + weight.shape[1:], lambda i: (i, 0, 0))
    return local(
        out_kernel,
        (own,) + (half,) * 6,
        grid=(count // at_once,),
        in_specs=[whole, whole, weights, weights],
        out_specs=(pl.BlockSpec((rows, columns), lambda i: (0, i)),)
        + (pl.BlockSpec((rows // 2, columns), lambda i: (0, i)),) * 6,
    )(mine, theirs, weight, other_weight)


def features_kernel(tokens, own, low_a, high_a, low_b, high_b, weight, features, descriptor, total):
    step = pl.program_id(0)
    summed = own[...]
    summed = summed + jnp.concatenate([low_a[...], high_a[...]], axis=0).astype(jnp.float32)
    summed = summed + jnp.concatenate([low_b[...], high_b[...]], axis=0).astype(jnp.float32)
    rounded = (tokens[...].astype(jnp.float32) + summed).astype(jnp.bfloat16)
    features[...] = rounded
    term = dot(rounded, weight[...])

    @pl.when(step == 0)
    def _():
        total[...] = term

    @pl.when(step > 0)
    def _():
        total[...] += term

    @pl.when(step == pl.num_programs(0) - 1)
    def _():
        descriptor[...] = total[...].astype(jnp.bfloat16)


def features_and_descriptor(tokens, own, halves, weight):
    rows, depth = tokens.shape
    width = weight.shape[1]
    wide = 1024
    whole = pl.BlockSpec((rows, wide), lambda i: (0, i))
    half = pl.BlockSpec((rows // 2, wide), lambda i: (0, i))
    return local(
        features_kernel,
        (
            jax.ShapeDtypeStruct((rows, depth), jnp.bfloat16),
            jax.ShapeDtypeStruct((rows, width), jnp.bfloat16),
        ),
        grid=(depth // wide,),
        in_specs=[whole, whole] + [half] * 4 + [pl.BlockSpec((wide, width), lambda i: (i, 0))],
        out_specs=(whole, pl.BlockSpec((rows, width), lambda i: (0, 0))),
        scratch_shapes=[pltpu.VMEM((rows, width), jnp.float32)],
    )(tokens, own, *halves, weight)


def matcher_kernel(*refs):
    descriptor, qkv, out_weight, *pieces, matched, keys, values, mixed = refs
    rows, width = descriptor.shape
    bf16 = jnp.bfloat16
    queries = dot(descriptor[...], qkv[:, :width]).astype(bf16)
    at = 0
    for piece in pieces:
        count = piece.shape[0]
        keys[at : at + count, :] = dot(piece[...], qkv[:, width : 2 * width]).astype(bf16)
        values[at : at + count, :] = dot(piece[...], qkv[:, 2 * width :]).astype(bf16)
        at += count
    head_width = width // MATCH_HEADS
    pair = 2 * head_width
    low = lax.broadcasted_iota(jnp.int32, (rows, pair), 1) < head_width
    for first in range(0, width, pair):
        span = slice(first, first + pair)
        two = queries[:, span]
        results = []
        for chosen in (low, jnp.logical_not(low)):
            asked = jnp.where(chosen, two, jnp.zeros_like(two))
            scores = dot_transposed(asked, keys[:, span]) * (1.0 / math.sqrt(head_width))
            results.append(dot(softmax_rows(scores), values[:, span]))
        mixed[:, span] = jnp.where(low, results[0], results[1]).astype(bf16)
    matched[...] = (descriptor[...].astype(jnp.float32) + dot(mixed[...], out_weight[...])).astype(
        bf16
    )


def match(descriptor, pieces, qkv, out_weight):
    count = sum(piece.shape[0] for piece in pieces)
    width = descriptor.shape[1]
    return local(
        matcher_kernel,
        jax.ShapeDtypeStruct(descriptor.shape, jnp.bfloat16),
        scratch_shapes=[
            pltpu.VMEM((count, width), jnp.bfloat16),
            pltpu.VMEM((count, width), jnp.bfloat16),
            pltpu.VMEM(descriptor.shape, jnp.bfloat16),
        ],
    )(descriptor, qkv, out_weight, *pieces)


def per_device(
    tokens, norm_gain, norm_bias, qkv_weight, out_weight, match_weight, matcher_qkv, matcher_out
):
    bf16, f32 = jnp.bfloat16, jnp.float32
    z, core = lax.axis_index("z"), lax.axis_index("core")
    x = lax.axis_index("xh") * 2 + lax.axis_index("xl")
    width = matcher_out.shape[0]
    rows, features_width = tokens.shape
    mid = rows // 2

    qkv_weight = swapped_roles(qkv_weight)
    qkv_weight = lax.all_gather(qkv_weight, ("z", "xh", "xl"), axis=0, tiled=True)
    tokens = swapped_roles(tokens)
    out_weight = swapped_roles(out_weight)

    normed = layer_norm(tokens, norm_gain, norm_bias)
    below, above = moved(normed, along_y(1)), moved(normed, along_y(-1))
    pieces = [normed, below, above]
    pieces += [moved(below[:mid], along_y(1)), moved(above[mid:], along_y(-1))]
    pieces += [moved(piece, other_core) for piece in pieces]
    mine, theirs = attention(pieces, qkv_weight)

    out_own = gathered_z(gathered_x(out_weight, x, 0), z)
    out_own = out_own.reshape((32,) + out_weight.shape)
    out_other = moved(out_own, other_core)
    theirs = moved(theirs, other_core)
    own, down_low, down_high, up_low, up_high, far_low, far_high = out_projection(
        mine, theirs, out_own, out_other
    )
    far_low, far_high = moved(far_low, along_y(1)), moved(far_high, along_y(-1))
    up_high, down_low = moved(up_high, along_y(1)), moved(down_low, along_y(-1))
    up_low = (up_low.astype(f32) + far_low.astype(f32)).astype(bf16)
    down_high = (down_high.astype(f32) + far_high.astype(f32)).astype(bf16)
    up_low, down_high = moved(up_low, along_y(1)), moved(down_high, along_y(-1))

    other_half = moved(match_weight, lambda p: {"xh": 1 - p["xh"], "xl": 1 - p["xl"]})
    match_pair = jnp.where(
        lax.axis_index("xh") == 0,
        jnp.concatenate([match_weight, other_half], axis=0),
        jnp.concatenate([other_half, match_weight], axis=0),
    )
    match_own = lax.all_gather(match_pair, "z", axis=0, tiled=True)
    match_own = match_own.reshape(16, match_weight.shape[0], width)
    match_other = moved(match_own, other_core)
    match_all = jnp.where(
        core == 0,
        jnp.stack([match_own, match_other], axis=1),
        jnp.stack([match_other, match_own], axis=1),
    ).reshape(features_width, width)

    features, descriptor = features_and_descriptor(
        tokens, own, (up_low, up_high, down_low, down_high), match_all
    )
    partner = moved(descriptor, along_z(4))
    pieces = [partner] + [moved(partner, along_y(k)) for k in (1, -1, 2)]
    pieces += [moved(piece, other_core) for piece in pieces]
    matched = match(descriptor, pieces, matcher_qkv, matcher_out)
    return (swapped_roles(features), swapped_roles(matched))


def solution(mesh):
    fine = Mesh(mesh.devices.reshape(SIZES), AXES)
    dp, tensor = ("z", "xh", "core"), ("xl", "y")
    return jax.shard_map(
        per_device,
        mesh=fine,
        in_specs=(
            P(AXES, None),
            P(),
            P(),
            P(dp, tensor),
            P(tensor, dp),
            P(dp, None),
            P(),
            P(),
        ),
        out_specs=(P(AXES, None), P(AXES, None)),
        check_vma=False,
    )
```

```python
import itertools
import math

import jax
import jax.numpy as jnp
from jax import lax
from jax.experimental import pallas as pl
from jax.experimental.pallas import tpu as pltpu
from jax.sharding import Mesh
from jax.sharding import PartitionSpec as P

HEAD_DIM = 128
MATCH_HEADS = 8
DISTANCES = (1, -1, 2)
LOG2_E = math.log2(math.e)
AXES = ("z", "xh", "core", "xl", "y")
SIZES = (8, 2, 2, 2, 4)


def moved(block, target):
    def index(place):
        at = 0
        for axis, size in zip(AXES, SIZES):
            at = at * size + place[axis]
        return at

    route = []
    for values in itertools.product(*[range(size) for size in SIZES]):
        place = dict(zip(AXES, values))
        route.append((index(place), index({**place, **target(place)})))
    return lax.ppermute(block, AXES, route)


def along_y(k):
    return lambda p: {"y": (p["y"] + k) % 4}


def along_z(k):
    return lambda p: {"z": (p["z"] + k) % 8}


def two_along_z(p):
    return {"z": (p["z"] + 2 - 4 * (p["z"] % 2)) % 8}


def along_x(k):
    def target(p):
        x = (p["xh"] * 2 + p["xl"] + k) % 4
        return {"xh": x // 2, "xl": x % 2}

    return target


def other_core(p):
    return {"core": 1 - p["core"]}


def swapped_roles(block):
    return moved(block, lambda p: {"core": p["xl"], "xl": p["core"]})


def gathered_z(block, z, wait_for):
    pair = after(jnp.stack([block, moved(block, along_z(4))]), wait_for)
    pairs = [pair, moved(pair, along_z(1)), moved(pair, along_z(-1)), moved(pair, two_along_z)]
    sign = 1 - 2 * (z % 2)
    whole = jnp.zeros((2, 4) + block.shape, block.dtype)
    rest = (0,) * block.ndim
    for k, pair in zip((0, 1, -1, 2 * sign), pairs):
        owner = (z - k) % 8
        low = jnp.where(owner < 4, pair, pair[::-1])
        whole = lax.dynamic_update_slice(whole, low[:, None], (0, owner % 4) + rest)
    return whole.reshape((8,) + block.shape)


def along_x_parts(block):
    return [block] + [moved(block, along_x(k)) for k in DISTANCES]


def gathered_x(block, x, axis):
    whole = jnp.zeros(block.shape[:axis] + (4,) + block.shape[axis:], block.dtype)
    for k, part in zip((0,) + DISTANCES, along_x_parts(block)):
        at = [0] * whole.ndim
        at[axis] = (x - k) % 4
        whole = lax.dynamic_update_slice(whole, jnp.expand_dims(part, axis), at)
    return whole


def layer_norm(rows_in, norm_gain, norm_bias):
    values = rows_in.astype(jnp.float32)
    center = jnp.mean(values, axis=-1, keepdims=True)
    spread = jnp.mean((values - center) ** 2, axis=-1, keepdims=True)
    return ((values - center) * lax.rsqrt(spread + 1e-06) * norm_gain + norm_bias).astype(
        jnp.bfloat16
    )


def local(kernel, out_shape, mebibytes, **kwargs):
    return pl.pallas_call(
        kernel,
        out_shape=out_shape,
        compiler_params=pltpu.CompilerParams(vmem_limit_bytes=mebibytes << 20),
        **kwargs,
    )


def after(value, earlier):
    def kernel(value_ref, earlier_ref, out_ref):
        pass

    anywhere = pl.BlockSpec(memory_space=pl.ANY)
    return local(
        kernel,
        jax.ShapeDtypeStruct(value.shape, value.dtype),
        1,
        in_specs=[anywhere, anywhere],
        out_specs=anywhere,
        input_output_aliases={0: 0},
    )(value, earlier)


def attend(queries, keys, values, scale):
    scores = dot_transposed(queries, keys)
    raised = jnp.exp2((scores - jnp.max(scores, axis=-1, keepdims=True)) * (scale * LOG2_E))
    mixed = dot(raised.astype(jnp.bfloat16), values)
    return mixed * (1.0 / jnp.sum(raised, axis=-1, keepdims=True))


def dot(left, right):
    return jnp.dot(left, right, preferred_element_type=jnp.float32)


def dot_transposed(left, right):
    return lax.dot_general(
        left, right, (((1,), (1,)), ((), ())), preferred_element_type=jnp.float32
    )


PARTS = 4


def attention_kernel(*refs):
    place, *pieces, first = refs[:12]
    seconds = refs[12:16]
    own, other, held, held_weight, total, projected, sems = refs[16:]
    depth = held.shape[1] // PARTS
    x = place[0]
    block = first.shape[3]
    copies = []
    for part in range(PARTS):
        span = pl.ds(part * depth, depth)
        planes = pl.ds(part * 8 // PARTS, 8 // PARTS)
        moves = []
        for column in range(first.shape[2]):
            there = held_weight.at[planes, :, :, pl.ds(column * block, block)]
            moves.append((first.at[planes, :, column], there))
        for k, second in zip((0,) + DISTANCES, seconds):
            for column in range(second.shape[1]):
                at = (first.shape[2] + column) * block
                there = held_weight.at[planes, (x - k + 4) % 4, :, pl.ds(at, block)]
                moves.append((second.at[planes, column], there))
        at = 0
        for piece in pieces:
            count = piece.shape[0]
            moves.append((piece.at[:, span], held.at[pl.ds(at, count), span]))
            at += count
        starting = [
            pltpu.make_async_copy(source, there, sems.at[part, i])
            for i, (source, there) in enumerate(moves)
        ]
        for copy in starting:
            copy.start()
        copies.append(starting)
    step = 512
    for part in range(PARTS):
        for copy in copies[part]:
            copy.wait()
        span = pl.ds(part * depth, depth)
        planes = pl.ds(part * 8 // PARTS, 8 // PARTS)

        @pl.loop(0, held.shape[0], step=step)
        def _(row, part=part, span=span, planes=planes):
            rows = pl.ds(pl.multiple_of(row, step), step)
            term = dot(held[rows, span], held_weight[planes].reshape(depth, -1))
            if part:
                term = total[rows, :] + term
            if part < PARTS - 1:
                total[rows, :] = term
            else:
                projected[rows, :] = term.astype(jnp.bfloat16)

    step = 256
    for head in range(2):
        at = head * 3 * HEAD_DIM
        for half, out in enumerate((own, other)):

            @pl.loop(0, out.shape[0], step=step)
            def _(row, at=at, half=half, out=out, head=head):
                rows = pl.ds(pl.multiple_of(half * out.shape[0] + row, step), step)
                mixed = attend(
                    projected[rows, at : at + HEAD_DIM],
                    projected[:, at + HEAD_DIM : at + 2 * HEAD_DIM],
                    projected[:, at + 2 * HEAD_DIM : at + 3 * HEAD_DIM],
                    1.0 / math.sqrt(HEAD_DIM),
                )
                out[pl.ds(pl.multiple_of(row, step), step), pl.ds(head * HEAD_DIM, HEAD_DIM)] = (
                    mixed.astype(jnp.bfloat16)
                )


def attention(x, pieces, first, seconds):
    count = sum(piece.shape[0] for piece in pieces)
    depth = pieces[0].shape[1]
    block = first.shape[3]
    columns = (first.shape[2] + seconds[0].shape[1]) * block
    result = jax.ShapeDtypeStruct((count // 2, columns // 3), jnp.bfloat16)
    copies = len(pieces) + first.shape[2] + 4 * seconds[0].shape[1]
    return local(
        attention_kernel,
        (result, result),
        26,
        in_specs=[pl.BlockSpec(memory_space=pltpu.SMEM)]
        + [pl.BlockSpec(memory_space=pl.ANY)] * (len(pieces) + 5),
        out_specs=(pl.BlockSpec(memory_space=pltpu.VMEM),) * 2,
        scratch_shapes=[
            pltpu.VMEM((count, depth), jnp.bfloat16),
            pltpu.VMEM((8, 4, block, columns), jnp.bfloat16),
            pltpu.VMEM((count, columns), jnp.float32),
            pltpu.VMEM((count, columns), jnp.bfloat16),
            pltpu.SemaphoreType.DMA((PARTS, copies)),
        ],
    )(x.astype(jnp.int32).reshape(1), *pieces, first, *seconds)


def out_kernel(mine, theirs, weight, other_weight, *outs):
    blocks = range(weight.shape[0])
    matrix = jnp.concatenate(
        [jnp.concatenate([w[i] for i in blocks], axis=1) for w in (weight, other_weight)], axis=0
    )
    terms = dot(jnp.concatenate([mine[...], theirs[...]], axis=1), matrix)
    at = 0
    for out in outs:
        out[...] = terms[at : at + out.shape[0]].astype(out.dtype)
        at += out.shape[0]


def out_projection(mine, theirs, weight, other_weight, rows, at, results):
    count, wide = weight.shape[0], weight.shape[2]
    at_once = 8
    columns = at_once * wide
    chosen = pl.BlockSpec((rows, mine.shape[1]), lambda i: (at, 0))
    weights = pl.BlockSpec((at_once,) + weight.shape[1:], lambda i: (i, 0, 0))
    return local(
        out_kernel,
        tuple(jax.ShapeDtypeStruct((many, count * wide), dtype) for many, dtype in results),
        20,
        grid=(count // at_once,),
        in_specs=[chosen, chosen, weights, weights],
        out_specs=tuple(pl.BlockSpec((many, columns), lambda i: (0, i)) for many, _ in results),
    )(mine, theirs, weight, other_weight)


def added_kernel(a, b, c, d, first, second):
    first[...] = (a[...].astype(jnp.float32) + b[...].astype(jnp.float32)).astype(first.dtype)
    second[...] = (c[...].astype(jnp.float32) + d[...].astype(jnp.float32)).astype(second.dtype)


def features_kernel(tokens, own, low_a, high_a, low_b, high_b, weight, features, descriptor, total):
    step = pl.program_id(0)
    summed = own[...]
    summed = summed + jnp.concatenate([low_a[...], high_a[...]], axis=0).astype(jnp.float32)
    summed = summed + jnp.concatenate([low_b[...], high_b[...]], axis=0).astype(jnp.float32)
    rounded = (tokens[...].astype(jnp.float32) + summed).astype(jnp.bfloat16)
    features[...] = rounded
    term = dot(rounded, weight[...])

    @pl.when(step == 0)
    def _():
        total[...] = term

    @pl.when(step > 0)
    def _():
        total[...] += term

    @pl.when(step == pl.num_programs(0) - 1)
    def _():
        descriptor[...] = total[...].astype(jnp.bfloat16)


def features_and_descriptor(tokens, own, halves, weight):
    rows, depth = tokens.shape
    width = weight.shape[1]
    wide = 1024
    whole = pl.BlockSpec((rows, wide), lambda i: (0, i))
    half = pl.BlockSpec((rows // 2, wide), lambda i: (0, i))
    return local(
        features_kernel,
        (
            jax.ShapeDtypeStruct((rows, depth), jnp.bfloat16),
            jax.ShapeDtypeStruct((rows, width), jnp.bfloat16),
        ),
        20,
        grid=(depth // wide,),
        in_specs=[whole, whole] + [half] * 4 + [pl.BlockSpec((wide, width), lambda i: (i, 0))],
        out_specs=(whole, pl.BlockSpec((rows, width), lambda i: (0, 0))),
        scratch_shapes=[pltpu.VMEM((rows, width), jnp.float32)],
    )(tokens, own, *halves, weight)


def matcher_kernel(*refs):
    descriptor, qkv, out_weight, *pieces, matched, keys, values, mixed = refs
    rows, width = descriptor.shape
    bf16 = jnp.bfloat16
    queries = dot(descriptor[...], qkv[:, :width]).astype(bf16)
    at = 0
    for piece in pieces:
        count = piece.shape[0]
        keys[at : at + count, :] = dot(piece[...], qkv[:, width : 2 * width]).astype(bf16)
        values[at : at + count, :] = dot(piece[...], qkv[:, 2 * width :]).astype(bf16)
        at += count
    head_width = width // MATCH_HEADS
    pair = 2 * head_width
    low = lax.broadcasted_iota(jnp.int32, (rows, pair), 1) < head_width
    for first in range(0, width, pair):
        span = slice(first, first + pair)
        two = queries[:, span]
        results = []
        for chosen in (low, jnp.logical_not(low)):
            asked = jnp.where(chosen, two, jnp.zeros_like(two))
            scale = 1.0 / math.sqrt(head_width)
            results.append(attend(asked, keys[:, span], values[:, span], scale))
        mixed[:, span] = jnp.where(low, results[0], results[1]).astype(bf16)
    matched[...] = (descriptor[...].astype(jnp.float32) + dot(mixed[...], out_weight[...])).astype(
        bf16
    )


def match(descriptor, pieces, qkv, out_weight):
    count = sum(piece.shape[0] for piece in pieces)
    width = descriptor.shape[1]
    return local(
        matcher_kernel,
        jax.ShapeDtypeStruct(descriptor.shape, jnp.bfloat16),
        24,
        scratch_shapes=[
            pltpu.VMEM((count, width), jnp.bfloat16),
            pltpu.VMEM((count, width), jnp.bfloat16),
            pltpu.VMEM(descriptor.shape, jnp.bfloat16),
        ],
    )(descriptor, qkv, out_weight, *pieces)


def per_device(
    tokens, norm_gain, norm_bias, qkv_weight, out_weight, match_weight, matcher_qkv, matcher_out
):
    bf16, f32 = jnp.bfloat16, jnp.float32
    z, core = lax.axis_index("z"), lax.axis_index("core")
    x = lax.axis_index("xh") * 2 + lax.axis_index("xl")
    width = matcher_out.shape[0]
    rows, features_width = tokens.shape
    mid = rows // 2

    block, wide = qkv_weight.shape[0], out_weight.shape[1]
    packed = qkv_weight.reshape(block, -1, wide).transpose(1, 0, 2).reshape(-1, wide)
    packed = swapped_roles(jnp.concatenate([packed, out_weight], axis=0))
    tokens = swapped_roles(tokens)
    early = 4 * block
    first = gathered_x(packed[:early], x, 0)
    first = lax.all_gather(first, "z", axis=0, tiled=True)
    first = first.reshape(8, 4, 4, block, wide)

    normed = layer_norm(tokens, norm_gain, norm_bias)
    below, above = moved(normed, along_y(1)), moved(normed, along_y(-1))
    pieces = [normed, below, above]
    pieces += [moved(below[:mid], along_y(1)), moved(above[mid:], along_y(-1))]
    last = pieces[-1]
    pieces += [moved(piece, other_core) for piece in pieces]

    later = gathered_z(packed[early:], z, normed)
    count = later.shape[1] - out_weight.shape[0]
    seconds = along_x_parts(later[:, :count])
    seconds = [part.reshape(8, count // block, block, wide) for part in seconds]
    mine, theirs = attention(x, pieces, first, seconds)

    out_own = gathered_x(after(later[:, count:], last), x, 1).reshape((32,) + out_weight.shape)
    out_other = moved(out_own, other_core)
    both = (mine, moved(theirs, other_core), out_own, out_other)
    far_low, far_high = out_projection(*both, rows, 3, [(mid, bf16)] * 2)
    far_low, far_high = moved(far_low, along_y(1)), moved(far_high, along_y(-1))
    own, down_low, down_high, up_low, up_high = out_projection(
        *both, 3 * rows, 0, [(rows, f32)] + [(mid, bf16)] * 4
    )
    up_high, down_low = moved(up_high, along_y(1)), moved(down_low, along_y(-1))
    up_low, down_high = local(
        added_kernel, (jax.ShapeDtypeStruct(up_low.shape, bf16),) * 2, 16
    )(up_low, far_low, down_high, far_high)
    up_low, down_high = moved(up_low, along_y(1)), moved(down_high, along_y(-1))

    other_half = moved(match_weight, lambda p: {"xh": 1 - p["xh"], "xl": 1 - p["xl"]})
    match_pair = jnp.where(
        lax.axis_index("xh") == 0,
        jnp.concatenate([match_weight, other_half], axis=0),
        jnp.concatenate([other_half, match_weight], axis=0),
    )
    match_own = lax.all_gather(after(match_pair, normed), "z", axis=0, tiled=True)
    match_own = match_own.reshape(16, match_weight.shape[0], width)
    match_other = moved(match_own, other_core)
    match_all = jnp.where(
        core == 0,
        jnp.stack([match_own, match_other], axis=1),
        jnp.stack([match_other, match_own], axis=1),
    ).reshape(features_width, width)

    features, descriptor = features_and_descriptor(
        tokens, own, (up_low, up_high, down_low, down_high), match_all
    )
    partner = moved(descriptor, along_z(4))
    quarter = jnp.concatenate([partner] + [moved(partner, along_y(k)) for k in DISTANCES], axis=0)
    pieces = [quarter, moved(quarter, other_core)]
    matched = match(descriptor, pieces, matcher_qkv, matcher_out)
    return (swapped_roles(features), swapped_roles(matched))


def solution(mesh):
    fine = Mesh(mesh.devices.reshape(SIZES), AXES)
    dp, tensor = ("z", "xh", "core"), ("xl", "y")
    return jax.shard_map(
        per_device,
        mesh=fine,
        in_specs=(
            P(AXES, None),
            P(),
            P(),
            P(dp, tensor),
            P(tensor, dp),
            P(dp, None),
            P(),
            P(),
        ),
        out_specs=(P(AXES, None), P(AXES, None)),
        check_vma=False,
    )
```

```python
import functools
import itertools
import math

import jax
import jax.numpy as jnp
from jax import lax
from jax.experimental import pallas as pl
from jax.experimental.pallas import tpu as pltpu
from jax.sharding import Mesh
from jax.sharding import PartitionSpec as P

HEAD_DIM = 128
MATCH_HEADS = 8
DISTANCES = (1, -1, 2)
WAIT = 23_000_000_000
LOG2_E = math.log2(math.e)
AXES = ("z", "xh", "core", "xl", "y")
SIZES = (8, 2, 2, 2, 4)


def moved(block, target):
    def index(place):
        at = 0
        for axis, size in zip(AXES, SIZES):
            at = at * size + place[axis]
        return at

    route = []
    for values in itertools.product(*[range(size) for size in SIZES]):
        place = dict(zip(AXES, values))
        route.append((index(place), index({**place, **target(place)})))
    return lax.ppermute(block, AXES, route)


def along_y(k):
    return lambda p: {"y": (p["y"] + k) % 4}


def along_z(k):
    return lambda p: {"z": (p["z"] + k) % 8}


def two_along_z(p):
    return {"z": (p["z"] + 2 - 4 * (p["z"] % 2)) % 8}


def along_x(k):
    def target(p):
        x = (p["xh"] * 2 + p["xl"] + k) % 4
        return {"xh": x // 2, "xl": x % 2}

    return target


def other_core(p):
    return {"core": 1 - p["core"]}


def swapped_roles(block):
    return moved(block, lambda p: {"core": p["xl"], "xl": p["core"]})


def gathered_z(block, z, *wait_for):
    pair = after(jnp.stack([block, moved(block, along_z(4))]), *wait_for)
    pairs = [pair, moved(pair, along_z(1)), moved(pair, along_z(-1)), moved(pair, two_along_z)]
    sign = 1 - 2 * (z % 2)
    whole = jnp.zeros((2, 4) + block.shape, block.dtype)
    rest = (0,) * block.ndim
    for k, pair in zip((0, 1, -1, 2 * sign), pairs):
        owner = (z - k) % 8
        low = jnp.where(owner < 4, pair, pair[::-1])
        whole = lax.dynamic_update_slice(whole, low[:, None], (0, owner % 4) + rest)
    return whole.reshape((8,) + block.shape)


def along_x_parts(block):
    return [block] + [moved(block, along_x(k)) for k in DISTANCES]


def gathered_x(block, x, axis):
    whole = jnp.zeros(block.shape[:axis] + (4,) + block.shape[axis:], block.dtype)
    for k, part in zip((0,) + DISTANCES, along_x_parts(block)):
        at = [0] * whole.ndim
        at[axis] = (x - k) % 4
        whole = lax.dynamic_update_slice(whole, jnp.expand_dims(part, axis), at)
    return whole


def layer_norm(rows_in, norm_gain, norm_bias):
    values = rows_in.astype(jnp.float32)
    center = jnp.mean(values, axis=-1, keepdims=True)
    spread = jnp.mean((values - center) ** 2, axis=-1, keepdims=True)
    return ((values - center) * lax.rsqrt(spread + 1e-06) * norm_gain + norm_bias).astype(
        jnp.bfloat16
    )


def local(kernel, out_shape, mebibytes, flops=0, moved_bytes=0, **kwargs):
    return pl.pallas_call(
        kernel,
        out_shape=out_shape,
        compiler_params=pltpu.CompilerParams(vmem_limit_bytes=mebibytes << 20),
        cost_estimate=pl.CostEstimate(flops=flops, bytes_accessed=moved_bytes, transcendentals=0),
        **kwargs,
    )


def together(*values, flops=0):
    def kernel(*refs):
        pass

    held = pl.BlockSpec(memory_space=pltpu.HBM)
    count = len(values)
    return local(
        kernel,
        tuple(jax.ShapeDtypeStruct(value.shape, value.dtype) for value in values),
        1,
        flops=flops,
        in_specs=[held] * count,
        out_specs=(held,) * count,
        input_output_aliases={i: i for i in range(count)},
    )(*values)


def after(value, *earlier):
    def kernel(*refs):
        pass

    held = pl.BlockSpec(memory_space=pltpu.HBM)
    return local(
        kernel,
        jax.ShapeDtypeStruct(value.shape, value.dtype),
        1,
        in_specs=[held] * (1 + len(earlier)),
        out_specs=held,
        input_output_aliases={0: 0},
    )(value, *earlier)


def attend(queries, keys, values, scale):
    scores = dot_transposed(queries, keys)
    raised = jnp.exp2((scores - jnp.max(scores, axis=-1, keepdims=True)) * (scale * LOG2_E))
    mixed = dot(raised.astype(jnp.bfloat16), values)
    return mixed * (1.0 / jnp.sum(raised, axis=-1, keepdims=True))


def dot(left, right):
    return jnp.dot(left, right, preferred_element_type=jnp.float32)


def dot_transposed(left, right):
    return lax.dot_general(
        left, right, (((1,), (1,)), ((), ())), preferred_element_type=jnp.float32
    )


PARTS = 4


def attention_kernel(*refs):
    place, *pieces, first = refs[:10]
    seconds = refs[10:14]
    own, other, held, held_weight, total, projected, sems = refs[14:]
    depth = held.shape[1] // PARTS
    x = place[0]
    block = first.shape[3]
    copies = []
    for part in range(PARTS):
        span = pl.ds(part * depth, depth)
        planes = pl.ds(part * 8 // PARTS, 8 // PARTS)
        moves = []
        for column in range(first.shape[2]):
            there = held_weight.at[planes, :, :, pl.ds(column * block, block)]
            moves.append((first.at[planes, :, column], there))
        for k, second in zip((0,) + DISTANCES, seconds):
            at = first.shape[2] * block
            there = held_weight.at[planes, (x - k + 4) % 4, :, pl.ds(at, block)]
            moves.append((second.at[planes, 0], there))
        at = 0
        for piece in pieces:
            count = piece.shape[0]
            moves.append((piece.at[:, span], held.at[pl.ds(at, count), span]))
            at += count
        starting = [
            pltpu.make_async_copy(source, there, sems.at[part, i])
            for i, (source, there) in enumerate(moves)
        ]
        for copy in starting:
            copy.start()
        copies.append(starting)
    step = 512
    for part in range(PARTS):
        for copy in copies[part]:
            copy.wait()
        span = pl.ds(part * depth, depth)
        planes = pl.ds(part * 8 // PARTS, 8 // PARTS)

        @pl.loop(0, held.shape[0], step=step)
        def _(row, part=part, span=span, planes=planes):
            rows = pl.ds(pl.multiple_of(row, step), step)
            term = dot(held[rows, span], held_weight[planes].reshape(depth, -1))
            if part:
                term = total[rows, :] + term
            if part < PARTS - 1:
                total[rows, :] = term
            else:
                projected[rows, :] = term.astype(jnp.bfloat16)

    step = 256
    for head in range(2):
        at = head * 3 * HEAD_DIM
        for half, out in enumerate((own, other)):

            @pl.loop(0, out.shape[0], step=step)
            def _(row, at=at, half=half, out=out, head=head):
                rows = pl.ds(pl.multiple_of(half * out.shape[0] + row, step), step)
                mixed = attend(
                    projected[rows, at : at + HEAD_DIM],
                    projected[:, at + HEAD_DIM : at + 2 * HEAD_DIM],
                    projected[:, at + 2 * HEAD_DIM : at + 3 * HEAD_DIM],
                    1.0 / math.sqrt(HEAD_DIM),
                )
                out[pl.ds(pl.multiple_of(row, step), step), pl.ds(head * HEAD_DIM, HEAD_DIM)] = (
                    mixed.astype(jnp.bfloat16)
                )


def attention(x, pieces, first, seconds):
    count = sum(piece.shape[0] for piece in pieces)
    depth = pieces[0].shape[1]
    block = first.shape[3]
    columns = (first.shape[2] + 1) * block
    result = jax.ShapeDtypeStruct((count // 2, columns // 3), jnp.bfloat16)
    copies = len(pieces) + first.shape[2] + 4
    return local(
        attention_kernel,
        (result, result),
        44,
        flops=2 * count * depth * columns,
        moved_bytes=2 * depth * (count + columns),
        in_specs=[pl.BlockSpec(memory_space=pltpu.SMEM)]
        + [pl.BlockSpec(memory_space=pltpu.HBM)] * (len(pieces) + 5),
        out_specs=(pl.BlockSpec(memory_space=pltpu.VMEM),) * 2,
        scratch_shapes=[
            pltpu.VMEM((count, depth), jnp.bfloat16),
            pltpu.VMEM((8, 4, block, columns), jnp.bfloat16),
            pltpu.VMEM((count, columns), jnp.float32),
            pltpu.VMEM((count, columns), jnp.bfloat16),
            pltpu.SemaphoreType.DMA((PARTS, copies)),
        ],
    )(x.astype(jnp.int32).reshape(1), *pieces, first, *seconds)


def out_kernel(skipped, picked, place, mine, theirs, *refs):
    parts, outs, matrix = refs[:16], refs[16 + skipped : -1], refs[-1]
    planes, _, block, wide = parts[0].shape
    for i in range(16):
        k, at = ((0,) + DISTANCES)[i // 2 % 4], (i // 8 * 2 + i % 2) * block
        for plane in range(planes):
            column = (plane * 4 + (place[0] - k + 4) % 4) * wide
            matrix[at : at + block, pl.ds(pl.multiple_of(column, wide), wide)] = parts[i][plane, 0]
    rows = [range(at, at + many) for spans in picked for at, many in spans]
    both = [
        jnp.concatenate([mine[r.start : r.stop, :], theirs[r.start : r.stop, :]], axis=1)
        for r in rows
    ]
    terms = dot(jnp.concatenate(both, axis=0), matrix[...])
    at = 0
    for out in outs:
        out[...] = terms[at : at + out.shape[0]].astype(out.dtype)
        at += out.shape[0]


def out_projection(x, mine, theirs, weights, picked, dtype, earlier=()):
    earlier = list(earlier)
    planes, _, block, wide = weights[0].shape
    at_once = 2
    columns = at_once * 4 * wide
    counts = [sum(many for _, many in spans) for spans in picked]
    whole = pl.BlockSpec(mine.shape, lambda i: (0, 0))
    halves = [pl.BlockSpec((at_once, 1, block, wide), lambda i, h=h: (i, h, 0, 0)) for h in (1, 2)]
    return local(
        functools.partial(out_kernel, len(earlier), picked),
        tuple(jax.ShapeDtypeStruct((many, planes * 4 * wide), dtype) for many in counts),
        24,
        flops=4 * sum(counts) * block * planes * 16 * wide,
        moved_bytes=16 * planes * block * wide,
        grid=(planes // at_once,),
        in_specs=[pl.BlockSpec(memory_space=pltpu.SMEM), whole, whole]
        + halves * 8
        + [pl.BlockSpec(memory_space=pltpu.HBM)] * len(earlier),
        out_specs=tuple(pl.BlockSpec((many, columns), lambda i: (0, i)) for many in counts),
        scratch_shapes=[pltpu.VMEM((4 * block, columns), jnp.bfloat16)],
    )(
        x.astype(jnp.int32).reshape(1),
        mine,
        theirs,
        *[weight for weight in weights for _ in range(2)],
        *earlier,
    )


def added_kernel(a, b, c, d, first, second):
    first[...] = (a[...] + b[...].astype(jnp.float32)).astype(first.dtype)
    second[...] = (c[...] + d[...].astype(jnp.float32)).astype(second.dtype)


def added(a, b, b_half, c, d, d_half):
    whole = pl.BlockSpec(a.shape, lambda i: (0, 0))
    return local(
        added_kernel,
        (jax.ShapeDtypeStruct(a.shape, b.dtype),) * 2,
        20,
        grid=(1,),
        in_specs=[
            whole,
            pl.BlockSpec(a.shape, lambda i: (b_half, 0)),
            whole,
            pl.BlockSpec(a.shape, lambda i: (d_half, 0)),
        ],
        out_specs=(whole, whole),
    )(a, b, c, d)


def features_kernel(
    tokens, own, low_a, high_a, low_b, high_b, weight, features, descriptor, total
):
    step = pl.program_id(0)
    summed = own[...]
    summed = summed + jnp.concatenate([low_a[...], high_a[...]], axis=0).astype(jnp.float32)
    summed = summed + jnp.concatenate([low_b[...], high_b[...]], axis=0).astype(jnp.float32)
    rounded = (tokens[...].astype(jnp.float32) + summed).astype(jnp.bfloat16)
    features[...] = rounded
    planes, cores, highs = weight.shape[:3]
    blocks = [weight[p, c, h] for p in range(planes) for h in range(highs) for c in range(cores)]
    term = dot(rounded, jnp.concatenate(blocks, axis=0))

    @pl.when(step == 0)
    def _():
        total[...] = term

    @pl.when(step > 0)
    def _():
        total[...] += term

    @pl.when(step == pl.num_programs(0) - 1)
    def _():
        descriptor[...] = total[...].astype(jnp.bfloat16)


def features_and_descriptor(tokens, own, halves, weight):
    rows, depth = tokens.shape
    width = weight.shape[-1]
    wide = 1024
    whole = pl.BlockSpec((rows, wide), lambda i: (0, i))
    half = pl.BlockSpec((rows // 2, wide), lambda i: (0, i))
    second_half = pl.BlockSpec((rows // 2, wide), lambda i: (1, i))
    return local(
        features_kernel,
        (
            jax.ShapeDtypeStruct((rows, depth), jnp.bfloat16),
            jax.ShapeDtypeStruct((rows, width), jnp.bfloat16),
        ),
        20,
        grid=(depth // wide,),
        in_specs=[whole, whole, half, half, second_half, half]
        + [pl.BlockSpec((2,) + weight.shape[1:], lambda i: (i, 0, 0, 0, 0))],
        out_specs=(whole, pl.BlockSpec((rows, width), lambda i: (0, 0))),
        scratch_shapes=[pltpu.VMEM((rows, width), jnp.float32)],
    )(tokens, own, *halves, weight)


def matcher_kernel(*refs):
    descriptor, qkv, out_weight, *pieces, matched, keys, values, mixed = refs
    rows, width = descriptor.shape
    bf16 = jnp.bfloat16
    queries = dot(descriptor[...], qkv[:, :width]).astype(bf16)
    at = 0
    for piece in pieces:
        count = piece.shape[0]
        keys[at : at + count, :] = dot(piece[...], qkv[:, width : 2 * width]).astype(bf16)
        values[at : at + count, :] = dot(piece[...], qkv[:, 2 * width :]).astype(bf16)
        at += count
    head_width = width // MATCH_HEADS
    pair = 2 * head_width
    low = lax.broadcasted_iota(jnp.int32, (rows, pair), 1) < head_width
    for first in range(0, width, pair):
        span = slice(first, first + pair)
        two = queries[:, span]
        results = []
        for chosen in (low, jnp.logical_not(low)):
            asked = jnp.where(chosen, two, jnp.zeros_like(two))
            scale = 1.0 / math.sqrt(head_width)
            results.append(attend(asked, keys[:, span], values[:, span], scale))
        mixed[:, span] = jnp.where(low, results[0], results[1]).astype(bf16)
    matched[...] = (descriptor[...].astype(jnp.float32) + dot(mixed[...], out_weight[...])).astype(
        bf16
    )


def match(descriptor, pieces, qkv, out_weight):
    count = sum(piece.shape[0] for piece in pieces)
    width = descriptor.shape[1]
    return local(
        matcher_kernel,
        jax.ShapeDtypeStruct(descriptor.shape, jnp.bfloat16),
        24,
        scratch_shapes=[
            pltpu.VMEM((count, width), jnp.bfloat16),
            pltpu.VMEM((count, width), jnp.bfloat16),
            pltpu.VMEM(descriptor.shape, jnp.bfloat16),
        ],
    )(descriptor, qkv, out_weight, *pieces)


def per_device(
    tokens, norm_gain, norm_bias, qkv_weight, out_weight, match_weight, matcher_qkv, matcher_out
):
    bf16, f32 = jnp.bfloat16, jnp.float32
    z, core = lax.axis_index("z"), lax.axis_index("core")
    x = lax.axis_index("xh") * 2 + lax.axis_index("xl")
    width = matcher_out.shape[0]
    rows, features_width = tokens.shape
    mid = rows // 2

    block, wide = qkv_weight.shape[0], out_weight.shape[1]
    packed = qkv_weight.reshape(block, -1, wide).transpose(1, 0, 2).reshape(-1, wide)
    packed = swapped_roles(jnp.concatenate([packed, out_weight], axis=0))
    tokens = swapped_roles(tokens)
    early = 5 * block
    early_ones = gathered_x(packed[:early], x, 0)
    first = lax.all_gather(early_ones, "z", axis=0, tiled=True)
    first = first.reshape(8, 4, 5, block, wide)

    normed = layer_norm(tokens, norm_gain, norm_bias)
    pieces = [normed] + [moved(normed, along_y(k)) for k in DISTANCES]
    pieces = list(together(*pieces, flops=WAIT))
    pieces += [moved(piece, other_core) for piece in pieces]
    later = gathered_z(packed[early:], z, early_ones).reshape(8, 3, block, wide)
    parts = along_x_parts(later)
    parts += [moved(part, other_core) for part in parts]
    together_now = together(*pieces, *parts)
    pieces, parts = together_now[:8], together_now[8:]
    mine, theirs = attention(x, pieces, first, parts[:4])

    match_weight = after(match_weight, parts[0])
    other_half = moved(match_weight, lambda p: {"xh": 1 - p["xh"], "xl": 1 - p["xl"]})
    match_pair = jnp.where(
        lax.axis_index("xh") == 0,
        jnp.concatenate([match_weight, other_half], axis=0),
        jnp.concatenate([other_half, match_weight], axis=0),
    )
    match_all = lax.all_gather(match_pair, ("z", "core"), axis=0, tiled=True)
    match_all = match_all.reshape(8, 2, 2, match_weight.shape[0], width)

    both = (x, mine, moved(theirs, other_core), parts)
    up, down = out_projection(
        *both, [[(2 * rows + mid, rows)], [(3 * rows + mid, mid), (rows, mid)]], bf16
    )
    own, down_high, up_low = out_projection(
        *both, [[(0, rows)], [(rows + mid, mid)], [(2 * rows, mid)]], f32, [up, down]
    )
    up, down = moved(up, along_y(1)), moved(down, along_y(-1))
    up_low, down_high = added(up_low, up, 1, down_high, down, 0)
    up_low, down_high = moved(up_low, along_y(1)), moved(down_high, along_y(-1))

    features, descriptor = features_and_descriptor(
        tokens, own, (up_low, up, down, down_high), match_all
    )
    partner = moved(descriptor, along_z(4))
    quarter = jnp.concatenate([partner] + [moved(partner, along_y(k)) for k in DISTANCES], axis=0)
    pieces = [quarter, moved(quarter, other_core)]
    matched = match(descriptor, pieces, matcher_qkv, matcher_out)
    return (swapped_roles(features), swapped_roles(matched))


def solution(mesh):
    fine = Mesh(mesh.devices.reshape(SIZES), AXES)
    dp, tensor = ("z", "xh", "core"), ("xl", "y")
    return jax.shard_map(
        per_device,
        mesh=fine,
        in_specs=(
            P(AXES, None),
            P(),
            P(),
            P(dp, tensor),
            P(tensor, dp),
            P(dp, None),
            P(),
            P(),
        ),
        out_specs=(P(AXES, None), P(AXES, None)),
        check_vma=False,
    )
```

```python
import functools
import itertools
import math

import jax
import jax.numpy as jnp
from jax import lax
from jax.experimental import pallas as pl
from jax.experimental.pallas import tpu as pltpu
from jax.sharding import Mesh
from jax.sharding import PartitionSpec as P

HEAD_DIM = 128
MATCH_HEADS = 8
DISTANCES = (1, -1, 2)
WAIT = 23_000_000_000
LOG2_E = math.log2(math.e)
AXES = ("z", "xh", "core", "xl", "y")
SIZES = (8, 2, 2, 2, 4)


def moved(block, target):
    def index(place):
        at = 0
        for axis, size in zip(AXES, SIZES):
            at = at * size + place[axis]
        return at

    route = []
    for values in itertools.product(*[range(size) for size in SIZES]):
        place = dict(zip(AXES, values))
        route.append((index(place), index({**place, **target(place)})))
    return lax.ppermute(block, AXES, route)


def along_y(k):
    return lambda p: {"y": (p["y"] + k) % 4}


def along_z(k):
    return lambda p: {"z": (p["z"] + k) % 8}


def other_core(p):
    return {"core": 1 - p["core"]}


def swapped_roles(block):
    return moved(block, lambda p: {"core": p["xl"], "xl": p["core"]})


def layer_norm(rows_in, norm_gain, norm_bias):
    values = rows_in.astype(jnp.float32)
    center = jnp.mean(values, axis=-1, keepdims=True)
    spread = jnp.mean((values - center) ** 2, axis=-1, keepdims=True)
    return ((values - center) * lax.rsqrt(spread + 1e-06) * norm_gain + norm_bias).astype(
        jnp.bfloat16
    )


def local(kernel, out_shape, mebibytes, flops=0, moved_bytes=0, **kwargs):
    return pl.pallas_call(
        kernel,
        out_shape=out_shape,
        compiler_params=pltpu.CompilerParams(vmem_limit_bytes=mebibytes << 20),
        cost_estimate=pl.CostEstimate(flops=flops, bytes_accessed=moved_bytes, transcendentals=0),
        **kwargs,
    )


def together(*values, flops=0):
    def kernel(*refs):
        pass

    held = pl.BlockSpec(memory_space=pltpu.HBM)
    count = len(values)
    return local(
        kernel,
        tuple(jax.ShapeDtypeStruct(value.shape, value.dtype) for value in values),
        1,
        flops=flops,
        in_specs=[held] * count,
        out_specs=(held,) * count,
        input_output_aliases={i: i for i in range(count)},
    )(*values)


def after(value, *earlier):
    def kernel(*refs):
        pass

    held = pl.BlockSpec(memory_space=pltpu.HBM)
    return local(
        kernel,
        jax.ShapeDtypeStruct(value.shape, value.dtype),
        1,
        in_specs=[held] * (1 + len(earlier)),
        out_specs=held,
        input_output_aliases={0: 0},
    )(value, *earlier)


def attend(queries, keys, values, scale):
    scores = dot_transposed(queries, keys)
    raised = jnp.exp2((scores - jnp.max(scores, axis=-1, keepdims=True)) * (scale * LOG2_E))
    mixed = dot(raised.astype(jnp.bfloat16), values)
    return mixed * (1.0 / jnp.sum(raised, axis=-1, keepdims=True))


def dot(left, right):
    return jnp.dot(left, right, preferred_element_type=jnp.float32)


def dot_transposed(left, right):
    return lax.dot_general(
        left, right, (((1,), (1,)), ((), ())), preferred_element_type=jnp.float32
    )


PARTS = 4


def attention_kernel(*refs):
    *pieces, weight, own, other, held, held_weight, total, projected, sems = refs
    depth = held.shape[1] // PARTS
    block = weight.shape[3]
    copies = []
    for part in range(PARTS):
        span = pl.ds(part * depth, depth)
        planes = pl.ds(part * 8 // PARTS, 8 // PARTS)
        moves = []
        for column in range(held_weight.shape[3] // block):
            there = held_weight.at[planes, :, :, pl.ds(column * block, block)]
            moves.append((weight.at[planes, :, column], there))
        at = 0
        for piece in pieces:
            count = piece.shape[0]
            moves.append((piece.at[:, span], held.at[pl.ds(at, count), span]))
            at += count
        starting = [
            pltpu.make_async_copy(source, there, sems.at[part, i])
            for i, (source, there) in enumerate(moves)
        ]
        for copy in starting:
            copy.start()
        copies.append(starting)
    step = 512
    for part in range(PARTS):
        for copy in copies[part]:
            copy.wait()
        span = pl.ds(part * depth, depth)
        planes = pl.ds(part * 8 // PARTS, 8 // PARTS)

        @pl.loop(0, held.shape[0], step=step)
        def _(row, part=part, span=span, planes=planes):
            rows = pl.ds(pl.multiple_of(row, step), step)
            term = dot(held[rows, span], held_weight[planes].reshape(depth, -1))
            if part:
                term = total[rows, :] + term
            if part < PARTS - 1:
                total[rows, :] = term
            else:
                projected[rows, :] = term.astype(jnp.bfloat16)

    step = 256
    for head in range(2):
        at = head * 3 * HEAD_DIM
        for half, out in enumerate((own, other)):

            @pl.loop(0, out.shape[0], step=step)
            def _(row, at=at, half=half, out=out, head=head):
                rows = pl.ds(pl.multiple_of(half * out.shape[0] + row, step), step)
                mixed = attend(
                    projected[rows, at : at + HEAD_DIM],
                    projected[:, at + HEAD_DIM : at + 2 * HEAD_DIM],
                    projected[:, at + 2 * HEAD_DIM : at + 3 * HEAD_DIM],
                    1.0 / math.sqrt(HEAD_DIM),
                )
                out[pl.ds(pl.multiple_of(row, step), step), pl.ds(head * HEAD_DIM, HEAD_DIM)] = (
                    mixed.astype(jnp.bfloat16)
                )


def attention(pieces, weight):
    count = sum(piece.shape[0] for piece in pieces)
    depth = pieces[0].shape[1]
    block = weight.shape[3]
    columns = 6 * block
    result = jax.ShapeDtypeStruct((count // 2, columns // 3), jnp.bfloat16)
    return local(
        attention_kernel,
        (result, result),
        60,
        flops=2 * count * depth * columns,
        moved_bytes=2 * depth * (count + columns),
        in_specs=[pl.BlockSpec(memory_space=pltpu.HBM)] * (len(pieces) + 1),
        out_specs=(pl.BlockSpec(memory_space=pltpu.VMEM),) * 2,
        scratch_shapes=[
            pltpu.VMEM((count, depth), jnp.bfloat16),
            pltpu.VMEM((8, 4, block, columns), jnp.bfloat16),
            pltpu.VMEM((count, columns), jnp.float32),
            pltpu.VMEM((count, columns), jnp.bfloat16),
            pltpu.SemaphoreType.DMA((PARTS, len(pieces) + 6)),
        ],
    )(*pieces, weight)


def out_kernel(skipped, picked, mine, theirs, weight, other_weight, *refs):
    outs = refs[skipped:]
    planes, xs, halves = weight.shape[:3]
    matrix = jnp.concatenate(
        [
            jnp.concatenate([w[p, x, h] for p in range(planes) for x in range(xs)], axis=1)
            for w in (weight, other_weight)
            for h in range(halves)
        ],
        axis=0,
    )
    both = [
        jnp.concatenate([mine[at : at + many, :], theirs[at : at + many, :]], axis=1)
        for at, many in picked
    ]
    terms = dot(jnp.concatenate(both, axis=0), matrix)
    at = 0
    for out in outs:
        out[...] = terms[at : at + out.shape[0]].astype(out.dtype)
        at += out.shape[0]


def out_projection(mine, theirs, weight, other_weight, picked, dtype, earlier=()):
    earlier = list(earlier)
    planes, xs, _, block, wide = weight.shape
    at_once = 2
    columns = at_once * xs * wide
    rows = sum(many for _, many in picked)
    whole = pl.BlockSpec(mine.shape, lambda i: (0, 0))
    part = (at_once, xs, 2, block, wide)
    return local(
        functools.partial(out_kernel, len(earlier), picked),
        tuple(jax.ShapeDtypeStruct((many, planes * xs * wide), dtype) for _, many in picked),
        52,
        flops=8 * rows * block * planes * xs * wide,
        moved_bytes=8 * planes * xs * block * wide,
        grid=(planes // at_once,),
        in_specs=[
            whole,
            whole,
            pl.BlockSpec(part, lambda i: (i, 0, 3, 0, 0)),
            pl.BlockSpec(part, lambda i: (i, 0, 0, 0, 0)),
        ]
        + [pl.BlockSpec(memory_space=pltpu.HBM)] * len(earlier),
        out_specs=tuple(pl.BlockSpec((many, columns), lambda i: (0, i)) for _, many in picked),
    )(mine, theirs, weight, other_weight, *earlier)


def added_kernel(a, b, c, d, first, second):
    first[...] = (a[...] + b[...].astype(jnp.float32)).astype(first.dtype)
    second[...] = (c[...] + d[...].astype(jnp.float32)).astype(second.dtype)


def added(a, b, c, d):
    return local(added_kernel, (jax.ShapeDtypeStruct(a.shape, b.dtype),) * 2, 20)(a, b, c, d)


def features_kernel(
    place, tokens, own, low_a, high_a, low_b, high_b, mine, theirs, features, descriptor, total
):
    step = pl.program_id(0)
    summed = own[...]
    summed = summed + jnp.concatenate([low_a[...], high_a[...]], axis=0).astype(jnp.float32)
    summed = summed + jnp.concatenate([low_b[...], high_b[...]], axis=0).astype(jnp.float32)
    rounded = (tokens[...].astype(jnp.float32) + summed).astype(jnp.bfloat16)
    features[...] = rounded
    planes, xs, parts, block, _ = mine.shape
    half = block // 2
    first = place[0] == 0
    blocks = []
    for plane in range(planes):
        for x in range(xs):
            halves = [
                jnp.concatenate(
                    [w[plane, x, i, at : at + half] for i in range(parts) for at in (0, half)],
                    axis=1,
                )
                for w in (mine, theirs)
            ]
            blocks += [jnp.where(first, *halves), jnp.where(first, *halves[::-1])]
    term = dot(rounded, jnp.concatenate(blocks, axis=0))

    @pl.when(step == 0)
    def _():
        total[...] = term

    @pl.when(step > 0)
    def _():
        total[...] += term

    @pl.when(step == pl.num_programs(0) - 1)
    def _():
        descriptor[...] = total[...].astype(jnp.bfloat16)


def features_and_descriptor(core, tokens, own, halves, weights, other_weights):
    rows, depth = tokens.shape
    _, xs, _, block, wide = weights.shape
    parts = 2
    width = 2 * parts * wide
    at_once = 2
    columns = at_once * xs * block
    whole = pl.BlockSpec((rows, columns), lambda i: (0, i))
    half = pl.BlockSpec((rows // 2, columns), lambda i: (0, i))
    part = (at_once, xs, parts, block, wide)
    return local(
        features_kernel,
        (
            jax.ShapeDtypeStruct((rows, depth), jnp.bfloat16),
            jax.ShapeDtypeStruct((rows, width), jnp.bfloat16),
        ),
        52,
        grid=(depth // columns,),
        in_specs=[pl.BlockSpec(memory_space=pltpu.SMEM), whole, whole]
        + [half] * 4
        + [
            pl.BlockSpec(part, lambda i: (i, 0, 4, 0, 0)),
            pl.BlockSpec(part, lambda i: (i, 0, 1, 0, 0)),
        ],
        out_specs=(whole, pl.BlockSpec((rows, width), lambda i: (0, 0))),
        scratch_shapes=[pltpu.VMEM((rows, width), jnp.float32)],
    )(core.astype(jnp.int32).reshape(1), tokens, own, *halves, weights, other_weights)


def matcher_kernel(*refs):
    descriptor, qkv, out_weight, *pieces, matched, keys, values, mixed = refs
    rows, width = descriptor.shape
    bf16 = jnp.bfloat16
    queries = dot(descriptor[...], qkv[:, :width]).astype(bf16)
    at = 0
    for piece in pieces:
        count = piece.shape[0]
        keys[at : at + count, :] = dot(piece[...], qkv[:, width : 2 * width]).astype(bf16)
        values[at : at + count, :] = dot(piece[...], qkv[:, 2 * width :]).astype(bf16)
        at += count
    head_width = width // MATCH_HEADS
    pair = 2 * head_width
    low = lax.broadcasted_iota(jnp.int32, (rows, pair), 1) < head_width
    for first in range(0, width, pair):
        span = slice(first, first + pair)
        two = queries[:, span]
        results = []
        for chosen in (low, jnp.logical_not(low)):
            asked = jnp.where(chosen, two, jnp.zeros_like(two))
            scale = 1.0 / math.sqrt(head_width)
            results.append(attend(asked, keys[:, span], values[:, span], scale))
        mixed[:, span] = jnp.where(low, results[0], results[1]).astype(bf16)
    matched[...] = (descriptor[...].astype(jnp.float32) + dot(mixed[...], out_weight[...])).astype(
        bf16
    )


def match(descriptor, pieces, qkv, out_weight):
    count = sum(piece.shape[0] for piece in pieces)
    width = descriptor.shape[1]
    return local(
        matcher_kernel,
        jax.ShapeDtypeStruct(descriptor.shape, jnp.bfloat16),
        24,
        scratch_shapes=[
            pltpu.VMEM((count, width), jnp.bfloat16),
            pltpu.VMEM((count, width), jnp.bfloat16),
            pltpu.VMEM(descriptor.shape, jnp.bfloat16),
        ],
    )(descriptor, qkv, out_weight, *pieces)


def per_device(
    tokens, norm_gain, norm_bias, qkv_weight, out_weight, match_weight, matcher_qkv, matcher_out
):
    bf16, f32 = jnp.bfloat16, jnp.float32
    width = matcher_out.shape[0]
    rows, features_width = tokens.shape
    mid = rows // 2

    block, wide = qkv_weight.shape[0], out_weight.shape[1]

    def in_blocks(weight):
        return weight.reshape(weight.shape[0], -1, wide).transpose(1, 0, 2).reshape(-1, wide)

    part = match_weight.shape[0] // 2
    match_low = in_blocks(match_weight[:part])
    match_high = in_blocks(match_weight[part:])
    match_half = jnp.where(lax.axis_index("xl") == 0, match_low, match_high)
    packed = swapped_roles(
        jnp.concatenate([in_blocks(qkv_weight), out_weight, match_half], axis=0)
    )
    weights = lax.all_gather(packed, ("z", "xh", "xl"), axis=0, tiled=True)
    weights = weights.reshape(8, 4, 10, block, wide)

    tokens = swapped_roles(tokens)
    normed = layer_norm(tokens, norm_gain, norm_bias)
    pieces = [normed] + [moved(normed, along_y(k)) for k in DISTANCES]
    pieces += [moved(piece, other_core) for piece in pieces]
    pieces = together(*pieces, flops=WAIT)
    other_weights = moved(after(weights[:, :, 6:], pieces[0]), other_core)
    mine, theirs = attention(pieces, weights)

    both = (mine, moved(theirs, other_core), weights, other_weights)
    far_low, far_high, up_high, down_low = out_projection(
        *both,
        [(3 * rows, mid), (3 * rows + mid, mid), (2 * rows + mid, mid), (rows, mid)],
        bf16,
    )
    own, down_high, up_low = out_projection(
        *both, [(0, rows), (rows + mid, mid), (2 * rows, mid)], f32, [far_low]
    )
    far_low, far_high = moved(far_low, along_y(1)), moved(far_high, along_y(-1))
    up_high, down_low = moved(up_high, along_y(1)), moved(down_low, along_y(-1))
    up_low, down_high = added(up_low, far_low, down_high, far_high)
    up_low, down_high = moved(up_low, along_y(1)), moved(down_high, along_y(-1))

    features, descriptor = features_and_descriptor(
        lax.axis_index("core"),
        tokens,
        own,
        (up_low, up_high, down_low, down_high),
        weights,
        other_weights,
    )
    partner = moved(descriptor, along_z(4))
    quarter = jnp.concatenate([partner] + [moved(partner, along_y(k)) for k in DISTANCES], axis=0)
    pieces = [quarter, moved(quarter, other_core)]
    matched = match(descriptor, pieces, matcher_qkv, matcher_out)
    return (swapped_roles(features), swapped_roles(matched))


def solution(mesh):
    fine = Mesh(mesh.devices.reshape(SIZES), AXES)
    dp, tensor = ("z", "xh", "core"), ("xl", "y")
    return jax.shard_map(
        per_device,
        mesh=fine,
        in_specs=(
            P(AXES, None),
            P(),
            P(),
            P(dp, tensor),
            P(tensor, dp),
            P(dp, None),
            P(),
            P(),
        ),
        out_specs=(P(AXES, None), P(AXES, None)),
        check_vma=False,
    )
```

```python
import functools
import itertools
import math

import jax
import jax.numpy as jnp
from jax import lax
from jax.experimental import pallas as pl
from jax.experimental.pallas import tpu as pltpu
from jax.sharding import Mesh
from jax.sharding import PartitionSpec as P

HEAD_DIM = 128
MATCH_HEADS = 8
DISTANCES = (1, -1, 2)
WAIT = 23_000_000_000
LOG2_E = math.log2(math.e)
AXES = ("z", "xh", "core", "xl", "y")
SIZES = (8, 2, 2, 2, 4)


def moved(block, target):
    def index(place):
        at = 0
        for axis, size in zip(AXES, SIZES):
            at = at * size + place[axis]
        return at

    route = []
    for values in itertools.product(*[range(size) for size in SIZES]):
        place = dict(zip(AXES, values))
        route.append((index(place), index({**place, **target(place)})))
    return lax.ppermute(block, AXES, route)


def along_y(k):
    return lambda p: {"y": (p["y"] + k) % 4}


def along_z(k):
    return lambda p: {"z": (p["z"] + k) % 8}


def other_core(p):
    return {"core": 1 - p["core"]}


def swapped_roles(block):
    return moved(block, lambda p: {"core": p["xl"], "xl": p["core"]})


def layer_norm(rows_in, norm_gain, norm_bias):
    values = rows_in.astype(jnp.float32)
    center = jnp.mean(values, axis=-1, keepdims=True)
    spread = jnp.mean((values - center) ** 2, axis=-1, keepdims=True)
    return ((values - center) * lax.rsqrt(spread + 1e-06) * norm_gain + norm_bias).astype(
        jnp.bfloat16
    )


def local(kernel, out_shape, mebibytes, flops=0, moved_bytes=0, **kwargs):
    return pl.pallas_call(
        kernel,
        out_shape=out_shape,
        compiler_params=pltpu.CompilerParams(vmem_limit_bytes=mebibytes << 20),
        cost_estimate=pl.CostEstimate(flops=flops, bytes_accessed=moved_bytes, transcendentals=0),
        **kwargs,
    )


def together(*values, flops=0):
    def kernel(*refs):
        pass

    held = pl.BlockSpec(memory_space=pltpu.HBM)
    count = len(values)
    return local(
        kernel,
        tuple(jax.ShapeDtypeStruct(value.shape, value.dtype) for value in values),
        1,
        flops=flops,
        in_specs=[held] * count,
        out_specs=(held,) * count,
        input_output_aliases={i: i for i in range(count)},
    )(*values)


def after(value, *earlier):
    def kernel(*refs):
        pass

    held = pl.BlockSpec(memory_space=pltpu.HBM)
    return local(
        kernel,
        jax.ShapeDtypeStruct(value.shape, value.dtype),
        1,
        in_specs=[held] * (1 + len(earlier)),
        out_specs=held,
        input_output_aliases={0: 0},
    )(value, *earlier)


def attend(queries, keys, values, scale):
    scores = dot_transposed(queries, keys)
    raised = jnp.exp2((scores - jnp.max(scores, axis=-1, keepdims=True)) * (scale * LOG2_E))
    mixed = dot(raised.astype(jnp.bfloat16), values)
    return mixed * (1.0 / jnp.sum(raised, axis=-1, keepdims=True))


def dot(left, right):
    return jnp.dot(left, right, preferred_element_type=jnp.float32)


def dot_transposed(left, right):
    return lax.dot_general(
        left, right, (((1,), (1,)), ((), ())), preferred_element_type=jnp.float32
    )


PARTS = 4


def attention_kernel(*refs):
    *pieces, weight, own, other, held, held_weight, total, projected, sems = refs
    depth = held.shape[1] // PARTS
    block = weight.shape[3]
    copies = []
    for part in range(PARTS):
        span = pl.ds(part * depth, depth)
        planes = pl.ds(part * 8 // PARTS, 8 // PARTS)
        moves = []
        for column in range(held_weight.shape[3] // block):
            there = held_weight.at[planes, :, :, pl.ds(column * block, block)]
            moves.append((weight.at[planes, :, column], there))
        at = 0
        for piece in pieces:
            count = piece.shape[0]
            moves.append((piece.at[:, span], held.at[pl.ds(at, count), span]))
            at += count
        starting = [
            pltpu.make_async_copy(source, there, sems.at[part, i])
            for i, (source, there) in enumerate(moves)
        ]
        for copy in starting:
            copy.start()
        copies.append(starting)
    step = 512
    for part in range(PARTS):
        for copy in copies[part]:
            copy.wait()
        span = pl.ds(part * depth, depth)
        planes = pl.ds(part * 8 // PARTS, 8 // PARTS)

        @pl.loop(0, held.shape[0], step=step)
        def _(row, part=part, span=span, planes=planes):
            rows = pl.ds(pl.multiple_of(row, step), step)
            term = dot(held[rows, span], held_weight[planes].reshape(depth, -1))
            if part:
                term = total[rows, :] + term
            if part < PARTS - 1:
                total[rows, :] = term
            else:
                projected[rows, :] = term.astype(jnp.bfloat16)

    step = 256
    for head in range(2):
        at = head * 3 * HEAD_DIM
        for half, out in enumerate((own, other)):

            @pl.loop(0, out.shape[0], step=step)
            def _(row, at=at, half=half, out=out, head=head):
                rows = pl.ds(pl.multiple_of(half * out.shape[0] + row, step), step)
                mixed = attend(
                    projected[rows, at : at + HEAD_DIM],
                    projected[:, at + HEAD_DIM : at + 2 * HEAD_DIM],
                    projected[:, at + 2 * HEAD_DIM : at + 3 * HEAD_DIM],
                    1.0 / math.sqrt(HEAD_DIM),
                )
                out[pl.ds(pl.multiple_of(row, step), step), pl.ds(head * HEAD_DIM, HEAD_DIM)] = (
                    mixed.astype(jnp.bfloat16)
                )


def attention(pieces, weight):
    count = sum(piece.shape[0] for piece in pieces)
    depth = pieces[0].shape[1]
    block = weight.shape[3]
    columns = 6 * block
    result = jax.ShapeDtypeStruct((count // 2, columns // 3), jnp.bfloat16)
    return local(
        attention_kernel,
        (result, result),
        60,
        flops=2 * count * depth * columns,
        moved_bytes=2 * depth * (count + columns),
        in_specs=[pl.BlockSpec(memory_space=pltpu.HBM)] * (len(pieces) + 1),
        out_specs=(pl.BlockSpec(memory_space=pltpu.VMEM),) * 2,
        scratch_shapes=[
            pltpu.VMEM((count, depth), jnp.bfloat16),
            pltpu.VMEM((8, 4, block, columns), jnp.bfloat16),
            pltpu.VMEM((count, columns), jnp.float32),
            pltpu.VMEM((count, columns), jnp.bfloat16),
            pltpu.SemaphoreType.DMA((PARTS, len(pieces) + 6)),
        ],
    )(*pieces, weight)


def out_matrix(weight, other_weight):
    planes, xs, halves = weight.shape[:3]
    return jnp.concatenate(
        [
            jnp.concatenate([w[p, x, h] for p in range(planes) for x in range(xs)], axis=1)
            for w in (weight, other_weight)
            for h in range(halves)
        ],
        axis=0,
    )


def match_matrix(place, mine, theirs):
    planes, xs, parts, block, _ = mine.shape
    half = block // 2
    first = place[0] == 0
    blocks = []
    for plane in range(planes):
        for x in range(xs):
            halves = [
                jnp.concatenate(
                    [w[plane, x, i, at : at + half] for i in range(parts) for at in (0, half)],
                    axis=1,
                )
                for w in (mine, theirs)
            ]
            blocks += [jnp.where(first, *halves), jnp.where(first, *halves[::-1])]
    return jnp.concatenate(blocks, axis=0)


def send_kernel(picked, mine, theirs, weight, other_weight, *outs):
    both = [
        jnp.concatenate([mine[at : at + many, :], theirs[at : at + many, :]], axis=1)
        for at, many in picked
    ]
    terms = dot(jnp.concatenate(both, axis=0), out_matrix(weight, other_weight))
    at = 0
    for out in outs:
        out[...] = terms[at : at + out.shape[0]].astype(out.dtype)
        at += out.shape[0]


def weight_part(weights, blocks):
    _, xs, _, block, wide = weights.shape
    return pl.BlockSpec((2, xs, 2, block, wide), lambda i: (i, 0, blocks // 2, 0, 0))


def terms_to_send(mine, theirs, weights, other_weights, picked):
    planes, xs, _, _, wide = weights.shape
    columns = 2 * xs * wide
    whole = pl.BlockSpec(mine.shape, lambda i: (0, 0))
    return local(
        functools.partial(send_kernel, picked),
        tuple(jax.ShapeDtypeStruct((many, planes * xs * wide), jnp.bfloat16) for _, many in picked),
        52,
        flops=2_000_000_000,
        moved_bytes=8_000_000,
        grid=(planes // 2,),
        in_specs=[whole, whole, weight_part(weights, 6), weight_part(other_weights, 0)],
        out_specs=tuple(pl.BlockSpec((many, columns), lambda i: (0, i)) for _, many in picked),
    )(mine, theirs, weights, other_weights)


def keep_kernel(
    place, tokens, mine, theirs, weight, other_weight, match_mine, match_theirs, _, own, down, up, *rest
):
    *sums, total = rest
    step = pl.program_id(0)
    terms = dot(
        jnp.concatenate([mine[...], theirs[...]], axis=1), out_matrix(weight, other_weight)
    )
    rows, mid = own.shape[0], down.shape[0]
    own[...] = terms[:rows]
    down[...] = terms[2 * rows - mid : 2 * rows]
    up[...] = terms[2 * rows : 2 * rows + mid]
    with_tokens = terms[:rows] + tokens[...].astype(jnp.float32)
    rounded = jnp.concatenate([with_tokens, terms[rows:]], axis=0).astype(jnp.bfloat16)
    product = dot(rounded, match_matrix(place, match_mine, match_theirs))

    @pl.when(step == 0)
    def _():
        total[...] = product

    @pl.when(step > 0)
    def _():
        total[...] += product

    @pl.when(step == pl.num_programs(0) - 1)
    def _():
        for i, out in enumerate(sums):
            out[...] = total[i * rows : (i + 1) * rows].astype(out.dtype)


def terms_to_keep(core, tokens, mine, theirs, weights, other_weights, earlier):
    planes, xs, _, block, wide = weights.shape
    rows, depth = tokens.shape
    width = 4 * wide
    columns = 2 * xs * wide
    whole = pl.BlockSpec(mine.shape, lambda i: (0, 0))
    full = pl.BlockSpec((rows, columns), lambda i: (0, i))
    half = pl.BlockSpec((rows // 2, columns), lambda i: (0, i))
    square = pl.BlockSpec((rows, width), lambda i: (0, 0))
    f32, bf16 = jnp.float32, jnp.bfloat16
    return local(
        keep_kernel,
        (jax.ShapeDtypeStruct((rows, depth), f32),)
        + (jax.ShapeDtypeStruct((rows // 2, depth), f32),) * 2
        + (jax.ShapeDtypeStruct((rows, width), f32),)
        + (jax.ShapeDtypeStruct((rows, width), bf16),) * 3,
        52,
        flops=4_000_000_000,
        moved_bytes=16_000_000,
        grid=(planes // 2,),
        in_specs=[
            pl.BlockSpec(memory_space=pltpu.SMEM),
            full,
            whole,
            whole,
            weight_part(weights, 6),
            weight_part(other_weights, 0),
            weight_part(weights, 8),
            weight_part(other_weights, 2),
            pl.BlockSpec(memory_space=pltpu.HBM),
        ],
        out_specs=(full, half, half) + (square,) * 4,
        scratch_shapes=[pltpu.VMEM((4 * rows, width), f32)],
    )(
        core.astype(jnp.int32).reshape(1),
        tokens,
        mine,
        theirs,
        weights,
        other_weights,
        weights,
        other_weights,
        earlier,
    )


def added_kernel(a, b, c, d, first, second):
    first[...] = (a[...] + b[...].astype(jnp.float32)).astype(first.dtype)
    second[...] = (c[...] + d[...].astype(jnp.float32)).astype(second.dtype)


def added(a, b, c, d):
    return local(added_kernel, (jax.ShapeDtypeStruct(a.shape, b.dtype),) * 2, 20)(a, b, c, d)


def features_kernel(tokens, own, low_a, high_a, low_b, high_b, features):
    summed = own[...]
    summed = summed + jnp.concatenate([low_a[...], high_a[...]], axis=0).astype(jnp.float32)
    summed = summed + jnp.concatenate([low_b[...], high_b[...]], axis=0).astype(jnp.float32)
    features[...] = (tokens[...].astype(jnp.float32) + summed).astype(jnp.bfloat16)


def features_of(tokens, own, halves):
    rows, depth = tokens.shape
    columns = 1024
    whole = pl.BlockSpec((rows, columns), lambda i: (0, i))
    half = pl.BlockSpec((rows // 2, columns), lambda i: (0, i))
    return local(
        features_kernel,
        jax.ShapeDtypeStruct((rows, depth), jnp.bfloat16),
        20,
        grid=(depth // columns,),
        in_specs=[whole, whole] + [half] * 4,
        out_specs=whole,
    )(tokens, own, *halves)


def matcher_kernel(*refs):
    descriptor, qkv, out_weight, *pieces, matched, keys, values, mixed = refs
    rows, width = descriptor.shape
    bf16 = jnp.bfloat16
    queries = dot(descriptor[...], qkv[:, :width]).astype(bf16)
    at = 0
    for piece in pieces:
        count = piece.shape[0]
        keys[at : at + count, :] = dot(piece[...], qkv[:, width : 2 * width]).astype(bf16)
        values[at : at + count, :] = dot(piece[...], qkv[:, 2 * width :]).astype(bf16)
        at += count
    head_width = width // MATCH_HEADS
    pair = 2 * head_width
    low = lax.broadcasted_iota(jnp.int32, (rows, pair), 1) < head_width
    for first in range(0, width, pair):
        span = slice(first, first + pair)
        two = queries[:, span]
        results = []
        for chosen in (low, jnp.logical_not(low)):
            asked = jnp.where(chosen, two, jnp.zeros_like(two))
            scale = 1.0 / math.sqrt(head_width)
            results.append(attend(asked, keys[:, span], values[:, span], scale))
        mixed[:, span] = jnp.where(low, results[0], results[1]).astype(bf16)
    matched[...] = (descriptor[...].astype(jnp.float32) + dot(mixed[...], out_weight[...])).astype(
        bf16
    )


def match(descriptor, pieces, qkv, out_weight):
    count = sum(piece.shape[0] for piece in pieces)
    width = descriptor.shape[1]
    return local(
        matcher_kernel,
        jax.ShapeDtypeStruct(descriptor.shape, jnp.bfloat16),
        24,
        scratch_shapes=[
            pltpu.VMEM((count, width), jnp.bfloat16),
            pltpu.VMEM((count, width), jnp.bfloat16),
            pltpu.VMEM(descriptor.shape, jnp.bfloat16),
        ],
    )(descriptor, qkv, out_weight, *pieces)


def per_device(
    tokens, norm_gain, norm_bias, qkv_weight, out_weight, match_weight, matcher_qkv, matcher_out
):
    bf16, f32 = jnp.bfloat16, jnp.float32
    width = matcher_out.shape[0]
    rows, features_width = tokens.shape
    mid = rows // 2

    block, wide = qkv_weight.shape[0], out_weight.shape[1]

    def in_blocks(weight):
        return weight.reshape(weight.shape[0], -1, wide).transpose(1, 0, 2).reshape(-1, wide)

    part = match_weight.shape[0] // 2
    match_low = in_blocks(match_weight[:part])
    match_high = in_blocks(match_weight[part:])
    match_half = jnp.where(lax.axis_index("xl") == 0, match_low, match_high)
    packed = swapped_roles(
        jnp.concatenate([in_blocks(qkv_weight), out_weight, match_half], axis=0)
    )
    weights = lax.all_gather(packed, ("z", "xh", "xl"), axis=0, tiled=True)
    weights = weights.reshape(8, 4, 10, block, wide)

    tokens = swapped_roles(tokens)
    normed = layer_norm(tokens, norm_gain, norm_bias)
    pieces = [normed] + [moved(normed, along_y(k)) for k in DISTANCES]
    pieces += [moved(piece, other_core) for piece in pieces]
    pieces = together(*pieces, flops=WAIT)
    other_weights = moved(after(weights[:, :, 6:], pieces[0]), other_core)
    mine, theirs = attention(pieces, weights)

    both = (mine, moved(theirs, other_core), weights, other_weights)
    far_low, far_high, up_high, down_low = terms_to_send(
        *both, [(3 * rows, mid), (3 * rows + mid, mid), (2 * rows + mid, mid), (rows, mid)]
    )
    own, down_high, up_low, *sums = terms_to_keep(
        lax.axis_index("core"), tokens, *both, far_low
    )
    far_low, far_high = moved(far_low, along_y(1)), moved(far_high, along_y(-1))
    up_high, down_low = moved(up_high, along_y(1)), moved(down_low, along_y(-1))

    received = [moved(part, along_y(k)) for part, k in zip(sums[1:], (-1, 1, 2))]
    descriptor = sums[0] + sum(part.astype(f32) for part in received)
    descriptor = descriptor.astype(bf16)

    up_low, down_high = added(up_low, far_low, down_high, far_high)
    up_low, down_high = moved(up_low, along_y(1)), moved(down_high, along_y(-1))
    features = features_of(tokens, own, (up_low, up_high, down_low, down_high))

    partner = moved(descriptor, along_z(4))
    quarter = jnp.concatenate([partner] + [moved(partner, along_y(k)) for k in DISTANCES], axis=0)
    pieces = [quarter, moved(quarter, other_core)]
    matched = match(descriptor, pieces, matcher_qkv, matcher_out)
    return (swapped_roles(features), swapped_roles(matched))


def solution(mesh):
    fine = Mesh(mesh.devices.reshape(SIZES), AXES)
    dp, tensor = ("z", "xh", "core"), ("xl", "y")
    return jax.shard_map(
        per_device,
        mesh=fine,
        in_specs=(
            P(AXES, None),
            P(),
            P(),
            P(dp, tensor),
            P(tensor, dp),
            P(dp, None),
            P(),
            P(),
        ),
        out_specs=(P(AXES, None), P(AXES, None)),
        check_vma=False,
    )
```

```python
import functools
import itertools
import math

import jax
import jax.numpy as jnp
from jax import lax
from jax.experimental import pallas as pl
from jax.experimental.pallas import tpu as pltpu
from jax.sharding import Mesh
from jax.sharding import PartitionSpec as P

HEAD_DIM = 128
MATCH_HEADS = 8
DISTANCES = (1, -1, 2)
WAIT = 6_000_000_000
LOG2_E = math.log2(math.e)
AXES = ("z", "xh", "core", "xl", "y")
SIZES = (8, 2, 2, 2, 4)


def moved(block, target):
    def index(place):
        at = 0
        for axis, size in zip(AXES, SIZES):
            at = at * size + place[axis]
        return at

    route = []
    for values in itertools.product(*[range(size) for size in SIZES]):
        place = dict(zip(AXES, values))
        route.append((index(place), index({**place, **target(place)})))
    return lax.ppermute(block, AXES, route)


def along_y(k):
    return lambda p: {"y": (p["y"] + k) % 4}


def along_z(k):
    return lambda p: {"z": (p["z"] + k) % 8}


def two_along_z(p):
    return {"z": (p["z"] + 2 - 4 * (p["z"] % 2)) % 8}


def along_x(k):
    def target(p):
        x = (p["xh"] * 2 + p["xl"] + k) % 4
        return {"xh": x // 2, "xl": x % 2}

    return target


def other_core(p):
    return {"core": 1 - p["core"]}


def swapped_roles(block):
    return moved(block, lambda p: {"core": p["xl"], "xl": p["core"]})


def gathered_z(block, z):
    pair = after(jnp.stack([block, moved(block, along_z(4))]))
    pairs = [pair, moved(pair, along_z(1)), moved(pair, along_z(-1)), moved(pair, two_along_z)]
    sign = 1 - 2 * (z % 2)
    whole = jnp.zeros((2, 4) + block.shape, block.dtype)
    rest = (0,) * block.ndim
    for k, pair in zip((0, 1, -1, 2 * sign), pairs):
        owner = (z - k) % 8
        low = jnp.where(owner < 4, pair, pair[::-1])
        whole = lax.dynamic_update_slice(whole, low[:, None], (0, owner % 4) + rest)
    return whole.reshape((8,) + block.shape)


def along_x_parts(block):
    return [block] + [moved(block, along_x(k)) for k in DISTANCES]


def gathered_x(block, x, axis):
    whole = jnp.zeros(block.shape[:axis] + (4,) + block.shape[axis:], block.dtype)
    for k, part in zip((0,) + DISTANCES, along_x_parts(block)):
        at = [0] * whole.ndim
        at[axis] = (x - k) % 4
        whole = lax.dynamic_update_slice(whole, jnp.expand_dims(part, axis), at)
    return whole


def layer_norm(rows_in, norm_gain, norm_bias):
    values = rows_in.astype(jnp.float32)
    center = jnp.mean(values, axis=-1, keepdims=True)
    spread = jnp.mean((values - center) ** 2, axis=-1, keepdims=True)
    return ((values - center) * lax.rsqrt(spread + 1e-06) * norm_gain + norm_bias).astype(
        jnp.bfloat16
    )


def local(kernel, out_shape, mebibytes, flops=0, moved_bytes=0, **kwargs):
    return pl.pallas_call(
        kernel,
        out_shape=out_shape,
        compiler_params=pltpu.CompilerParams(vmem_limit_bytes=mebibytes << 20),
        cost_estimate=pl.CostEstimate(flops=flops, bytes_accessed=moved_bytes, transcendentals=0),
        **kwargs,
    )


def together(*values, flops=0):
    def kernel(*refs):
        pass

    held = pl.BlockSpec(memory_space=pltpu.HBM)
    count = len(values)
    return local(
        kernel,
        tuple(jax.ShapeDtypeStruct(value.shape, value.dtype) for value in values),
        1,
        flops=flops,
        in_specs=[held] * count,
        out_specs=(held,) * count,
        input_output_aliases={i: i for i in range(count)},
    )(*values)


def after(value, *earlier):
    def kernel(*refs):
        pass

    held = pl.BlockSpec(memory_space=pltpu.HBM)
    return local(
        kernel,
        jax.ShapeDtypeStruct(value.shape, value.dtype),
        1,
        in_specs=[held] * (1 + len(earlier)),
        out_specs=held,
        input_output_aliases={0: 0},
    )(value, *earlier)


def attend(queries, keys, values, scale):
    scores = dot_transposed(queries, keys)
    raised = jnp.exp2((scores - jnp.max(scores, axis=-1, keepdims=True)) * (scale * LOG2_E))
    mixed = dot(raised.astype(jnp.bfloat16), values)
    return mixed * (1.0 / jnp.sum(raised, axis=-1, keepdims=True))


def dot(left, right):
    return jnp.dot(left, right, preferred_element_type=jnp.float32)


def dot_transposed(left, right):
    return lax.dot_general(
        left, right, (((1,), (1,)), ((), ())), preferred_element_type=jnp.float32
    )


PARTS = 4


def attention_kernel(*refs):
    *pieces, weight, _, own, other, held, held_weight, total, projected, sems = refs
    depth = held.shape[1] // PARTS
    block = weight.shape[3]
    copies = []
    for part in range(PARTS):
        span = pl.ds(part * depth, depth)
        planes = pl.ds(part * 8 // PARTS, 8 // PARTS)
        moves = []
        for column in range(held_weight.shape[3] // block):
            there = held_weight.at[planes, :, :, pl.ds(column * block, block)]
            moves.append((weight.at[planes, :, column], there))
        at = 0
        for piece in pieces:
            count = piece.shape[0]
            moves.append((piece.at[:, span], held.at[pl.ds(at, count), span]))
            at += count
        starting = [
            pltpu.make_async_copy(source, there, sems.at[part, i])
            for i, (source, there) in enumerate(moves)
        ]
        for copy in starting:
            copy.start()
        copies.append(starting)
    step = 512
    for part in range(PARTS):
        for copy in copies[part]:
            copy.wait()
        span = pl.ds(part * depth, depth)
        planes = pl.ds(part * 8 // PARTS, 8 // PARTS)

        @pl.loop(0, held.shape[0], step=step)
        def _(row, part=part, span=span, planes=planes):
            rows = pl.ds(pl.multiple_of(row, step), step)
            term = dot(held[rows, span], held_weight[planes].reshape(depth, -1))
            if part:
                term = total[rows, :] + term
            if part < PARTS - 1:
                total[rows, :] = term
            else:
                projected[rows, :] = term.astype(jnp.bfloat16)

    step = 256
    for head in range(2):
        at = head * 3 * HEAD_DIM
        for half, out in enumerate((own, other)):

            @pl.loop(0, out.shape[0], step=step)
            def _(row, at=at, half=half, out=out, head=head):
                rows = pl.ds(pl.multiple_of(half * out.shape[0] + row, step), step)
                mixed = attend(
                    projected[rows, at : at + HEAD_DIM],
                    projected[:, at + HEAD_DIM : at + 2 * HEAD_DIM],
                    projected[:, at + 2 * HEAD_DIM : at + 3 * HEAD_DIM],
                    1.0 / math.sqrt(HEAD_DIM),
                )
                out[pl.ds(pl.multiple_of(row, step), step), pl.ds(head * HEAD_DIM, HEAD_DIM)] = (
                    mixed.astype(jnp.bfloat16)
                )


def attention(pieces, weight, earlier):
    count = sum(piece.shape[0] for piece in pieces)
    depth = pieces[0].shape[1]
    block = weight.shape[3]
    columns = 6 * block
    result = jax.ShapeDtypeStruct((count // 2, columns // 3), jnp.bfloat16)
    return local(
        attention_kernel,
        (result, result),
        60,
        flops=2 * count * depth * columns,
        moved_bytes=2 * depth * (count + columns),
        in_specs=[pl.BlockSpec(memory_space=pltpu.HBM)] * (len(pieces) + 2),
        out_specs=(pl.BlockSpec(memory_space=pltpu.VMEM),) * 2,
        scratch_shapes=[
            pltpu.VMEM((count, depth), jnp.bfloat16),
            pltpu.VMEM((8, 4, block, columns), jnp.bfloat16),
            pltpu.VMEM((count, columns), jnp.float32),
            pltpu.VMEM((count, columns), jnp.bfloat16),
            pltpu.SemaphoreType.DMA((PARTS, len(pieces) + 6)),
        ],
    )(*pieces, weight, earlier)


def out_matrix(weight, other_weight):
    planes, xs, halves = weight.shape[:3]
    return jnp.concatenate(
        [
            jnp.concatenate([w[p, x, h] for p in range(planes) for x in range(xs)], axis=1)
            for w in (weight, other_weight)
            for h in range(halves)
        ],
        axis=0,
    )


def match_matrix(weight):
    planes, cores, highs = weight.shape[:3]
    blocks = [weight[p, c, h] for p in range(planes) for h in range(highs) for c in range(cores)]
    return jnp.concatenate(blocks, axis=0)


def send_kernel(skipped, picked, mine, theirs, weight, other_weight, *refs):
    outs = refs[skipped:]
    both = [
        jnp.concatenate([mine[at : at + many, :], theirs[at : at + many, :]], axis=1)
        for at, many in picked
    ]
    products = dot(jnp.concatenate(both, axis=0), out_matrix(weight, other_weight))
    at = 0
    for out in outs:
        out[...] = products[at : at + out.shape[0]].astype(out.dtype)
        at += out.shape[0]


def weight_part(weight):
    return pl.BlockSpec((2,) + weight.shape[1:], lambda i: (i, 0, 0, 0, 0))


def terms(mine, theirs, weight, other_weight, picked, dtype, earlier=()):
    earlier = list(earlier)
    planes, xs, _, _, wide = weight.shape
    columns = 2 * xs * wide
    whole = pl.BlockSpec(mine.shape, lambda i: (0, 0))
    return local(
        functools.partial(send_kernel, len(earlier), picked),
        tuple(jax.ShapeDtypeStruct((many, planes * xs * wide), dtype) for _, many in picked),
        52,
        flops=2_000_000_000,
        moved_bytes=8_000_000,
        grid=(planes // 2,),
        in_specs=[whole, whole, weight_part(weight), weight_part(other_weight)]
        + [pl.BlockSpec(memory_space=pltpu.HBM)] * len(earlier),
        out_specs=tuple(pl.BlockSpec((many, columns), lambda i: (0, i)) for _, many in picked),
    )(mine, theirs, weight, other_weight, *earlier)


def descriptor_kernel(tokens, mine, theirs, weight, other_weight, match_weight, _, __, *rest):
    *sums, total = rest
    step = pl.program_id(0)
    rows = tokens.shape[0]
    both = jnp.concatenate([mine[...], theirs[...]], axis=1)
    products = dot(both, out_matrix(weight, other_weight))
    with_tokens = products[:rows] + tokens[...].astype(jnp.float32)
    rounded = jnp.concatenate([with_tokens, products[rows:]], axis=0).astype(jnp.bfloat16)
    product = dot(rounded, match_matrix(match_weight))

    @pl.when(step == 0)
    def _():
        total[...] = product

    @pl.when(step > 0)
    def _():
        total[...] += product

    @pl.when(step == pl.num_programs(0) - 1)
    def _():
        for i, out in enumerate(sums):
            out[...] = total[i * rows : (i + 1) * rows].astype(out.dtype)


def descriptor_terms(tokens, mine, theirs, weight, other_weight, match_weight, *earlier):
    planes, xs, _, _, wide = weight.shape
    rows = tokens.shape[0]
    width = match_weight.shape[-1]
    whole = pl.BlockSpec(mine.shape, lambda i: (0, 0))
    square = pl.BlockSpec((rows, width), lambda i: (0, 0))
    f32, bf16 = jnp.float32, jnp.bfloat16
    return local(
        descriptor_kernel,
        (jax.ShapeDtypeStruct((rows, width), f32),)
        + (jax.ShapeDtypeStruct((rows, width), bf16),) * 3,
        52,
        flops=4_000_000_000,
        moved_bytes=12_000_000,
        grid=(planes // 2,),
        in_specs=[
            pl.BlockSpec((rows, 2 * xs * wide), lambda i: (0, i)),
            whole,
            whole,
            weight_part(weight),
            weight_part(other_weight),
            weight_part(match_weight),
        ]
        + [pl.BlockSpec(memory_space=pltpu.HBM)] * len(earlier),
        out_specs=(square,) * 4,
        scratch_shapes=[pltpu.VMEM((4 * rows, width), f32)],
    )(tokens, mine, theirs, weight, other_weight, match_weight, *earlier)


def added_kernel(a, b, c, d, first, second):
    first[...] = (a[...] + b[...].astype(jnp.float32)).astype(first.dtype)
    second[...] = (c[...] + d[...].astype(jnp.float32)).astype(second.dtype)


def added(a, b, c, d):
    return local(added_kernel, (jax.ShapeDtypeStruct(a.shape, b.dtype),) * 2, 20)(a, b, c, d)


def features_kernel(tokens, own, low_a, high_a, low_b, high_b, features):
    summed = own[...]
    summed = summed + jnp.concatenate([low_a[...], high_a[...]], axis=0).astype(jnp.float32)
    summed = summed + jnp.concatenate([low_b[...], high_b[...]], axis=0).astype(jnp.float32)
    features[...] = (tokens[...].astype(jnp.float32) + summed).astype(jnp.bfloat16)


def features_of(tokens, own, halves):
    rows, depth = tokens.shape
    columns = 1024
    whole = pl.BlockSpec((rows, columns), lambda i: (0, i))
    half = pl.BlockSpec((rows // 2, columns), lambda i: (0, i))
    return local(
        features_kernel,
        jax.ShapeDtypeStruct((rows, depth), jnp.bfloat16),
        20,
        grid=(depth // columns,),
        in_specs=[whole, whole] + [half] * 4,
        out_specs=whole,
    )(tokens, own, *halves)


def matcher_kernel(*refs):
    descriptor, qkv, out_weight, *pieces, matched, keys, values, mixed = refs
    rows, width = descriptor.shape
    bf16 = jnp.bfloat16
    queries = dot(descriptor[...], qkv[:, :width]).astype(bf16)
    at = 0
    for piece in pieces:
        count = piece.shape[0]
        keys[at : at + count, :] = dot(piece[...], qkv[:, width : 2 * width]).astype(bf16)
        values[at : at + count, :] = dot(piece[...], qkv[:, 2 * width :]).astype(bf16)
        at += count
    head_width = width // MATCH_HEADS
    pair = 2 * head_width
    low = lax.broadcasted_iota(jnp.int32, (rows, pair), 1) < head_width
    for first in range(0, width, pair):
        span = slice(first, first + pair)
        two = queries[:, span]
        results = []
        for chosen in (low, jnp.logical_not(low)):
            asked = jnp.where(chosen, two, jnp.zeros_like(two))
            scale = 1.0 / math.sqrt(head_width)
            results.append(attend(asked, keys[:, span], values[:, span], scale))
        mixed[:, span] = jnp.where(low, results[0], results[1]).astype(bf16)
    matched[...] = (descriptor[...].astype(jnp.float32) + dot(mixed[...], out_weight[...])).astype(
        bf16
    )


def match(descriptor, pieces, qkv, out_weight):
    count = sum(piece.shape[0] for piece in pieces)
    width = descriptor.shape[1]
    return local(
        matcher_kernel,
        jax.ShapeDtypeStruct(descriptor.shape, jnp.bfloat16),
        24,
        scratch_shapes=[
            pltpu.VMEM((count, width), jnp.bfloat16),
            pltpu.VMEM((count, width), jnp.bfloat16),
            pltpu.VMEM(descriptor.shape, jnp.bfloat16),
        ],
    )(descriptor, qkv, out_weight, *pieces)


def per_device(
    tokens, norm_gain, norm_bias, qkv_weight, out_weight, match_weight, matcher_qkv, matcher_out
):
    bf16, f32 = jnp.bfloat16, jnp.float32
    z = lax.axis_index("z")
    x = lax.axis_index("xh") * 2 + lax.axis_index("xl")
    width = matcher_out.shape[0]
    rows, features_width = tokens.shape
    mid = rows // 2

    block, wide = qkv_weight.shape[0], out_weight.shape[1]
    packed = qkv_weight.reshape(block, -1, wide).transpose(1, 0, 2).reshape(-1, wide)
    packed = swapped_roles(jnp.concatenate([packed, out_weight], axis=0))
    split = packed.shape[0] - out_weight.shape[0]
    weights = lax.all_gather(packed[:split], ("z", "xh", "xl"), axis=0, tiled=True)
    weights = weights.reshape(8, 4, split // block, block, wide)

    match_weight = after(match_weight, packed)
    other_half = moved(match_weight, lambda p: {"xh": 1 - p["xh"], "xl": 1 - p["xl"]})
    match_pair = jnp.where(
        lax.axis_index("xh") == 0,
        jnp.concatenate([match_weight, other_half], axis=0),
        jnp.concatenate([other_half, match_weight], axis=0),
    )
    match_all = lax.all_gather(match_pair, ("z", "core"), axis=0, tiled=True)
    match_all = match_all.reshape(8, 2, 2, match_weight.shape[0], width)

    tokens = swapped_roles(tokens)
    normed = layer_norm(tokens, norm_gain, norm_bias)
    out_own = gathered_x(gathered_z(packed[split:], z), x, 1)
    out_other = moved(out_own, other_core)
    pieces = [normed] + [moved(normed, along_y(k)) for k in DISTANCES]
    pieces += [moved(piece, other_core) for piece in pieces]
    pieces = together(*pieces, flops=WAIT)
    mine, theirs = attention(pieces, weights, out_own)

    shape = (8, 4, 2, block, wide)
    both = (mine, moved(theirs, other_core), out_own.reshape(shape), out_other.reshape(shape))
    far_low, far_high, up_high, down_low = terms(
        *both, [(3 * rows, mid), (3 * rows + mid, mid), (2 * rows + mid, mid), (rows, mid)], bf16
    )
    own, down_high, up_low = terms(
        *both, [(0, rows), (rows + mid, mid), (2 * rows, mid)], f32, [far_low]
    )
    far_low, far_high = moved(far_low, along_y(1)), moved(far_high, along_y(-1))
    up_high, down_low = moved(up_high, along_y(1)), moved(down_low, along_y(-1))
    up_low, down_high = added(up_low, far_low, down_high, far_high)
    up_low, down_high = moved(up_low, along_y(1)), moved(down_high, along_y(-1))
    sums = descriptor_terms(tokens, *both, match_all, up_high, down_low)
    features = features_of(tokens, own, (up_low, up_high, down_low, down_high))

    received = [moved(part, along_y(k)) for part, k in zip(sums[1:], (-1, 1, 2))]
    descriptor = sums[0] + sum(part.astype(f32) for part in received)
    descriptor = descriptor.astype(bf16)
    partner = moved(descriptor, along_z(4))
    quarter = jnp.concatenate([partner] + [moved(partner, along_y(k)) for k in DISTANCES], axis=0)
    pieces = [quarter, moved(quarter, other_core)]
    matched = match(descriptor, pieces, matcher_qkv, matcher_out)
    return (swapped_roles(features), swapped_roles(matched))


def solution(mesh):
    fine = Mesh(mesh.devices.reshape(SIZES), AXES)
    dp, tensor = ("z", "xh", "core"), ("xl", "y")
    return jax.shard_map(
        per_device,
        mesh=fine,
        in_specs=(
            P(AXES, None),
            P(),
            P(),
            P(dp, tensor),
            P(tensor, dp),
            P(dp, None),
            P(),
            P(),
        ),
        out_specs=(P(AXES, None), P(AXES, None)),
        check_vma=False,
    )
```

```python
import functools
import itertools
import math

import jax
import jax.numpy as jnp
from jax import lax
from jax.experimental import pallas as pl
from jax.experimental.pallas import tpu as pltpu
from jax.sharding import Mesh
from jax.sharding import PartitionSpec as P

HEAD_DIM = 128
MATCH_HEADS = 8
DISTANCES = (1, -1, 2)
WAIT = 6_000_000_000
LOG2_E = math.log2(math.e)
AXES = ("z", "xh", "core", "xl", "y")
SIZES = (8, 2, 2, 2, 4)


def moved(block, target):
    def index(place):
        at = 0
        for axis, size in zip(AXES, SIZES):
            at = at * size + place[axis]
        return at

    route = []
    for values in itertools.product(*[range(size) for size in SIZES]):
        place = dict(zip(AXES, values))
        route.append((index(place), index({**place, **target(place)})))
    return lax.ppermute(block, AXES, route)


def along_y(k):
    return lambda p: {"y": (p["y"] + k) % 4}


def along_z(k):
    return lambda p: {"z": (p["z"] + k) % 8}


def two_along_z(p):
    return {"z": (p["z"] + 2 - 4 * (p["z"] % 2)) % 8}


def along_x(k):
    def target(p):
        x = (p["xh"] * 2 + p["xl"] + k) % 4
        return {"xh": x // 2, "xl": x % 2}

    return target


def other_core(p):
    return {"core": 1 - p["core"]}


def swapped_roles(block):
    return moved(block, lambda p: {"core": p["xl"], "xl": p["core"]})


def gathered_z(block, z):
    pair = after(jnp.stack([block, moved(block, along_z(4))]))
    pairs = [pair, moved(pair, along_z(1)), moved(pair, along_z(-1)), moved(pair, two_along_z)]
    sign = 1 - 2 * (z % 2)
    whole = jnp.zeros((2, 4) + block.shape, block.dtype)
    rest = (0,) * block.ndim
    for k, pair in zip((0, 1, -1, 2 * sign), pairs):
        owner = (z - k) % 8
        low = jnp.where(owner < 4, pair, pair[::-1])
        whole = lax.dynamic_update_slice(whole, low[:, None], (0, owner % 4) + rest)
    return whole.reshape((8,) + block.shape)


def layer_norm(rows_in, norm_gain, norm_bias):
    values = rows_in.astype(jnp.float32)
    center = jnp.mean(values, axis=-1, keepdims=True)
    spread = jnp.mean((values - center) ** 2, axis=-1, keepdims=True)
    return ((values - center) * lax.rsqrt(spread + 1e-06) * norm_gain + norm_bias).astype(
        jnp.bfloat16
    )


def local(kernel, out_shape, mebibytes, flops=0, moved_bytes=0, **kwargs):
    return pl.pallas_call(
        kernel,
        out_shape=out_shape,
        compiler_params=pltpu.CompilerParams(vmem_limit_bytes=mebibytes << 20),
        cost_estimate=pl.CostEstimate(flops=flops, bytes_accessed=moved_bytes, transcendentals=0),
        **kwargs,
    )


def together(*values, flops=0):
    def kernel(*refs):
        pass

    held = pl.BlockSpec(memory_space=pltpu.HBM)
    count = len(values)
    return local(
        kernel,
        tuple(jax.ShapeDtypeStruct(value.shape, value.dtype) for value in values),
        1,
        flops=flops,
        in_specs=[held] * count,
        out_specs=(held,) * count,
        input_output_aliases={i: i for i in range(count)},
    )(*values)


def after(value, *earlier):
    def kernel(*refs):
        pass

    held = pl.BlockSpec(memory_space=pltpu.HBM)
    return local(
        kernel,
        jax.ShapeDtypeStruct(value.shape, value.dtype),
        1,
        in_specs=[held] * (1 + len(earlier)),
        out_specs=held,
        input_output_aliases={0: 0},
    )(value, *earlier)


def attend(queries, keys, values, scale):
    scores = dot_transposed(queries, keys)
    raised = jnp.exp2((scores - jnp.max(scores, axis=-1, keepdims=True)) * (scale * LOG2_E))
    mixed = dot(raised.astype(jnp.bfloat16), values)
    return mixed * (1.0 / jnp.sum(raised, axis=-1, keepdims=True))


def dot(left, right):
    return jnp.dot(left, right, preferred_element_type=jnp.float32)


def dot_transposed(left, right):
    return lax.dot_general(
        left, right, (((1,), (1,)), ((), ())), preferred_element_type=jnp.float32
    )


PARTS = 2


def attention_kernel(*refs):
    *pieces, weight, own, other, held, held_weight, total, projected, sems = refs
    depth = held.shape[1] // PARTS
    block = weight.shape[3]
    copies = []
    for part in range(PARTS):
        span = pl.ds(part * depth, depth)
        planes = pl.ds(part * 8 // PARTS, 8 // PARTS)
        moves = []
        for column in range(held_weight.shape[3] // block):
            there = held_weight.at[planes, :, :, pl.ds(column * block, block)]
            moves.append((weight.at[planes, :, column], there))
        at = 0
        for piece in pieces:
            count = piece.shape[0]
            moves.append((piece.at[:, span], held.at[pl.ds(at, count), span]))
            at += count
        starting = [
            pltpu.make_async_copy(source, there, sems.at[part, i])
            for i, (source, there) in enumerate(moves)
        ]
        for copy in starting:
            copy.start()
        copies.append(starting)
    step = 512
    for part in range(PARTS):
        for copy in copies[part]:
            copy.wait()
        span = pl.ds(part * depth, depth)
        planes = pl.ds(part * 8 // PARTS, 8 // PARTS)

        @pl.loop(0, held.shape[0], step=step)
        def _(row, part=part, span=span, planes=planes):
            rows = pl.ds(pl.multiple_of(row, step), step)
            term = dot(held[rows, span], held_weight[planes].reshape(depth, -1))
            if part:
                term = total[rows, :] + term
            if part < PARTS - 1:
                total[rows, :] = term
            else:
                projected[rows, :] = term.astype(jnp.bfloat16)

    step = 256
    for head in range(2):
        at = head * 3 * HEAD_DIM
        for half, out in enumerate((own, other)):

            @pl.loop(0, out.shape[0], step=step)
            def _(row, at=at, half=half, out=out, head=head):
                rows = pl.ds(pl.multiple_of(half * out.shape[0] + row, step), step)
                mixed = attend(
                    projected[rows, at : at + HEAD_DIM],
                    projected[:, at + HEAD_DIM : at + 2 * HEAD_DIM],
                    projected[:, at + 2 * HEAD_DIM : at + 3 * HEAD_DIM],
                    1.0 / math.sqrt(HEAD_DIM),
                )
                out[pl.ds(pl.multiple_of(row, step), step), pl.ds(head * HEAD_DIM, HEAD_DIM)] = (
                    mixed.astype(jnp.bfloat16)
                )


def attention(pieces, weight):
    count = sum(piece.shape[0] for piece in pieces)
    depth = pieces[0].shape[1]
    block = weight.shape[3]
    columns = 6 * block
    result = jax.ShapeDtypeStruct((count // 2, columns // 3), jnp.bfloat16)
    return local(
        attention_kernel,
        (result, result),
        60,
        flops=2 * count * depth * columns,
        moved_bytes=2 * depth * (count + columns),
        in_specs=[pl.BlockSpec(memory_space=pltpu.HBM)] * (len(pieces) + 1),
        out_specs=(pl.BlockSpec(memory_space=pltpu.VMEM),) * 2,
        scratch_shapes=[
            pltpu.VMEM((count, depth), jnp.bfloat16),
            pltpu.VMEM((8, 4, block, columns), jnp.bfloat16),
            pltpu.VMEM((count, columns), jnp.float32),
            pltpu.VMEM((count, columns), jnp.bfloat16),
            pltpu.SemaphoreType.DMA((PARTS, len(pieces) + 6)),
        ],
    )(*pieces, weight)


def place_weights(matrix, place, parts, others):
    planes, _, block, wide = parts[0].shape
    for i, side in enumerate((parts, others)):
        for k, part in zip((0,) + DISTANCES, side):
            for plane in range(planes):
                at = (plane * 4 + (place[0] - k + 4) % 4) * wide
                columns = pl.ds(pl.multiple_of(at, wide), wide)
                for half in range(2):
                    first = (2 * i + half) * block
                    matrix[first : first + block, columns] = part[plane, half]


def match_matrix(weight):
    planes, cores, highs = weight.shape[:3]
    blocks = [weight[p, c, h] for p in range(planes) for h in range(highs) for c in range(cores)]
    return jnp.concatenate(blocks, axis=0)


def terms_kernel(skipped, picked, place, mine, theirs, *refs):
    parts, others, outs, matrix = refs[:4], refs[4:8], refs[8 + skipped : -1], refs[-1]
    place_weights(matrix, place, parts, others)
    both = [
        jnp.concatenate([mine[at : at + many, :], theirs[at : at + many, :]], axis=1)
        for spans, _ in picked
        for at, many in spans
    ]
    products = dot(jnp.concatenate(both, axis=0), matrix[...])
    at = 0
    for out in outs:
        out[...] = products[at : at + out.shape[0]].astype(out.dtype)
        at += out.shape[0]


def terms(x, mine, theirs, parts, picked, earlier=()):
    counts = [sum(many for _, many in spans) for spans, _ in picked]
    earlier = list(earlier)
    planes, halves, block, wide = parts[0].shape
    columns = 2 * 4 * wide
    whole = pl.BlockSpec(mine.shape, lambda i: (0, 0))
    part = pl.BlockSpec((2, halves, block, wide), lambda i: (i, 0, 0, 0))
    return local(
        functools.partial(terms_kernel, len(earlier), picked),
        tuple(
            jax.ShapeDtypeStruct((many, planes * 4 * wide), kind)
            for many, (_, kind) in zip(counts, picked)
        ),
        24,
        flops=2_000_000_000,
        moved_bytes=8_000_000,
        grid=(planes // 2,),
        in_specs=[pl.BlockSpec(memory_space=pltpu.SMEM), whole, whole]
        + [part] * 8
        + [pl.BlockSpec(memory_space=pltpu.HBM)] * len(earlier),
        out_specs=tuple(pl.BlockSpec((many, columns), lambda i: (0, i)) for many in counts),
        scratch_shapes=[pltpu.VMEM((4 * block, columns), jnp.bfloat16)],
    )(x.astype(jnp.int32).reshape(1), mine, theirs, *parts, *earlier)


def descriptor_kernel(tokens, own, down, down_high, up_low, up, match_weight, *rest):
    *sums, total = rest
    mid = up_low.shape[0]
    others = [down[mid:, :], down_high[...], up_low[...], up[...], down[:mid, :]]
    step = pl.program_id(0)
    rows = tokens.shape[0]
    with_tokens = (own[...] + tokens[...].astype(jnp.float32)).astype(jnp.bfloat16)
    product = dot(
        jnp.concatenate([with_tokens] + others, axis=0),
        match_matrix(match_weight),
    )

    @pl.when(step == 0)
    def _():
        total[...] = product

    @pl.when(step > 0)
    def _():
        total[...] += product

    @pl.when(step == pl.num_programs(0) - 1)
    def _():
        for i, out in enumerate(sums):
            out[...] = total[i * rows : (i + 1) * rows].astype(out.dtype)


def descriptor_terms(tokens, own, down, down_high, up_low, up, match_weight):
    rows, depth = tokens.shape
    width = match_weight.shape[-1]
    columns = 1024
    full = pl.BlockSpec((rows, columns), lambda i: (0, i))
    half = pl.BlockSpec((rows // 2, columns), lambda i: (0, i))
    square = pl.BlockSpec((rows, width), lambda i: (0, 0))
    f32, bf16 = jnp.float32, jnp.bfloat16
    return local(
        descriptor_kernel,
        (jax.ShapeDtypeStruct((rows, width), f32),)
        + (jax.ShapeDtypeStruct((rows, width), bf16),) * 3,
        52,
        flops=4_000_000_000,
        moved_bytes=12_000_000,
        grid=(depth // columns,),
        in_specs=[full, full, full, half, half, full]
        + [pl.BlockSpec((2,) + match_weight.shape[1:], lambda i: (i, 0, 0, 0, 0))],
        out_specs=(square,) * 4,
        scratch_shapes=[pltpu.VMEM((4 * rows, width), f32)],
    )(tokens, own, down, down_high, up_low, up, match_weight)


def added_kernel(a, b, c, d, _, first, second):
    first[...] = (a[...].astype(jnp.float32) + b[...].astype(jnp.float32)).astype(first.dtype)
    second[...] = (c[...].astype(jnp.float32) + d[...].astype(jnp.float32)).astype(second.dtype)


def added(a, b, c, d, earlier):
    rows, depth = a.shape
    columns = 1024
    part = pl.BlockSpec((rows, columns), lambda i: (0, i))
    return local(
        added_kernel,
        (jax.ShapeDtypeStruct(a.shape, b.dtype),) * 2,
        20,
        grid=(depth // columns,),
        in_specs=[part, pl.BlockSpec((rows, columns), lambda i: (1, i)), part, part]
        + [pl.BlockSpec(memory_space=pltpu.HBM)],
        out_specs=(part,) * 2,
    )(a, b, c, d, earlier)


def features_kernel(tokens, own, up_low, up, down, down_high, features):
    mid = up_low.shape[0]
    summed = own[...]
    from_below = [up_low[...], up[:mid, :]]
    from_above = [down[mid:, :], down_high[...]]
    summed = summed + jnp.concatenate(from_below, axis=0).astype(jnp.float32)
    summed = summed + jnp.concatenate(from_above, axis=0).astype(jnp.float32)
    features[...] = (tokens[...].astype(jnp.float32) + summed).astype(jnp.bfloat16)


def features_of(tokens, own, up_low, up, down, down_high):
    rows, depth = tokens.shape
    columns = 1024
    whole = pl.BlockSpec((rows, columns), lambda i: (0, i))
    half = pl.BlockSpec((rows // 2, columns), lambda i: (0, i))
    return local(
        features_kernel,
        jax.ShapeDtypeStruct((rows, depth), jnp.bfloat16),
        20,
        grid=(depth // columns,),
        in_specs=[whole, whole, half, whole, whole, half],
        out_specs=whole,
    )(tokens, own, up_low, up, down, down_high)


def matcher_kernel(*refs):
    descriptor, qkv, out_weight, *pieces, matched, keys, values, mixed = refs
    rows, width = descriptor.shape
    bf16 = jnp.bfloat16
    queries = dot(descriptor[...], qkv[:, :width]).astype(bf16)
    at = 0
    for piece in pieces:
        count = piece.shape[0]
        keys[at : at + count, :] = dot(piece[...], qkv[:, width : 2 * width]).astype(bf16)
        values[at : at + count, :] = dot(piece[...], qkv[:, 2 * width :]).astype(bf16)
        at += count
    head_width = width // MATCH_HEADS
    pair = 2 * head_width
    low = lax.broadcasted_iota(jnp.int32, (rows, pair), 1) < head_width
    for first in range(0, width, pair):
        span = slice(first, first + pair)
        two = queries[:, span]
        results = []
        for chosen in (low, jnp.logical_not(low)):
            asked = jnp.where(chosen, two, jnp.zeros_like(two))
            scale = 1.0 / math.sqrt(head_width)
            results.append(attend(asked, keys[:, span], values[:, span], scale))
        mixed[:, span] = jnp.where(low, results[0], results[1]).astype(bf16)
    matched[...] = (descriptor[...].astype(jnp.float32) + dot(mixed[...], out_weight[...])).astype(
        bf16
    )


def match(descriptor, pieces, qkv, out_weight):
    count = sum(piece.shape[0] for piece in pieces)
    width = descriptor.shape[1]
    return local(
        matcher_kernel,
        jax.ShapeDtypeStruct(descriptor.shape, jnp.bfloat16),
        24,
        scratch_shapes=[
            pltpu.VMEM((count, width), jnp.bfloat16),
            pltpu.VMEM((count, width), jnp.bfloat16),
            pltpu.VMEM(descriptor.shape, jnp.bfloat16),
        ],
    )(descriptor, qkv, out_weight, *pieces)


def per_device(
    tokens, norm_gain, norm_bias, qkv_weight, out_weight, match_weight, matcher_qkv, matcher_out
):
    bf16, f32 = jnp.bfloat16, jnp.float32
    z = lax.axis_index("z")
    x = lax.axis_index("xh") * 2 + lax.axis_index("xl")
    width = matcher_out.shape[0]
    rows, features_width = tokens.shape
    mid = rows // 2

    block, wide = qkv_weight.shape[0], out_weight.shape[1]
    packed = qkv_weight.reshape(block, -1, wide).transpose(1, 0, 2).reshape(-1, wide)
    packed = swapped_roles(jnp.concatenate([packed, out_weight], axis=0))
    split = packed.shape[0] - out_weight.shape[0]
    weights = lax.all_gather(packed[:split], ("z", "xh", "xl"), axis=0, tiled=True)
    weights = weights.reshape(8, 4, split // block, block, wide)

    match_weight = after(match_weight, packed)
    other_half = moved(match_weight, lambda p: {"xh": 1 - p["xh"], "xl": 1 - p["xl"]})
    match_pair = jnp.where(
        lax.axis_index("xh") == 0,
        jnp.concatenate([match_weight, other_half], axis=0),
        jnp.concatenate([other_half, match_weight], axis=0),
    )
    match_all = lax.all_gather(match_pair, ("z", "core"), axis=0, tiled=True)
    match_all = match_all.reshape(8, 2, 2, match_weight.shape[0], width)

    tokens = swapped_roles(tokens)
    normed = layer_norm(tokens, norm_gain, norm_bias)
    out_z = gathered_z(packed[split:], z)
    pieces = [normed] + [moved(normed, along_y(k)) for k in DISTANCES]
    *received, out_z = together(*pieces[1:], out_z)
    pieces = pieces[:1] + received
    pieces += [moved(piece, other_core) for piece in pieces]
    out_z = out_z.reshape(8, 2, block, wide)
    pieces = together(*pieces, flops=WAIT)
    parts = [out_z] + [moved(out_z, along_x(k)) for k in DISTANCES]
    others = [moved(out_z, other_core)]
    mine, theirs = attention(pieces, weights)
    mine, *parts[1:] = together(mine, *parts[1:])
    others += [moved(part, other_core) for part in parts[1:]]

    both = (x, mine, moved(theirs, other_core), parts + others)
    up, down = terms(
        *both,
        [([(2 * rows + mid, rows)], bf16), ([(3 * rows + mid, mid), (rows, mid)], bf16)],
    )
    own, down_high, up_low = terms(
        *both, [([(0, rows)], f32), ([(rows + mid, mid)], bf16), ([(2 * rows, mid)], bf16)], [up]
    )
    sums = descriptor_terms(tokens, own, down, down_high, up_low, up, match_all)
    up, down = moved(up, along_y(1)), moved(down, along_y(-1))
    sums_there = [moved(part, along_y(k)) for part, k in zip(sums[1:], (-1, 1, 2))]
    descriptor = sums[0] + sum(part.astype(f32) for part in sums_there)
    descriptor = descriptor.astype(bf16)
    up_low, down_high = added(up_low, up, down_high, down, descriptor)
    up_low, down_high = moved(up_low, along_y(1)), moved(down_high, along_y(-1))
    features = features_of(tokens, own, up_low, up, down, down_high)

    partner = moved(descriptor, along_z(4))
    quarter = jnp.concatenate([partner] + [moved(partner, along_y(k)) for k in DISTANCES], axis=0)
    pieces = [quarter, moved(quarter, other_core)]
    matched = match(descriptor, pieces, matcher_qkv, matcher_out)
    return (swapped_roles(features), swapped_roles(matched))


def solution(mesh):
    fine = Mesh(mesh.devices.reshape(SIZES), AXES)
    dp, tensor = ("z", "xh", "core"), ("xl", "y")
    return jax.shard_map(
        per_device,
        mesh=fine,
        in_specs=(
            P(AXES, None),
            P(),
            P(),
            P(dp, tensor),
            P(tensor, dp),
            P(dp, None),
            P(),
            P(),
        ),
        out_specs=(P(AXES, None), P(AXES, None)),
        check_vma=False,
    )
```

```python
import functools
import itertools
import math

import jax
import jax.numpy as jnp
from jax import lax
from jax.experimental import pallas as pl
from jax.experimental.pallas import tpu as pltpu
from jax.sharding import Mesh
from jax.sharding import PartitionSpec as P

HEAD_DIM = 128
MATCH_HEADS = 8
DISTANCES = (1, -1, 2)
WAIT = 6_000_000_000
LOG2_E = math.log2(math.e)
AXES = ("z", "xh", "core", "xl", "y")
SIZES = (8, 2, 2, 2, 4)


def moved(block, target):
    def index(place):
        at = 0
        for axis, size in zip(AXES, SIZES):
            at = at * size + place[axis]
        return at

    route = []
    for values in itertools.product(*[range(size) for size in SIZES]):
        place = dict(zip(AXES, values))
        route.append((index(place), index({**place, **target(place)})))
    return lax.ppermute(block, AXES, route)


def along_y(k):
    return lambda p: {"y": (p["y"] + k) % 4}


def along_z(k):
    return lambda p: {"z": (p["z"] + k) % 8}


def two_along_z(p):
    return {"z": (p["z"] + 2 - 4 * (p["z"] % 2)) % 8}


def along_x(k):
    def target(p):
        x = (p["xh"] * 2 + p["xl"] + k) % 4
        return {"xh": x // 2, "xl": x % 2}

    return target


def other_core(p):
    return {"core": 1 - p["core"]}


def swapped_roles(block):
    return moved(block, lambda p: {"core": p["xl"], "xl": p["core"]})


def gathered_z(block, z):
    pair = after(jnp.stack([block, moved(block, along_z(4))]))
    pairs = [pair, moved(pair, along_z(1)), moved(pair, along_z(-1)), moved(pair, two_along_z)]
    sign = 1 - 2 * (z % 2)
    whole = jnp.zeros((2, 4) + block.shape, block.dtype)
    rest = (0,) * block.ndim
    for k, pair in zip((0, 1, -1, 2 * sign), pairs):
        owner = (z - k) % 8
        low = jnp.where(owner < 4, pair, pair[::-1])
        whole = lax.dynamic_update_slice(whole, low[:, None], (0, owner % 4) + rest)
    return whole.reshape((8,) + block.shape)


def gathered_x(block, x, axis):
    whole = jnp.zeros(block.shape[:axis] + (4,) + block.shape[axis:], block.dtype)
    for k, part in [(0, block)] + [(k, moved(block, along_x(k))) for k in DISTANCES]:
        at = [0] * whole.ndim
        at[axis] = (x - k) % 4
        whole = lax.dynamic_update_slice(whole, jnp.expand_dims(part, axis), at)
    return whole


def layer_norm(rows_in, norm_gain, norm_bias):
    values = rows_in.astype(jnp.float32)
    center = jnp.mean(values, axis=-1, keepdims=True)
    spread = jnp.mean((values - center) ** 2, axis=-1, keepdims=True)
    return ((values - center) * lax.rsqrt(spread + 1e-06) * norm_gain + norm_bias).astype(
        jnp.bfloat16
    )


def local(kernel, out_shape, mebibytes, flops=0, moved_bytes=0, **kwargs):
    return pl.pallas_call(
        kernel,
        out_shape=out_shape,
        compiler_params=pltpu.CompilerParams(vmem_limit_bytes=mebibytes << 20),
        cost_estimate=pl.CostEstimate(flops=flops, bytes_accessed=moved_bytes, transcendentals=0),
        **kwargs,
    )


def together(*values, flops=0):
    def kernel(*refs):
        pass

    held = pl.BlockSpec(memory_space=pltpu.HBM)
    count = len(values)
    return local(
        kernel,
        tuple(jax.ShapeDtypeStruct(value.shape, value.dtype) for value in values),
        1,
        flops=flops,
        in_specs=[held] * count,
        out_specs=(held,) * count,
        input_output_aliases={i: i for i in range(count)},
    )(*values)


def after(value, *earlier):
    def kernel(*refs):
        pass

    held = pl.BlockSpec(memory_space=pltpu.HBM)
    return local(
        kernel,
        jax.ShapeDtypeStruct(value.shape, value.dtype),
        1,
        in_specs=[held] * (1 + len(earlier)),
        out_specs=held,
        input_output_aliases={0: 0},
    )(value, *earlier)


def attend(queries, keys, values, scale):
    scores = dot_transposed(queries, keys)
    raised = jnp.exp2((scores - jnp.max(scores, axis=-1, keepdims=True)) * (scale * LOG2_E))
    mixed = dot(raised.astype(jnp.bfloat16), values)
    return mixed * (1.0 / jnp.sum(raised, axis=-1, keepdims=True))


def dot(left, right):
    return jnp.dot(left, right, preferred_element_type=jnp.float32)


def dot_transposed(left, right):
    return lax.dot_general(
        left, right, (((1,), (1,)), ((), ())), preferred_element_type=jnp.float32
    )


PARTS = 2


def attention_kernel(*refs):
    *pieces, weight, _, own, other, held, held_weight, total, projected, sems = refs
    depth = held.shape[1] // PARTS
    block = weight.shape[3]
    copies = []
    for part in range(PARTS):
        span = pl.ds(part * depth, depth)
        planes = pl.ds(part * 8 // PARTS, 8 // PARTS)
        moves = []
        for column in range(held_weight.shape[3] // block):
            there = held_weight.at[planes, :, :, pl.ds(column * block, block)]
            moves.append((weight.at[planes, :, column], there))
        at = 0
        for piece in pieces:
            count = piece.shape[0]
            moves.append((piece.at[:, span], held.at[pl.ds(at, count), span]))
            at += count
        starting = [
            pltpu.make_async_copy(source, there, sems.at[part, i])
            for i, (source, there) in enumerate(moves)
        ]
        for copy in starting:
            copy.start()
        copies.append(starting)
    step = 512
    for part in range(PARTS):
        for copy in copies[part]:
            copy.wait()
        span = pl.ds(part * depth, depth)
        planes = pl.ds(part * 8 // PARTS, 8 // PARTS)

        @pl.loop(0, held.shape[0], step=step)
        def _(row, part=part, span=span, planes=planes):
            rows = pl.ds(pl.multiple_of(row, step), step)
            term = dot(held[rows, span], held_weight[planes].reshape(depth, -1))
            if part:
                term = total[rows, :] + term
            if part < PARTS - 1:
                total[rows, :] = term
            else:
                projected[rows, :] = term.astype(jnp.bfloat16)

    step = 256
    for head in range(2):
        at = head * 3 * HEAD_DIM
        for half, out in enumerate((own, other)):

            @pl.loop(0, out.shape[0], step=step)
            def _(row, at=at, half=half, out=out, head=head):
                rows = pl.ds(pl.multiple_of(half * out.shape[0] + row, step), step)
                mixed = attend(
                    projected[rows, at : at + HEAD_DIM],
                    projected[:, at + HEAD_DIM : at + 2 * HEAD_DIM],
                    projected[:, at + 2 * HEAD_DIM : at + 3 * HEAD_DIM],
                    1.0 / math.sqrt(HEAD_DIM),
                )
                out[pl.ds(pl.multiple_of(row, step), step), pl.ds(head * HEAD_DIM, HEAD_DIM)] = (
                    mixed.astype(jnp.bfloat16)
                )


def attention(pieces, weight, earlier):
    count = sum(piece.shape[0] for piece in pieces)
    depth = pieces[0].shape[1]
    block = weight.shape[3]
    columns = 6 * block
    result = jax.ShapeDtypeStruct((count // 2, columns // 3), jnp.bfloat16)
    return local(
        attention_kernel,
        (result, result),
        60,
        flops=2 * count * depth * columns,
        moved_bytes=2 * depth * (count + columns),
        in_specs=[pl.BlockSpec(memory_space=pltpu.HBM)] * (len(pieces) + 2),
        out_specs=(pl.BlockSpec(memory_space=pltpu.VMEM),) * 2,
        scratch_shapes=[
            pltpu.VMEM((count, depth), jnp.bfloat16),
            pltpu.VMEM((8, 4, block, columns), jnp.bfloat16),
            pltpu.VMEM((count, columns), jnp.float32),
            pltpu.VMEM((count, columns), jnp.bfloat16),
            pltpu.SemaphoreType.DMA((PARTS, len(pieces) + 6)),
        ],
    )(*pieces, weight, earlier)


def out_matrix(weight, other_weight):
    planes, xs, halves = weight.shape[:3]
    return jnp.concatenate(
        [
            jnp.concatenate([w[p, x, h] for p in range(planes) for x in range(xs)], axis=1)
            for w in (weight, other_weight)
            for h in range(halves)
        ],
        axis=0,
    )


def match_matrix(weight):
    planes, cores, highs = weight.shape[:3]
    blocks = [weight[p, c, h] for p in range(planes) for h in range(highs) for c in range(cores)]
    return jnp.concatenate(blocks, axis=0)


def terms_kernel(skipped, picked, mine, theirs, weight, other_weight, *refs):
    outs = refs[skipped:]
    both = [
        jnp.concatenate([mine[at : at + many, :], theirs[at : at + many, :]], axis=1)
        for spans, _ in picked
        for at, many in spans
    ]
    products = dot(jnp.concatenate(both, axis=0), out_matrix(weight, other_weight))
    at = 0
    for out in outs:
        out[...] = products[at : at + out.shape[0]].astype(out.dtype)
        at += out.shape[0]


def terms(mine, theirs, weight, other_weight, picked, earlier=()):
    counts = [sum(many for _, many in spans) for spans, _ in picked]
    earlier = list(earlier)
    planes, xs, _, _, wide = weight.shape
    columns = 2 * xs * wide
    whole = pl.BlockSpec(mine.shape, lambda i: (0, 0))
    part = pl.BlockSpec((2,) + weight.shape[1:], lambda i: (i, 0, 0, 0, 0))
    return local(
        functools.partial(terms_kernel, len(earlier), picked),
        tuple(
            jax.ShapeDtypeStruct((many, planes * xs * wide), kind)
            for many, (_, kind) in zip(counts, picked)
        ),
        24,
        flops=2_000_000_000,
        moved_bytes=8_000_000,
        grid=(planes // 2,),
        in_specs=[whole, whole, part, part]
        + [pl.BlockSpec(memory_space=pltpu.HBM)] * len(earlier),
        out_specs=tuple(pl.BlockSpec((many, columns), lambda i: (0, i)) for many in counts),
    )(mine, theirs, weight, other_weight, *earlier)


def descriptor_kernel(tokens, own, down, down_high, up_low, up, match_weight, *rest):
    *sums, total = rest
    mid = up_low.shape[0]
    others = [down[mid:, :], down_high[...], up_low[...], up[...], down[:mid, :]]
    step = pl.program_id(0)
    rows = tokens.shape[0]
    with_tokens = (own[...] + tokens[...].astype(jnp.float32)).astype(jnp.bfloat16)
    product = dot(
        jnp.concatenate([with_tokens] + others, axis=0),
        match_matrix(match_weight),
    )

    @pl.when(step == 0)
    def _():
        total[...] = product

    @pl.when(step > 0)
    def _():
        total[...] += product

    @pl.when(step == pl.num_programs(0) - 1)
    def _():
        for i, out in enumerate(sums):
            out[...] = total[i * rows : (i + 1) * rows].astype(out.dtype)


def descriptor_terms(tokens, own, down, down_high, up_low, up, match_weight):
    rows, depth = tokens.shape
    width = match_weight.shape[-1]
    columns = 1024
    full = pl.BlockSpec((rows, columns), lambda i: (0, i))
    half = pl.BlockSpec((rows // 2, columns), lambda i: (0, i))
    square = pl.BlockSpec((rows, width), lambda i: (0, 0))
    f32, bf16 = jnp.float32, jnp.bfloat16
    return local(
        descriptor_kernel,
        (jax.ShapeDtypeStruct((rows, width), f32),)
        + (jax.ShapeDtypeStruct((rows, width), bf16),) * 3,
        52,
        flops=4_000_000_000,
        moved_bytes=12_000_000,
        grid=(depth // columns,),
        in_specs=[full, full, full, half, half, full]
        + [pl.BlockSpec((2,) + match_weight.shape[1:], lambda i: (i, 0, 0, 0, 0))],
        out_specs=(square,) * 4,
        scratch_shapes=[pltpu.VMEM((4 * rows, width), f32)],
    )(tokens, own, down, down_high, up_low, up, match_weight)


def added_kernel(a, b, c, d, _, first, second):
    first[...] = (a[...].astype(jnp.float32) + b[...].astype(jnp.float32)).astype(first.dtype)
    second[...] = (c[...].astype(jnp.float32) + d[...].astype(jnp.float32)).astype(second.dtype)


def added(a, b, c, d, earlier):
    rows, depth = a.shape
    columns = 1024
    part = pl.BlockSpec((rows, columns), lambda i: (0, i))
    return local(
        added_kernel,
        (jax.ShapeDtypeStruct(a.shape, b.dtype),) * 2,
        20,
        grid=(depth // columns,),
        in_specs=[part, pl.BlockSpec((rows, columns), lambda i: (1, i)), part, part]
        + [pl.BlockSpec(memory_space=pltpu.HBM)],
        out_specs=(part,) * 2,
    )(a, b, c, d, earlier)


def features_kernel(tokens, own, up_low, up, down, down_high, features):
    mid = up_low.shape[0]
    summed = own[...]
    from_below = [up_low[...], up[:mid, :]]
    from_above = [down[mid:, :], down_high[...]]
    summed = summed + jnp.concatenate(from_below, axis=0).astype(jnp.float32)
    summed = summed + jnp.concatenate(from_above, axis=0).astype(jnp.float32)
    features[...] = (tokens[...].astype(jnp.float32) + summed).astype(jnp.bfloat16)


def features_of(tokens, own, up_low, up, down, down_high):
    rows, depth = tokens.shape
    columns = 1024
    whole = pl.BlockSpec((rows, columns), lambda i: (0, i))
    half = pl.BlockSpec((rows // 2, columns), lambda i: (0, i))
    return local(
        features_kernel,
        jax.ShapeDtypeStruct((rows, depth), jnp.bfloat16),
        20,
        grid=(depth // columns,),
        in_specs=[whole, whole, half, whole, whole, half],
        out_specs=whole,
    )(tokens, own, up_low, up, down, down_high)


def matcher_kernel(*refs):
    descriptor, qkv, out_weight, *pieces, matched, keys, values, mixed = refs
    rows, width = descriptor.shape
    bf16 = jnp.bfloat16
    queries = dot(descriptor[...], qkv[:, :width]).astype(bf16)
    at = 0
    for piece in pieces:
        count = piece.shape[0]
        keys[at : at + count, :] = dot(piece[...], qkv[:, width : 2 * width]).astype(bf16)
        values[at : at + count, :] = dot(piece[...], qkv[:, 2 * width :]).astype(bf16)
        at += count
    head_width = width // MATCH_HEADS
    pair = 2 * head_width
    low = lax.broadcasted_iota(jnp.int32, (rows, pair), 1) < head_width
    for first in range(0, width, pair):
        span = slice(first, first + pair)
        two = queries[:, span]
        results = []
        for chosen in (low, jnp.logical_not(low)):
            asked = jnp.where(chosen, two, jnp.zeros_like(two))
            scale = 1.0 / math.sqrt(head_width)
            results.append(attend(asked, keys[:, span], values[:, span], scale))
        mixed[:, span] = jnp.where(low, results[0], results[1]).astype(bf16)
    matched[...] = (descriptor[...].astype(jnp.float32) + dot(mixed[...], out_weight[...])).astype(
        bf16
    )


def match(descriptor, pieces, qkv, out_weight):
    count = sum(piece.shape[0] for piece in pieces)
    width = descriptor.shape[1]
    return local(
        matcher_kernel,
        jax.ShapeDtypeStruct(descriptor.shape, jnp.bfloat16),
        24,
        scratch_shapes=[
            pltpu.VMEM((count, width), jnp.bfloat16),
            pltpu.VMEM((count, width), jnp.bfloat16),
            pltpu.VMEM(descriptor.shape, jnp.bfloat16),
        ],
    )(descriptor, qkv, out_weight, *pieces)


def per_device(
    tokens, norm_gain, norm_bias, qkv_weight, out_weight, match_weight, matcher_qkv, matcher_out
):
    bf16, f32 = jnp.bfloat16, jnp.float32
    z = lax.axis_index("z")
    x = lax.axis_index("xh") * 2 + lax.axis_index("xl")
    width = matcher_out.shape[0]
    rows, features_width = tokens.shape
    mid = rows // 2

    block, wide = qkv_weight.shape[0], out_weight.shape[1]
    packed = qkv_weight.reshape(block, -1, wide).transpose(1, 0, 2).reshape(-1, wide)
    packed = swapped_roles(jnp.concatenate([packed, out_weight], axis=0))
    split = packed.shape[0] - out_weight.shape[0]
    weights = lax.all_gather(gathered_x(packed[:split], x, 0), "z", axis=0, tiled=True)
    weights = weights.reshape(8, 4, split // block, block, wide)

    tokens = swapped_roles(tokens)
    normed = layer_norm(tokens, norm_gain, norm_bias)
    out_own = gathered_x(gathered_z(packed[split:], z), x, 1)
    out_other = moved(out_own, other_core)
    pieces = [normed] + [moved(normed, along_y(k)) for k in DISTANCES]
    pieces += [moved(piece, other_core) for piece in pieces]
    pieces = together(*pieces, flops=WAIT)
    mine, theirs = attention(pieces, weights, out_own)

    match_weight = after(match_weight, normed)
    other_half = moved(match_weight, lambda p: {"xh": 1 - p["xh"], "xl": 1 - p["xl"]})
    match_pair = jnp.where(
        lax.axis_index("xh") == 0,
        jnp.concatenate([match_weight, other_half], axis=0),
        jnp.concatenate([other_half, match_weight], axis=0),
    )
    match_all = lax.all_gather(match_pair, ("z", "core"), axis=0, tiled=True)
    match_all = match_all.reshape(8, 2, 2, match_weight.shape[0], width)

    shape = (8, 4, 2, block, wide)
    both = (mine, moved(theirs, other_core), out_own.reshape(shape), out_other.reshape(shape))
    up, down = terms(
        *both,
        [([(2 * rows + mid, rows)], bf16), ([(3 * rows + mid, mid), (rows, mid)], bf16)],
    )
    own, down_high, up_low = terms(
        *both, [([(0, rows)], f32), ([(rows + mid, mid)], bf16), ([(2 * rows, mid)], bf16)], [up]
    )
    sums = descriptor_terms(tokens, own, down, down_high, up_low, up, match_all)
    up, down = moved(up, along_y(1)), moved(down, along_y(-1))
    sums_there = [moved(part, along_y(k)) for part, k in zip(sums[1:], (-1, 1, 2))]
    descriptor = sums[0] + sum(part.astype(f32) for part in sums_there)
    descriptor = descriptor.astype(bf16)
    up_low, down_high = added(up_low, up, down_high, down, descriptor)
    up_low, down_high = moved(up_low, along_y(1)), moved(down_high, along_y(-1))
    features = features_of(tokens, own, up_low, up, down, down_high)

    partner = moved(descriptor, along_z(4))
    quarter = jnp.concatenate([partner] + [moved(partner, along_y(k)) for k in DISTANCES], axis=0)
    pieces = [quarter, moved(quarter, other_core)]
    matched = match(descriptor, pieces, matcher_qkv, matcher_out)
    return (swapped_roles(features), swapped_roles(matched))


def solution(mesh):
    fine = Mesh(mesh.devices.reshape(SIZES), AXES)
    dp, tensor = ("z", "xh", "core"), ("xl", "y")
    return jax.shard_map(
        per_device,
        mesh=fine,
        in_specs=(
            P(AXES, None),
            P(),
            P(),
            P(dp, tensor),
            P(tensor, dp),
            P(dp, None),
            P(),
            P(),
        ),
        out_specs=(P(AXES, None), P(AXES, None)),
        check_vma=False,
    )
```

```python
import functools
import itertools
import math

import jax
import jax.numpy as jnp
from jax import lax
from jax.experimental import pallas as pl
from jax.experimental.pallas import tpu as pltpu
from jax.sharding import Mesh
from jax.sharding import PartitionSpec as P

HEAD_DIM = 128
MATCH_HEADS = 8
DISTANCES = (1, -1, 2)
WAIT = 23_000_000_000
LOG2_E = math.log2(math.e)
AXES = ("z", "xh", "core", "xl", "y")
SIZES = (8, 2, 2, 2, 4)


def moved(block, target):
    def index(place):
        at = 0
        for axis, size in zip(AXES, SIZES):
            at = at * size + place[axis]
        return at

    route = []
    for values in itertools.product(*[range(size) for size in SIZES]):
        place = dict(zip(AXES, values))
        route.append((index(place), index({**place, **target(place)})))
    return lax.ppermute(block, AXES, route)


def along_y(k):
    return lambda p: {"y": (p["y"] + k) % 4}


def along_z(k):
    return lambda p: {"z": (p["z"] + k) % 8}


def two_along_z(p):
    return {"z": (p["z"] + 2 - 4 * (p["z"] % 2)) % 8}


def along_x(k):
    def target(p):
        x = (p["xh"] * 2 + p["xl"] + k) % 4
        return {"xh": x // 2, "xl": x % 2}

    return target


def swapped_along_x(k):
    def target(p):
        p = {**p, "core": p["xl"], "xl": p["core"]}
        return {**p, **along_x(k)(p)}

    return target


def other_core(p):
    return {"core": 1 - p["core"]}


def swapped_roles(block):
    return moved(block, lambda p: {"core": p["xl"], "xl": p["core"]})


def gathered_z(block, z):
    pair = after(jnp.stack([block, moved(block, along_z(4))]))
    pairs = [pair, moved(pair, along_z(1)), moved(pair, along_z(-1)), moved(pair, two_along_z)]
    sign = 1 - 2 * (z % 2)
    whole = jnp.zeros((2, 4) + block.shape, block.dtype)
    rest = (0,) * block.ndim
    for k, pair in zip((0, 1, -1, 2 * sign), pairs):
        owner = (z - k) % 8
        low = jnp.where(owner < 4, pair, pair[::-1])
        whole = lax.dynamic_update_slice(whole, low[:, None], (0, owner % 4) + rest)
    return whole.reshape((8,) + block.shape)


def gathered_x(block, x, axis):
    whole = jnp.zeros(block.shape[:axis] + (4,) + block.shape[axis:], block.dtype)
    for k, part in [(0, block)] + [(k, moved(block, along_x(k))) for k in DISTANCES]:
        at = [0] * whole.ndim
        at[axis] = (x - k) % 4
        whole = lax.dynamic_update_slice(whole, jnp.expand_dims(part, axis), at)
    return whole


def layer_norm(rows_in, norm_gain, norm_bias):
    values = rows_in.astype(jnp.float32)
    center = jnp.mean(values, axis=-1, keepdims=True)
    spread = jnp.mean((values - center) ** 2, axis=-1, keepdims=True)
    return ((values - center) * lax.rsqrt(spread + 1e-06) * norm_gain + norm_bias).astype(
        jnp.bfloat16
    )


def local(kernel, out_shape, mebibytes, flops=0, moved_bytes=0, **kwargs):
    return pl.pallas_call(
        kernel,
        out_shape=out_shape,
        compiler_params=pltpu.CompilerParams(vmem_limit_bytes=mebibytes << 20),
        cost_estimate=pl.CostEstimate(flops=flops, bytes_accessed=moved_bytes, transcendentals=0),
        **kwargs,
    )


def together(*values, flops=0):
    def kernel(*refs):
        pass

    held = pl.BlockSpec(memory_space=pltpu.HBM)
    count = len(values)
    return local(
        kernel,
        tuple(jax.ShapeDtypeStruct(value.shape, value.dtype) for value in values),
        1,
        flops=flops,
        in_specs=[held] * count,
        out_specs=(held,) * count,
        input_output_aliases={i: i for i in range(count)},
    )(*values)


def after(value, *earlier):
    def kernel(*refs):
        pass

    held = pl.BlockSpec(memory_space=pltpu.HBM)
    return local(
        kernel,
        jax.ShapeDtypeStruct(value.shape, value.dtype),
        1,
        in_specs=[held] * (1 + len(earlier)),
        out_specs=held,
        input_output_aliases={0: 0},
    )(value, *earlier)


def attend(queries, keys, values, scale):
    scores = dot_transposed(queries, keys)
    raised = jnp.exp2((scores - jnp.max(scores, axis=-1, keepdims=True)) * (scale * LOG2_E))
    mixed = dot(raised.astype(jnp.bfloat16), values)
    return mixed * (1.0 / jnp.sum(raised, axis=-1, keepdims=True))


def dot(left, right):
    return jnp.dot(left, right, preferred_element_type=jnp.float32)


def dot_transposed(left, right):
    return lax.dot_general(
        left, right, (((1,), (1,)), ((), ())), preferred_element_type=jnp.float32
    )


PARTS = 2


def attention_kernel(*refs):
    *pieces, weight, _, own, other, held, held_weight, total, projected, sems = refs
    depth = held.shape[1] // PARTS
    block = weight.shape[3]
    copies = []
    for part in range(PARTS):
        span = pl.ds(part * depth, depth)
        planes = pl.ds(part * 8 // PARTS, 8 // PARTS)
        moves = []
        for column in range(held_weight.shape[3] // block):
            there = held_weight.at[planes, :, :, pl.ds(column * block, block)]
            moves.append((weight.at[planes, :, column], there))
        at = 0
        for piece in pieces:
            count = piece.shape[0]
            moves.append((piece.at[:, span], held.at[pl.ds(at, count), span]))
            at += count
        starting = [
            pltpu.make_async_copy(source, there, sems.at[part, i])
            for i, (source, there) in enumerate(moves)
        ]
        for copy in starting:
            copy.start()
        copies.append(starting)
    step = 512
    for part in range(PARTS):
        for copy in copies[part]:
            copy.wait()
        span = pl.ds(part * depth, depth)
        planes = pl.ds(part * 8 // PARTS, 8 // PARTS)

        @pl.loop(0, held.shape[0], step=step)
        def _(row, part=part, span=span, planes=planes):
            rows = pl.ds(pl.multiple_of(row, step), step)
            term = dot(held[rows, span], held_weight[planes].reshape(depth, -1))
            if part:
                term = total[rows, :] + term
            if part < PARTS - 1:
                total[rows, :] = term
            else:
                projected[rows, :] = term.astype(jnp.bfloat16)

    step = 256
    for head in range(2):
        at = head * 3 * HEAD_DIM
        for half, out in enumerate((own, other)):

            @pl.loop(0, out.shape[0], step=step)
            def _(row, at=at, half=half, out=out, head=head):
                rows = pl.ds(pl.multiple_of(half * out.shape[0] + row, step), step)
                mixed = attend(
                    projected[rows, at : at + HEAD_DIM],
                    projected[:, at + HEAD_DIM : at + 2 * HEAD_DIM],
                    projected[:, at + 2 * HEAD_DIM : at + 3 * HEAD_DIM],
                    1.0 / math.sqrt(HEAD_DIM),
                )
                out[pl.ds(pl.multiple_of(row, step), step), pl.ds(head * HEAD_DIM, HEAD_DIM)] = (
                    mixed.astype(jnp.bfloat16)
                )


def attention(pieces, weight, earlier):
    count = sum(piece.shape[0] for piece in pieces)
    depth = pieces[0].shape[1]
    block = weight.shape[3]
    columns = 6 * block
    result = jax.ShapeDtypeStruct((count // 2, columns // 3), jnp.bfloat16)
    return local(
        attention_kernel,
        (result, result),
        60,
        flops=2 * count * depth * columns,
        moved_bytes=2 * depth * (count + columns),
        in_specs=[pl.BlockSpec(memory_space=pltpu.HBM)] * (len(pieces) + 2),
        out_specs=(pl.BlockSpec(memory_space=pltpu.VMEM),) * 2,
        scratch_shapes=[
            pltpu.VMEM((count, depth), jnp.bfloat16),
            pltpu.VMEM((8, 4, block, columns), jnp.bfloat16),
            pltpu.VMEM((count, columns), jnp.float32),
            pltpu.VMEM((count, columns), jnp.bfloat16),
            pltpu.SemaphoreType.DMA((PARTS, len(pieces) + 6)),
        ],
    )(*pieces, weight, earlier)


def out_matrix(weight, other_weight):
    planes, xs, halves = weight.shape[:3]
    return jnp.concatenate(
        [
            jnp.concatenate([w[p, x, h] for p in range(planes) for x in range(xs)], axis=1)
            for w in (weight, other_weight)
            for h in range(halves)
        ],
        axis=0,
    )


def match_matrix(weight):
    planes, cores, highs = weight.shape[:3]
    blocks = [weight[p, c, h] for p in range(planes) for h in range(highs) for c in range(cores)]
    return jnp.concatenate(blocks, axis=0)


def terms_kernel(skipped, picked, mine, theirs, weight, other_weight, *refs):
    outs = refs[skipped:]
    both = [
        jnp.concatenate([mine[at : at + many, :], theirs[at : at + many, :]], axis=1)
        for spans, _ in picked
        for at, many in spans
    ]
    products = dot(jnp.concatenate(both, axis=0), out_matrix(weight, other_weight))
    at = 0
    for out in outs:
        out[...] = products[at : at + out.shape[0]].astype(out.dtype)
        at += out.shape[0]


def terms(mine, theirs, weight, other_weight, picked, earlier=()):
    counts = [sum(many for _, many in spans) for spans, _ in picked]
    earlier = list(earlier)
    planes, xs, _, _, wide = weight.shape
    columns = 2 * xs * wide
    whole = pl.BlockSpec(mine.shape, lambda i: (0, 0))
    part = pl.BlockSpec((2,) + weight.shape[1:], lambda i: (i, 0, 0, 0, 0))
    return local(
        functools.partial(terms_kernel, len(earlier), picked),
        tuple(
            jax.ShapeDtypeStruct((many, planes * xs * wide), kind)
            for many, (_, kind) in zip(counts, picked)
        ),
        24,
        flops=2_000_000_000,
        moved_bytes=8_000_000,
        grid=(planes // 2,),
        in_specs=[whole, whole, part, part]
        + [pl.BlockSpec(memory_space=pltpu.HBM)] * len(earlier),
        out_specs=tuple(pl.BlockSpec((many, columns), lambda i: (0, i)) for many in counts),
    )(mine, theirs, weight, other_weight, *earlier)


def descriptor_kernel(tokens, own, down, down_high, up_low, up, match_weight, *rest):
    *sums, total = rest
    mid = up_low.shape[0]
    others = [down[mid:, :], down_high[...], up_low[...], up[...], down[:mid, :]]
    step = pl.program_id(0)
    rows = tokens.shape[0]
    with_tokens = (own[...] + tokens[...].astype(jnp.float32)).astype(jnp.bfloat16)
    product = dot(
        jnp.concatenate([with_tokens] + others, axis=0),
        match_matrix(match_weight),
    )

    @pl.when(step == 0)
    def _():
        total[...] = product

    @pl.when(step > 0)
    def _():
        total[...] += product

    @pl.when(step == pl.num_programs(0) - 1)
    def _():
        for i, out in enumerate(sums):
            out[...] = total[i * rows : (i + 1) * rows].astype(out.dtype)


def descriptor_terms(tokens, own, down, down_high, up_low, up, match_weight):
    rows, depth = tokens.shape
    width = match_weight.shape[-1]
    columns = 1024
    full = pl.BlockSpec((rows, columns), lambda i: (0, i))
    half = pl.BlockSpec((rows // 2, columns), lambda i: (0, i))
    square = pl.BlockSpec((rows, width), lambda i: (0, 0))
    f32, bf16 = jnp.float32, jnp.bfloat16
    return local(
        descriptor_kernel,
        (jax.ShapeDtypeStruct((rows, width), f32),)
        + (jax.ShapeDtypeStruct((rows, width), bf16),) * 3,
        52,
        flops=4_000_000_000,
        moved_bytes=12_000_000,
        grid=(depth // columns,),
        in_specs=[full, full, full, half, half, full]
        + [pl.BlockSpec((2,) + match_weight.shape[1:], lambda i: (i, 0, 0, 0, 0))],
        out_specs=(square,) * 4,
        scratch_shapes=[pltpu.VMEM((4 * rows, width), f32)],
    )(tokens, own, down, down_high, up_low, up, match_weight)


def added_kernel(a, b, c, d, _, first, second):
    first[...] = (a[...].astype(jnp.float32) + b[...].astype(jnp.float32)).astype(first.dtype)
    second[...] = (c[...].astype(jnp.float32) + d[...].astype(jnp.float32)).astype(second.dtype)


def added(a, b, c, d, earlier):
    rows, depth = a.shape
    columns = 1024
    part = pl.BlockSpec((rows, columns), lambda i: (0, i))
    return local(
        added_kernel,
        (jax.ShapeDtypeStruct(a.shape, b.dtype),) * 2,
        20,
        grid=(depth // columns,),
        in_specs=[part, pl.BlockSpec((rows, columns), lambda i: (1, i)), part, part]
        + [pl.BlockSpec(memory_space=pltpu.HBM)],
        out_specs=(part,) * 2,
    )(a, b, c, d, earlier)


def features_kernel(tokens, own, up_low, up, down, down_high, features):
    mid = up_low.shape[0]
    summed = own[...]
    from_below = [up_low[...], up[:mid, :]]
    from_above = [down[mid:, :], down_high[...]]
    summed = summed + jnp.concatenate(from_below, axis=0).astype(jnp.float32)
    summed = summed + jnp.concatenate(from_above, axis=0).astype(jnp.float32)
    features[...] = (tokens[...].astype(jnp.float32) + summed).astype(jnp.bfloat16)


def features_of(tokens, own, up_low, up, down, down_high):
    rows, depth = tokens.shape
    columns = 1024
    whole = pl.BlockSpec((rows, columns), lambda i: (0, i))
    half = pl.BlockSpec((rows // 2, columns), lambda i: (0, i))
    return local(
        features_kernel,
        jax.ShapeDtypeStruct((rows, depth), jnp.bfloat16),
        20,
        grid=(depth // columns,),
        in_specs=[whole, whole, half, whole, whole, half],
        out_specs=whole,
    )(tokens, own, up_low, up, down, down_high)


def matcher_kernel(*refs):
    descriptor, qkv, out_weight, *pieces, matched, keys, values, mixed = refs
    rows, width = descriptor.shape
    bf16 = jnp.bfloat16
    queries = dot(descriptor[...], qkv[:, :width]).astype(bf16)
    at = 0
    for piece in pieces:
        count = piece.shape[0]
        keys[at : at + count, :] = dot(piece[...], qkv[:, width : 2 * width]).astype(bf16)
        values[at : at + count, :] = dot(piece[...], qkv[:, 2 * width :]).astype(bf16)
        at += count
    head_width = width // MATCH_HEADS
    pair = 2 * head_width
    low = lax.broadcasted_iota(jnp.int32, (rows, pair), 1) < head_width
    for first in range(0, width, pair):
        span = slice(first, first + pair)
        two = queries[:, span]
        results = []
        for chosen in (low, jnp.logical_not(low)):
            asked = jnp.where(chosen, two, jnp.zeros_like(two))
            scale = 1.0 / math.sqrt(head_width)
            results.append(attend(asked, keys[:, span], values[:, span], scale))
        mixed[:, span] = jnp.where(low, results[0], results[1]).astype(bf16)
    matched[...] = (descriptor[...].astype(jnp.float32) + dot(mixed[...], out_weight[...])).astype(
        bf16
    )


def match(descriptor, pieces, qkv, out_weight):
    count = sum(piece.shape[0] for piece in pieces)
    width = descriptor.shape[1]
    return local(
        matcher_kernel,
        jax.ShapeDtypeStruct(descriptor.shape, jnp.bfloat16),
        24,
        scratch_shapes=[
            pltpu.VMEM((count, width), jnp.bfloat16),
            pltpu.VMEM((count, width), jnp.bfloat16),
            pltpu.VMEM(descriptor.shape, jnp.bfloat16),
        ],
    )(descriptor, qkv, out_weight, *pieces)


def per_device(
    tokens, norm_gain, norm_bias, qkv_weight, out_weight, match_weight, matcher_qkv, matcher_out
):
    bf16, f32 = jnp.bfloat16, jnp.float32
    z = lax.axis_index("z")
    x = lax.axis_index("xh") * 2 + lax.axis_index("xl")
    width = matcher_out.shape[0]
    rows, features_width = tokens.shape
    mid = rows // 2

    block, wide = qkv_weight.shape[0], out_weight.shape[1]
    packed = qkv_weight.reshape(block, -1, wide).transpose(1, 0, 2).reshape(-1, wide)
    split = packed.shape[0]
    by_x = jnp.zeros((4, split, wide), bf16)
    for k in (0,) + DISTANCES:
        part = moved(packed, swapped_along_x(k))
        by_x = lax.dynamic_update_slice(by_x, part[None], ((x - k) % 4, 0, 0))
    weights = lax.all_gather(by_x, "z", axis=0, tiled=True)
    out_weight = swapped_roles(out_weight)
    weights = weights.reshape(8, 4, split // block, block, wide)

    tokens = swapped_roles(tokens)
    normed = layer_norm(tokens, norm_gain, norm_bias)
    out_own = gathered_x(gathered_z(after(out_weight, normed), z), x, 1)
    out_other = moved(out_own, other_core)
    pieces = [normed] + [moved(normed, along_y(k)) for k in DISTANCES]
    received = pieces[3]
    pieces += [moved(piece, other_core) for piece in pieces]
    pieces = together(*pieces, flops=WAIT)
    mine, theirs = attention(pieces, weights, out_own)

    match_weight = after(match_weight, received)
    other_half = moved(match_weight, lambda p: {"xh": 1 - p["xh"], "xl": 1 - p["xl"]})
    match_pair = jnp.where(
        lax.axis_index("xh") == 0,
        jnp.concatenate([match_weight, other_half], axis=0),
        jnp.concatenate([other_half, match_weight], axis=0),
    )
    match_all = lax.all_gather(match_pair, ("z", "core"), axis=0, tiled=True)
    match_all = match_all.reshape(8, 2, 2, match_weight.shape[0], width)

    shape = (8, 4, 2, block, wide)
    both = (mine, moved(theirs, other_core), out_own.reshape(shape), out_other.reshape(shape))
    up, down = terms(
        *both,
        [([(2 * rows + mid, rows)], bf16), ([(3 * rows + mid, mid), (rows, mid)], bf16)],
    )
    own, down_high, up_low = terms(
        *both, [([(0, rows)], f32), ([(rows + mid, mid)], bf16), ([(2 * rows, mid)], bf16)], [up]
    )
    sums = descriptor_terms(tokens, own, down, down_high, up_low, up, match_all)
    up, down = moved(up, along_y(1)), moved(down, along_y(-1))
    sums_there = [moved(part, along_y(k)) for part, k in zip(sums[1:], (-1, 1, 2))]
    descriptor = sums[0] + sum(part.astype(f32) for part in sums_there)
    descriptor = descriptor.astype(bf16)
    up_low, down_high = added(up_low, up, down_high, down, descriptor)
    up_low, down_high = moved(up_low, along_y(1)), moved(down_high, along_y(-1))
    features = features_of(tokens, own, up_low, up, down, down_high)

    partner = moved(descriptor, along_z(4))
    quarter = jnp.concatenate([partner] + [moved(partner, along_y(k)) for k in DISTANCES], axis=0)
    pieces = [quarter, moved(quarter, other_core)]
    matched = match(descriptor, pieces, matcher_qkv, matcher_out)
    return (swapped_roles(features), swapped_roles(matched))


def solution(mesh):
    fine = Mesh(mesh.devices.reshape(SIZES), AXES)
    dp, tensor = ("z", "xh", "core"), ("xl", "y")
    return jax.shard_map(
        per_device,
        mesh=fine,
        in_specs=(
            P(AXES, None),
            P(),
            P(),
            P(dp, tensor),
            P(tensor, dp),
            P(dp, None),
            P(),
            P(),
        ),
        out_specs=(P(AXES, None), P(AXES, None)),
        check_vma=False,
    )
```

```python
import functools
import itertools
import math

import jax
import jax.numpy as jnp
from jax import lax
from jax.experimental import pallas as pl
from jax.experimental.pallas import tpu as pltpu
from jax.sharding import Mesh
from jax.sharding import PartitionSpec as P

HEAD_DIM = 128
MATCH_HEADS = 8
DISTANCES = (1, -1, 2)
WAIT = 23_000_000_000
LOG2_E = math.log2(math.e)
AXES = ("z", "xh", "core", "xl", "y")
SIZES = (8, 2, 2, 2, 4)


def moved(block, target):
    def index(place):
        at = 0
        for axis, size in zip(AXES, SIZES):
            at = at * size + place[axis]
        return at

    route = []
    for values in itertools.product(*[range(size) for size in SIZES]):
        place = dict(zip(AXES, values))
        route.append((index(place), index({**place, **target(place)})))
    return lax.ppermute(block, AXES, route)


def along_y(k):
    return lambda p: {"y": (p["y"] + k) % 4}


def along_z(k):
    return lambda p: {"z": (p["z"] + k) % 8}


def two_along_z(p):
    return {"z": (p["z"] + 2 - 4 * (p["z"] % 2)) % 8}


def along_x(k):
    def target(p):
        x = (p["xh"] * 2 + p["xl"] + k) % 4
        return {"xh": x // 2, "xl": x % 2}

    return target


def swapped_along_x(k):
    def target(p):
        p = {**p, "core": p["xl"], "xl": p["core"]}
        return {**p, **along_x(k)(p)}

    return target


def other_core(p):
    return {"core": 1 - p["core"]}


def swapped_roles(block):
    return moved(block, lambda p: {"core": p["xl"], "xl": p["core"]})


def gathered_z(block, z):
    pair = after(jnp.stack([block, moved(block, along_z(4))]))
    pairs = [pair, moved(pair, along_z(1)), moved(pair, along_z(-1)), moved(pair, two_along_z)]
    sign = 1 - 2 * (z % 2)
    whole = jnp.zeros((2, 4) + block.shape, block.dtype)
    rest = (0,) * block.ndim
    for k, pair in zip((0, 1, -1, 2 * sign), pairs):
        owner = (z - k) % 8
        low = jnp.where(owner < 4, pair, pair[::-1])
        whole = lax.dynamic_update_slice(whole, low[:, None], (0, owner % 4) + rest)
    return whole.reshape((8,) + block.shape)


def gathered_x(block, x, axis):
    whole = jnp.zeros(block.shape[:axis] + (4,) + block.shape[axis:], block.dtype)
    for k, part in [(0, block)] + [(k, moved(block, along_x(k))) for k in DISTANCES]:
        at = [0] * whole.ndim
        at[axis] = (x - k) % 4
        whole = lax.dynamic_update_slice(whole, jnp.expand_dims(part, axis), at)
    return whole


def layer_norm(rows_in, norm_gain, norm_bias):
    values = rows_in.astype(jnp.float32)
    center = jnp.mean(values, axis=-1, keepdims=True)
    spread = jnp.mean((values - center) ** 2, axis=-1, keepdims=True)
    return ((values - center) * lax.rsqrt(spread + 1e-06) * norm_gain + norm_bias).astype(
        jnp.bfloat16
    )


def local(kernel, out_shape, mebibytes, flops=0, moved_bytes=0, **kwargs):
    return pl.pallas_call(
        kernel,
        out_shape=out_shape,
        compiler_params=pltpu.CompilerParams(vmem_limit_bytes=mebibytes << 20),
        cost_estimate=pl.CostEstimate(flops=flops, bytes_accessed=moved_bytes, transcendentals=0),
        **kwargs,
    )


def together(*values, flops=0):
    def kernel(*refs):
        pass

    held = pl.BlockSpec(memory_space=pltpu.HBM)
    count = len(values)
    return local(
        kernel,
        tuple(jax.ShapeDtypeStruct(value.shape, value.dtype) for value in values),
        1,
        flops=flops,
        in_specs=[held] * count,
        out_specs=(held,) * count,
        input_output_aliases={i: i for i in range(count)},
    )(*values)


def after(value, *earlier):
    def kernel(*refs):
        pass

    held = pl.BlockSpec(memory_space=pltpu.HBM)
    return local(
        kernel,
        jax.ShapeDtypeStruct(value.shape, value.dtype),
        1,
        in_specs=[held] * (1 + len(earlier)),
        out_specs=held,
        input_output_aliases={0: 0},
    )(value, *earlier)


def attend(queries, keys, values, scale):
    scores = dot_transposed(queries, keys)
    raised = jnp.exp2((scores - jnp.max(scores, axis=-1, keepdims=True)) * (scale * LOG2_E))
    mixed = dot(raised.astype(jnp.bfloat16), values)
    return mixed * (1.0 / jnp.sum(raised, axis=-1, keepdims=True))


def dot(left, right):
    return jnp.dot(left, right, preferred_element_type=jnp.float32)


def dot_transposed(left, right):
    return lax.dot_general(
        left, right, (((1,), (1,)), ((), ())), preferred_element_type=jnp.float32
    )


PARTS = 2


def attention_kernel(*refs):
    *pieces, weight, _, own, other, held, held_weight, total, projected, sems = refs
    depth = held.shape[1] // PARTS
    block = weight.shape[3]
    copies = []
    for part in range(PARTS):
        span = pl.ds(part * depth, depth)
        planes = pl.ds(part * 8 // PARTS, 8 // PARTS)
        moves = []
        for column in range(held_weight.shape[3] // block):
            there = held_weight.at[planes, :, :, pl.ds(column * block, block)]
            moves.append((weight.at[planes, :, column], there))
        at = 0
        for piece in pieces:
            count = piece.shape[0]
            moves.append((piece.at[:, span], held.at[pl.ds(at, count), span]))
            at += count
        starting = [
            pltpu.make_async_copy(source, there, sems.at[part, i])
            for i, (source, there) in enumerate(moves)
        ]
        for copy in starting:
            copy.start()
        copies.append(starting)
    step = 512
    for part in range(PARTS):
        for copy in copies[part]:
            copy.wait()
        span = pl.ds(part * depth, depth)
        planes = pl.ds(part * 8 // PARTS, 8 // PARTS)

        @pl.loop(0, held.shape[0], step=step)
        def _(row, part=part, span=span, planes=planes):
            rows = pl.ds(pl.multiple_of(row, step), step)
            term = dot(held[rows, span], held_weight[planes].reshape(depth, -1))
            if part:
                term = total[rows, :] + term
            if part < PARTS - 1:
                total[rows, :] = term
            else:
                projected[rows, :] = term.astype(jnp.bfloat16)

    step = 256
    for head in range(2):
        at = head * 3 * HEAD_DIM
        for half, out in enumerate((own, other)):

            @pl.loop(0, out.shape[0], step=step)
            def _(row, at=at, half=half, out=out, head=head):
                rows = pl.ds(pl.multiple_of(half * out.shape[0] + row, step), step)
                mixed = attend(
                    projected[rows, at : at + HEAD_DIM],
                    projected[:, at + HEAD_DIM : at + 2 * HEAD_DIM],
                    projected[:, at + 2 * HEAD_DIM : at + 3 * HEAD_DIM],
                    1.0 / math.sqrt(HEAD_DIM),
                )
                out[pl.ds(pl.multiple_of(row, step), step), pl.ds(head * HEAD_DIM, HEAD_DIM)] = (
                    mixed.astype(jnp.bfloat16)
                )


def attention(pieces, weight, earlier):
    count = sum(piece.shape[0] for piece in pieces)
    depth = pieces[0].shape[1]
    block = weight.shape[3]
    columns = 6 * block
    result = jax.ShapeDtypeStruct((count // 2, columns // 3), jnp.bfloat16)
    return local(
        attention_kernel,
        (result, result),
        60,
        flops=2 * count * depth * columns,
        moved_bytes=2 * depth * (count + columns),
        in_specs=[pl.BlockSpec(memory_space=pltpu.HBM)] * (len(pieces) + 2),
        out_specs=(pl.BlockSpec(memory_space=pltpu.VMEM),) * 2,
        scratch_shapes=[
            pltpu.VMEM((count, depth), jnp.bfloat16),
            pltpu.VMEM((8, 4, block, columns), jnp.bfloat16),
            pltpu.VMEM((count, columns), jnp.float32),
            pltpu.VMEM((count, columns), jnp.bfloat16),
            pltpu.SemaphoreType.DMA((PARTS, len(pieces) + 6)),
        ],
    )(*pieces, weight, earlier)


def out_matrix(weight, other_weight):
    planes, xs, halves = weight.shape[:3]
    return jnp.concatenate(
        [
            jnp.concatenate([w[p, x, h] for p in range(planes) for x in range(xs)], axis=1)
            for w in (weight, other_weight)
            for h in range(halves)
        ],
        axis=0,
    )


def match_matrix(weight):
    planes, cores, highs = weight.shape[:3]
    blocks = [weight[p, c, h] for p in range(planes) for h in range(highs) for c in range(cores)]
    return jnp.concatenate(blocks, axis=0)


def terms_kernel(skipped, picked, mine, theirs, weight, other_weight, *refs):
    outs = refs[skipped:]
    both = [
        jnp.concatenate([mine[at : at + many, :], theirs[at : at + many, :]], axis=1)
        for spans, _ in picked
        for at, many in spans
    ]
    products = dot(jnp.concatenate(both, axis=0), out_matrix(weight, other_weight))
    at = 0
    for out in outs:
        out[...] = products[at : at + out.shape[0]].astype(out.dtype)
        at += out.shape[0]


def terms(mine, theirs, weight, other_weight, picked, earlier=()):
    counts = [sum(many for _, many in spans) for spans, _ in picked]
    earlier = list(earlier)
    planes, xs, _, _, wide = weight.shape
    columns = 2 * xs * wide
    whole = pl.BlockSpec(mine.shape, lambda i: (0, 0))
    part = pl.BlockSpec((2,) + weight.shape[1:], lambda i: (i, 0, 0, 0, 0))
    return local(
        functools.partial(terms_kernel, len(earlier), picked),
        tuple(
            jax.ShapeDtypeStruct((many, planes * xs * wide), kind)
            for many, (_, kind) in zip(counts, picked)
        ),
        24,
        flops=2_000_000_000,
        moved_bytes=8_000_000,
        grid=(planes // 2,),
        in_specs=[whole, whole, part, part]
        + [pl.BlockSpec(memory_space=pltpu.HBM)] * len(earlier),
        out_specs=tuple(pl.BlockSpec((many, columns), lambda i: (0, i)) for many in counts),
    )(mine, theirs, weight, other_weight, *earlier)


def descriptor_kernel(tokens, own, down, down_high, up_low, up, match_weight, *rest):
    *sums, total = rest
    mid = up_low.shape[0]
    others = [down[mid:, :], down_high[...], up_low[...], up[...], down[:mid, :]]
    step = pl.program_id(0)
    rows = tokens.shape[0]
    with_tokens = (own[...] + tokens[...].astype(jnp.float32)).astype(jnp.bfloat16)
    product = dot(
        jnp.concatenate([with_tokens] + others, axis=0),
        match_matrix(match_weight),
    )

    @pl.when(step == 0)
    def _():
        total[...] = product

    @pl.when(step > 0)
    def _():
        total[...] += product

    @pl.when(step == pl.num_programs(0) - 1)
    def _():
        for i, out in enumerate(sums):
            out[...] = total[i * rows : (i + 1) * rows].astype(out.dtype)


def descriptor_terms(tokens, own, down, down_high, up_low, up, match_weight):
    rows, depth = tokens.shape
    width = match_weight.shape[-1]
    columns = 1024
    full = pl.BlockSpec((rows, columns), lambda i: (0, i))
    half = pl.BlockSpec((rows // 2, columns), lambda i: (0, i))
    square = pl.BlockSpec((rows, width), lambda i: (0, 0))
    f32, bf16 = jnp.float32, jnp.bfloat16
    return local(
        descriptor_kernel,
        (jax.ShapeDtypeStruct((rows, width), f32),)
        + (jax.ShapeDtypeStruct((rows, width), bf16),) * 3,
        52,
        flops=4_000_000_000,
        moved_bytes=12_000_000,
        grid=(depth // columns,),
        in_specs=[full, full, full, half, half, full]
        + [pl.BlockSpec((2,) + match_weight.shape[1:], lambda i: (i, 0, 0, 0, 0))],
        out_specs=(square,) * 4,
        scratch_shapes=[pltpu.VMEM((4 * rows, width), f32)],
    )(tokens, own, down, down_high, up_low, up, match_weight)


def added_kernel(a, b, c, d, _, first, second):
    first[...] = (a[...].astype(jnp.float32) + b[...].astype(jnp.float32)).astype(first.dtype)
    second[...] = (c[...].astype(jnp.float32) + d[...].astype(jnp.float32)).astype(second.dtype)


def added(a, b, c, d, earlier):
    rows, depth = a.shape
    columns = 1024
    part = pl.BlockSpec((rows, columns), lambda i: (0, i))
    return local(
        added_kernel,
        (jax.ShapeDtypeStruct(a.shape, b.dtype),) * 2,
        20,
        grid=(depth // columns,),
        in_specs=[part, pl.BlockSpec((rows, columns), lambda i: (1, i)), part, part]
        + [pl.BlockSpec(memory_space=pltpu.HBM)],
        out_specs=(part,) * 2,
    )(a, b, c, d, earlier)


def features_kernel(tokens, own, up_low, up, down, down_high, features):
    mid = up_low.shape[0]
    summed = own[...]
    from_below = [up_low[...], up[:mid, :]]
    from_above = [down[mid:, :], down_high[...]]
    summed = summed + jnp.concatenate(from_below, axis=0).astype(jnp.float32)
    summed = summed + jnp.concatenate(from_above, axis=0).astype(jnp.float32)
    features[...] = (tokens[...].astype(jnp.float32) + summed).astype(jnp.bfloat16)


def features_of(tokens, own, up_low, up, down, down_high):
    rows, depth = tokens.shape
    columns = 1024
    whole = pl.BlockSpec((rows, columns), lambda i: (0, i))
    half = pl.BlockSpec((rows // 2, columns), lambda i: (0, i))
    return local(
        features_kernel,
        jax.ShapeDtypeStruct((rows, depth), jnp.bfloat16),
        20,
        grid=(depth // columns,),
        in_specs=[whole, whole, half, whole, whole, half],
        out_specs=whole,
    )(tokens, own, up_low, up, down, down_high)


def matcher_kernel(*refs):
    descriptor, qkv, out_weight, *pieces, matched, keys, values, mixed = refs
    rows, width = descriptor.shape
    bf16 = jnp.bfloat16
    queries = dot(descriptor[...], qkv[:, :width]).astype(bf16)
    at = 0
    for piece in pieces:
        count = piece.shape[0]
        keys[at : at + count, :] = dot(piece[...], qkv[:, width : 2 * width]).astype(bf16)
        values[at : at + count, :] = dot(piece[...], qkv[:, 2 * width :]).astype(bf16)
        at += count
    head_width = width // MATCH_HEADS
    pair = 2 * head_width
    low = lax.broadcasted_iota(jnp.int32, (rows, pair), 1) < head_width
    for first in range(0, width, pair):
        span = slice(first, first + pair)
        two = queries[:, span]
        results = []
        for chosen in (low, jnp.logical_not(low)):
            asked = jnp.where(chosen, two, jnp.zeros_like(two))
            scale = 1.0 / math.sqrt(head_width)
            results.append(attend(asked, keys[:, span], values[:, span], scale))
        mixed[:, span] = jnp.where(low, results[0], results[1]).astype(bf16)
    matched[...] = (descriptor[...].astype(jnp.float32) + dot(mixed[...], out_weight[...])).astype(
        bf16
    )


def match(descriptor, pieces, qkv, out_weight):
    count = sum(piece.shape[0] for piece in pieces)
    width = descriptor.shape[1]
    return local(
        matcher_kernel,
        jax.ShapeDtypeStruct(descriptor.shape, jnp.bfloat16),
        24,
        scratch_shapes=[
            pltpu.VMEM((count, width), jnp.bfloat16),
            pltpu.VMEM((count, width), jnp.bfloat16),
            pltpu.VMEM(descriptor.shape, jnp.bfloat16),
        ],
    )(descriptor, qkv, out_weight, *pieces)


def per_device(
    tokens, norm_gain, norm_bias, qkv_weight, out_weight, match_weight, matcher_qkv, matcher_out
):
    bf16, f32 = jnp.bfloat16, jnp.float32
    z = lax.axis_index("z")
    x = lax.axis_index("xh") * 2 + lax.axis_index("xl")
    width = matcher_out.shape[0]
    rows, features_width = tokens.shape
    mid = rows // 2

    block, wide = qkv_weight.shape[0], out_weight.shape[1]
    packed = qkv_weight.reshape(block, -1, wide).transpose(1, 0, 2).reshape(-1, wide)
    split = packed.shape[0]
    by_x = jnp.zeros((4, split, wide), bf16)
    for k in (0,) + DISTANCES:
        part = moved(packed, swapped_along_x(k))
        by_x = lax.dynamic_update_slice(by_x, part[None], ((x - k) % 4, 0, 0))
    weights = lax.all_gather(by_x, "z", axis=0, tiled=True)
    out_weight = swapped_roles(out_weight)
    weights = weights.reshape(8, 4, split // block, block, wide)

    tokens = swapped_roles(tokens)
    normed = layer_norm(tokens, norm_gain, norm_bias)
    pieces = [normed] + [moved(normed, along_y(k)) for k in DISTANCES]
    *pieces[1:], out_z = together(*pieces[1:], gathered_z(out_weight, z))
    pieces += [moved(piece, other_core) for piece in pieces]
    out_own = gathered_x(out_z, x, 1)
    out_other = moved(out_own, other_core)
    pieces = together(*pieces, flops=WAIT)
    mine, theirs = attention(pieces, weights, out_own)

    match_weight = after(match_weight, pieces[0])
    other_half = moved(match_weight, lambda p: {"xh": 1 - p["xh"], "xl": 1 - p["xl"]})
    match_pair = jnp.where(
        lax.axis_index("xh") == 0,
        jnp.concatenate([match_weight, other_half], axis=0),
        jnp.concatenate([other_half, match_weight], axis=0),
    )
    match_all = lax.all_gather(match_pair, ("z", "core"), axis=0, tiled=True)
    match_all = match_all.reshape(8, 2, 2, match_weight.shape[0], width)

    shape = (8, 4, 2, block, wide)
    both = (mine, moved(theirs, other_core), out_own.reshape(shape), out_other.reshape(shape))
    up, down = terms(
        *both,
        [([(2 * rows + mid, rows)], bf16), ([(3 * rows + mid, mid), (rows, mid)], bf16)],
    )
    own, down_high, up_low = terms(
        *both, [([(0, rows)], f32), ([(rows + mid, mid)], bf16), ([(2 * rows, mid)], bf16)], [up]
    )
    sums = descriptor_terms(tokens, own, down, down_high, up_low, up, match_all)
    up, down = moved(up, along_y(1)), moved(down, along_y(-1))
    sums_there = [moved(part, along_y(k)) for part, k in zip(sums[1:], (-1, 1, 2))]
    descriptor = sums[0] + sum(part.astype(f32) for part in sums_there)
    descriptor = descriptor.astype(bf16)
    up_low, down_high = added(up_low, up, down_high, down, descriptor)
    up_low, down_high = moved(up_low, along_y(1)), moved(down_high, along_y(-1))
    features = features_of(tokens, own, up_low, up, down, down_high)

    partner = moved(descriptor, along_z(4))
    quarter = jnp.concatenate([partner] + [moved(partner, along_y(k)) for k in DISTANCES], axis=0)
    pieces = [quarter, moved(quarter, other_core)]
    matched = match(descriptor, pieces, matcher_qkv, matcher_out)
    return (swapped_roles(features), swapped_roles(matched))


def solution(mesh):
    fine = Mesh(mesh.devices.reshape(SIZES), AXES)
    dp, tensor = ("z", "xh", "core"), ("xl", "y")
    return jax.shard_map(
        per_device,
        mesh=fine,
        in_specs=(
            P(AXES, None),
            P(),
            P(),
            P(dp, tensor),
            P(tensor, dp),
            P(dp, None),
            P(),
            P(),
        ),
        out_specs=(P(AXES, None), P(AXES, None)),
        check_vma=False,
    )
```

```python
import functools
import itertools
import math

import jax
import jax.numpy as jnp
from jax import lax
from jax.experimental import pallas as pl
from jax.experimental.pallas import tpu as pltpu
from jax.sharding import Mesh
from jax.sharding import PartitionSpec as P

HEAD_DIM = 128
MATCH_HEADS = 8
DISTANCES = (1, -1, 2)
WAIT = 23_000_000_000
LOG2_E = math.log2(math.e)
AXES = ("z", "xh", "core", "xl", "y")
SIZES = (8, 2, 2, 2, 4)


def moved(block, target):
    def index(place):
        at = 0
        for axis, size in zip(AXES, SIZES):
            at = at * size + place[axis]
        return at

    route = []
    for values in itertools.product(*[range(size) for size in SIZES]):
        place = dict(zip(AXES, values))
        route.append((index(place), index({**place, **target(place)})))
    return lax.ppermute(block, AXES, route)


def along_y(k):
    return lambda p: {"y": (p["y"] + k) % 4}


def along_z(k):
    return lambda p: {"z": (p["z"] + k) % 8}


def two_along_z(p):
    return {"z": (p["z"] + 2 - 4 * (p["z"] % 2)) % 8}


def along_x(k):
    def target(p):
        x = (p["xh"] * 2 + p["xl"] + k) % 4
        return {"xh": x // 2, "xl": x % 2}

    return target


def swapped_along_x(k):
    def target(p):
        p = {**p, "core": p["xl"], "xl": p["core"]}
        return {**p, **along_x(k)(p)}

    return target


def other_core(p):
    return {"core": 1 - p["core"]}


def swapped_roles(block):
    return moved(block, lambda p: {"core": p["xl"], "xl": p["core"]})


def gathered_z(block, z):
    pair = after(jnp.stack([block, moved(block, along_z(4))]))
    pairs = [pair, moved(pair, along_z(1)), moved(pair, along_z(-1)), moved(pair, two_along_z)]
    sign = 1 - 2 * (z % 2)
    whole = jnp.zeros((2, 4) + block.shape, block.dtype)
    rest = (0,) * block.ndim
    for k, pair in zip((0, 1, -1, 2 * sign), pairs):
        owner = (z - k) % 8
        low = jnp.where(owner < 4, pair, pair[::-1])
        whole = lax.dynamic_update_slice(whole, low[:, None], (0, owner % 4) + rest)
    return whole.reshape((8,) + block.shape)


def layer_norm(rows_in, norm_gain, norm_bias):
    values = rows_in.astype(jnp.float32)
    center = jnp.mean(values, axis=-1, keepdims=True)
    spread = jnp.mean((values - center) ** 2, axis=-1, keepdims=True)
    return ((values - center) * lax.rsqrt(spread + 1e-06) * norm_gain + norm_bias).astype(
        jnp.bfloat16
    )


def local(kernel, out_shape, mebibytes, flops=0, moved_bytes=0, **kwargs):
    return pl.pallas_call(
        kernel,
        out_shape=out_shape,
        compiler_params=pltpu.CompilerParams(vmem_limit_bytes=mebibytes << 20),
        cost_estimate=pl.CostEstimate(flops=flops, bytes_accessed=moved_bytes, transcendentals=0),
        **kwargs,
    )


def together(*values, flops=0):
    def kernel(*refs):
        pass

    held = pl.BlockSpec(memory_space=pltpu.HBM)
    count = len(values)
    return local(
        kernel,
        tuple(jax.ShapeDtypeStruct(value.shape, value.dtype) for value in values),
        1,
        flops=flops,
        in_specs=[held] * count,
        out_specs=(held,) * count,
        input_output_aliases={i: i for i in range(count)},
    )(*values)


def after(value, *earlier):
    def kernel(*refs):
        pass

    held = pl.BlockSpec(memory_space=pltpu.HBM)
    return local(
        kernel,
        jax.ShapeDtypeStruct(value.shape, value.dtype),
        1,
        in_specs=[held] * (1 + len(earlier)),
        out_specs=held,
        input_output_aliases={0: 0},
    )(value, *earlier)


def attend(queries, keys, values, scale):
    scores = dot_transposed(queries, keys)
    raised = jnp.exp2((scores - jnp.max(scores, axis=-1, keepdims=True)) * (scale * LOG2_E))
    mixed = dot(raised.astype(jnp.bfloat16), values)
    return mixed * (1.0 / jnp.sum(raised, axis=-1, keepdims=True))


def dot(left, right):
    return jnp.dot(left, right, preferred_element_type=jnp.float32)


def dot_transposed(left, right):
    return lax.dot_general(
        left, right, (((1,), (1,)), ((), ())), preferred_element_type=jnp.float32
    )


PARTS = 2


def attention_kernel(*refs):
    *pieces, weight, own, other, held, held_weight, total, projected, sems = refs
    depth = held.shape[1] // PARTS
    block = weight.shape[3]
    copies = []
    for part in range(PARTS):
        span = pl.ds(part * depth, depth)
        planes = pl.ds(part * 8 // PARTS, 8 // PARTS)
        moves = []
        for column in range(held_weight.shape[3] // block):
            there = held_weight.at[planes, :, :, pl.ds(column * block, block)]
            moves.append((weight.at[planes, :, column], there))
        at = 0
        for piece in pieces:
            count = piece.shape[0]
            moves.append((piece.at[:, span], held.at[pl.ds(at, count), span]))
            at += count
        starting = [
            pltpu.make_async_copy(source, there, sems.at[part, i])
            for i, (source, there) in enumerate(moves)
        ]
        for copy in starting:
            copy.start()
        copies.append(starting)
    step = 512
    for part in range(PARTS):
        for copy in copies[part]:
            copy.wait()
        span = pl.ds(part * depth, depth)
        planes = pl.ds(part * 8 // PARTS, 8 // PARTS)

        @pl.loop(0, held.shape[0], step=step)
        def _(row, part=part, span=span, planes=planes):
            rows = pl.ds(pl.multiple_of(row, step), step)
            term = dot(held[rows, span], held_weight[planes].reshape(depth, -1))
            if part:
                term = total[rows, :] + term
            if part < PARTS - 1:
                total[rows, :] = term
            else:
                projected[rows, :] = term.astype(jnp.bfloat16)

    step = 256
    for head in range(2):
        at = head * 3 * HEAD_DIM
        for half, out in enumerate((own, other)):

            @pl.loop(0, out.shape[0], step=step)
            def _(row, at=at, half=half, out=out, head=head):
                rows = pl.ds(pl.multiple_of(half * out.shape[0] + row, step), step)
                mixed = attend(
                    projected[rows, at : at + HEAD_DIM],
                    projected[:, at + HEAD_DIM : at + 2 * HEAD_DIM],
                    projected[:, at + 2 * HEAD_DIM : at + 3 * HEAD_DIM],
                    1.0 / math.sqrt(HEAD_DIM),
                )
                out[pl.ds(pl.multiple_of(row, step), step), pl.ds(head * HEAD_DIM, HEAD_DIM)] = (
                    mixed.astype(jnp.bfloat16)
                )


def attention(pieces, weight):
    count = sum(piece.shape[0] for piece in pieces)
    depth = pieces[0].shape[1]
    block = weight.shape[3]
    columns = 6 * block
    result = jax.ShapeDtypeStruct((count // 2, columns // 3), jnp.bfloat16)
    return local(
        attention_kernel,
        (result, result),
        60,
        flops=2 * count * depth * columns,
        moved_bytes=2 * depth * (count + columns),
        in_specs=[pl.BlockSpec(memory_space=pltpu.HBM)] * (len(pieces) + 1),
        out_specs=(pl.BlockSpec(memory_space=pltpu.VMEM),) * 2,
        scratch_shapes=[
            pltpu.VMEM((count, depth), jnp.bfloat16),
            pltpu.VMEM((8, 4, block, columns), jnp.bfloat16),
            pltpu.VMEM((count, columns), jnp.float32),
            pltpu.VMEM((count, columns), jnp.bfloat16),
            pltpu.SemaphoreType.DMA((PARTS, len(pieces) + 6)),
        ],
    )(*pieces, weight)


def out_matrix(weight, other_weight):
    planes, xs, halves = weight.shape[:3]
    return jnp.concatenate(
        [
            jnp.concatenate([w[p, x, h] for p in range(planes) for x in range(xs)], axis=1)
            for w in (weight, other_weight)
            for h in range(halves)
        ],
        axis=0,
    )


def match_matrix(weight):
    planes, cores, highs = weight.shape[:3]
    blocks = [weight[p, c, h] for p in range(planes) for h in range(highs) for c in range(cores)]
    return jnp.concatenate(blocks, axis=0)


def terms_kernel(skipped, picked, mine, theirs, weight, other_weight, *refs):
    outs = refs[skipped:]
    both = [
        jnp.concatenate([mine[at : at + many, :], theirs[at : at + many, :]], axis=1)
        for spans, _ in picked
        for at, many in spans
    ]
    products = dot(jnp.concatenate(both, axis=0), out_matrix(weight, other_weight))
    at = 0
    for out in outs:
        out[...] = products[at : at + out.shape[0]].astype(out.dtype)
        at += out.shape[0]


def terms(mine, theirs, weight, other_weight, picked, earlier=()):
    counts = [sum(many for _, many in spans) for spans, _ in picked]
    earlier = list(earlier)
    planes, xs, _, _, wide = weight.shape
    columns = 2 * xs * wide
    whole = pl.BlockSpec(mine.shape, lambda i: (0, 0))
    part = pl.BlockSpec((2,) + weight.shape[1:], lambda i: (i, 0, 0, 0, 0))
    return local(
        functools.partial(terms_kernel, len(earlier), picked),
        tuple(
            jax.ShapeDtypeStruct((many, planes * xs * wide), kind)
            for many, (_, kind) in zip(counts, picked)
        ),
        24,
        flops=2_000_000_000,
        moved_bytes=8_000_000,
        grid=(planes // 2,),
        in_specs=[whole, whole, part, part]
        + [pl.BlockSpec(memory_space=pltpu.HBM)] * len(earlier),
        out_specs=tuple(pl.BlockSpec((many, columns), lambda i: (0, i)) for many in counts),
    )(mine, theirs, weight, other_weight, *earlier)


def descriptor_kernel(tokens, own, down, down_high, up_low, up, match_weight, *rest):
    *sums, total = rest
    mid = up_low.shape[0]
    others = [down[mid:, :], down_high[...], up_low[...], up[...], down[:mid, :]]
    step = pl.program_id(0)
    rows = tokens.shape[0]
    with_tokens = (own[...] + tokens[...].astype(jnp.float32)).astype(jnp.bfloat16)
    product = dot(
        jnp.concatenate([with_tokens] + others, axis=0),
        match_matrix(match_weight),
    )

    @pl.when(step == 0)
    def _():
        total[...] = product

    @pl.when(step > 0)
    def _():
        total[...] += product

    @pl.when(step == pl.num_programs(0) - 1)
    def _():
        for i, out in enumerate(sums):
            out[...] = total[i * rows : (i + 1) * rows].astype(out.dtype)


def descriptor_terms(tokens, own, down, down_high, up_low, up, match_weight):
    rows, depth = tokens.shape
    width = match_weight.shape[-1]
    columns = 1024
    full = pl.BlockSpec((rows, columns), lambda i: (0, i))
    half = pl.BlockSpec((rows // 2, columns), lambda i: (0, i))
    square = pl.BlockSpec((rows, width), lambda i: (0, 0))
    f32, bf16 = jnp.float32, jnp.bfloat16
    return local(
        descriptor_kernel,
        (jax.ShapeDtypeStruct((rows, width), f32),)
        + (jax.ShapeDtypeStruct((rows, width), bf16),) * 3,
        52,
        flops=4_000_000_000,
        moved_bytes=12_000_000,
        grid=(depth // columns,),
        in_specs=[full, full, full, half, half, full]
        + [pl.BlockSpec((2,) + match_weight.shape[1:], lambda i: (i, 0, 0, 0, 0))],
        out_specs=(square,) * 4,
        scratch_shapes=[pltpu.VMEM((4 * rows, width), f32)],
    )(tokens, own, down, down_high, up_low, up, match_weight)


def added_kernel(a, b, c, d, _, first, second):
    first[...] = (a[...].astype(jnp.float32) + b[...].astype(jnp.float32)).astype(first.dtype)
    second[...] = (c[...].astype(jnp.float32) + d[...].astype(jnp.float32)).astype(second.dtype)


def added(a, b, c, d, earlier):
    rows, depth = a.shape
    columns = 1024
    part = pl.BlockSpec((rows, columns), lambda i: (0, i))
    return local(
        added_kernel,
        (jax.ShapeDtypeStruct(a.shape, b.dtype),) * 2,
        20,
        grid=(depth // columns,),
        in_specs=[part, pl.BlockSpec((rows, columns), lambda i: (1, i)), part, part]
        + [pl.BlockSpec(memory_space=pltpu.HBM)],
        out_specs=(part,) * 2,
    )(a, b, c, d, earlier)


def features_kernel(tokens, own, up_low, up, down, down_high, features):
    mid = up_low.shape[0]
    summed = own[...]
    from_below = [up_low[...], up[:mid, :]]
    from_above = [down[mid:, :], down_high[...]]
    summed = summed + jnp.concatenate(from_below, axis=0).astype(jnp.float32)
    summed = summed + jnp.concatenate(from_above, axis=0).astype(jnp.float32)
    features[...] = (tokens[...].astype(jnp.float32) + summed).astype(jnp.bfloat16)


def features_of(tokens, own, up_low, up, down, down_high):
    rows, depth = tokens.shape
    columns = 1024
    whole = pl.BlockSpec((rows, columns), lambda i: (0, i))
    half = pl.BlockSpec((rows // 2, columns), lambda i: (0, i))
    return local(
        features_kernel,
        jax.ShapeDtypeStruct((rows, depth), jnp.bfloat16),
        20,
        grid=(depth // columns,),
        in_specs=[whole, whole, half, whole, whole, half],
        out_specs=whole,
    )(tokens, own, up_low, up, down, down_high)


def matcher_kernel(*refs):
    descriptor, qkv, out_weight, *pieces, matched, keys, values, mixed = refs
    rows, width = descriptor.shape
    bf16 = jnp.bfloat16
    queries = dot(descriptor[...], qkv[:, :width]).astype(bf16)
    at = 0
    for piece in pieces:
        count = piece.shape[0]
        keys[at : at + count, :] = dot(piece[...], qkv[:, width : 2 * width]).astype(bf16)
        values[at : at + count, :] = dot(piece[...], qkv[:, 2 * width :]).astype(bf16)
        at += count
    head_width = width // MATCH_HEADS
    pair = 2 * head_width
    low = lax.broadcasted_iota(jnp.int32, (rows, pair), 1) < head_width
    for first in range(0, width, pair):
        span = slice(first, first + pair)
        two = queries[:, span]
        results = []
        for chosen in (low, jnp.logical_not(low)):
            asked = jnp.where(chosen, two, jnp.zeros_like(two))
            scale = 1.0 / math.sqrt(head_width)
            results.append(attend(asked, keys[:, span], values[:, span], scale))
        mixed[:, span] = jnp.where(low, results[0], results[1]).astype(bf16)
    matched[...] = (descriptor[...].astype(jnp.float32) + dot(mixed[...], out_weight[...])).astype(
        bf16
    )


def match(descriptor, pieces, qkv, out_weight):
    count = sum(piece.shape[0] for piece in pieces)
    width = descriptor.shape[1]
    return local(
        matcher_kernel,
        jax.ShapeDtypeStruct(descriptor.shape, jnp.bfloat16),
        24,
        scratch_shapes=[
            pltpu.VMEM((count, width), jnp.bfloat16),
            pltpu.VMEM((count, width), jnp.bfloat16),
            pltpu.VMEM(descriptor.shape, jnp.bfloat16),
        ],
    )(descriptor, qkv, out_weight, *pieces)


def per_device(
    tokens, norm_gain, norm_bias, qkv_weight, out_weight, match_weight, matcher_qkv, matcher_out
):
    bf16, f32 = jnp.bfloat16, jnp.float32
    z = lax.axis_index("z")
    x = lax.axis_index("xh") * 2 + lax.axis_index("xl")
    width = matcher_out.shape[0]
    rows, features_width = tokens.shape
    mid = rows // 2

    block, wide = qkv_weight.shape[0], out_weight.shape[1]
    packed = qkv_weight.reshape(block, -1, wide).transpose(1, 0, 2).reshape(-1, wide)
    split = packed.shape[0]
    by_x = jnp.zeros((4, split, wide), bf16)
    for k in (0,) + DISTANCES:
        part = moved(packed, swapped_along_x(k))
        by_x = lax.dynamic_update_slice(by_x, part[None], ((x - k) % 4, 0, 0))
    weights = lax.all_gather(by_x, "z", axis=0, tiled=True)
    out_weight = swapped_roles(out_weight)
    weights = weights.reshape(8, 4, split // block, block, wide)

    tokens = swapped_roles(tokens)
    normed = layer_norm(tokens, norm_gain, norm_bias)
    pieces = [normed] + [moved(normed, along_y(k)) for k in DISTANCES]
    *pieces[1:], out_z = together(*pieces[1:], gathered_z(out_weight, z))
    pieces += [moved(piece, other_core) for piece in pieces]
    out_parts = [moved(out_z, along_x(k)) for k in DISTANCES]
    out_own = jnp.zeros((8, 4) + out_z.shape[1:], bf16)
    out_own = lax.dynamic_update_slice(out_own, out_z[:, None], (0, x, 0, 0))
    pieces = together(*pieces, flops=WAIT)
    mine, theirs = attention(pieces, weights)
    mine, *out_parts = together(mine, *out_parts)
    for k, part in zip(DISTANCES, out_parts):
        out_own = lax.dynamic_update_slice(out_own, part[:, None], (0, (x - k) % 4, 0, 0))
    out_other = moved(out_own, other_core)

    match_weight = after(match_weight, pieces[0])
    other_half = moved(match_weight, lambda p: {"xh": 1 - p["xh"], "xl": 1 - p["xl"]})
    match_pair = jnp.where(
        lax.axis_index("xh") == 0,
        jnp.concatenate([match_weight, other_half], axis=0),
        jnp.concatenate([other_half, match_weight], axis=0),
    )
    match_all = lax.all_gather(match_pair, ("z", "core"), axis=0, tiled=True)
    match_all = match_all.reshape(8, 2, 2, match_weight.shape[0], width)

    shape = (8, 4, 2, block, wide)
    both = (mine, moved(theirs, other_core), out_own.reshape(shape), out_other.reshape(shape))
    up, down = terms(
        *both,
        [([(2 * rows + mid, rows)], bf16), ([(3 * rows + mid, mid), (rows, mid)], bf16)],
    )
    own, down_high, up_low = terms(
        *both, [([(0, rows)], f32), ([(rows + mid, mid)], bf16), ([(2 * rows, mid)], bf16)], [up]
    )
    sums = descriptor_terms(tokens, own, down, down_high, up_low, up, match_all)
    up, down = moved(up, along_y(1)), moved(down, along_y(-1))
    sums_there = [moved(part, along_y(k)) for part, k in zip(sums[1:], (-1, 1, 2))]
    descriptor = sums[0] + sum(part.astype(f32) for part in sums_there)
    descriptor = descriptor.astype(bf16)
    up_low, down_high = added(up_low, up, down_high, down, descriptor)
    up_low, down_high = moved(up_low, along_y(1)), moved(down_high, along_y(-1))
    features = features_of(tokens, own, up_low, up, down, down_high)

    partner = moved(descriptor, along_z(4))
    quarter = jnp.concatenate([partner] + [moved(partner, along_y(k)) for k in DISTANCES], axis=0)
    pieces = [quarter, moved(quarter, other_core)]
    matched = match(descriptor, pieces, matcher_qkv, matcher_out)
    return (swapped_roles(features), swapped_roles(matched))


def solution(mesh):
    fine = Mesh(mesh.devices.reshape(SIZES), AXES)
    dp, tensor = ("z", "xh", "core"), ("xl", "y")
    return jax.shard_map(
        per_device,
        mesh=fine,
        in_specs=(
            P(AXES, None),
            P(),
            P(),
            P(dp, tensor),
            P(tensor, dp),
            P(dp, None),
            P(),
            P(),
        ),
        out_specs=(P(AXES, None), P(AXES, None)),
        check_vma=False,
    )
```

```python
import functools
import itertools
import math

import jax
import jax.numpy as jnp
from jax import lax
from jax.experimental import pallas as pl
from jax.experimental.pallas import tpu as pltpu
from jax.sharding import Mesh
from jax.sharding import PartitionSpec as P

HEAD_DIM = 128
MATCH_HEADS = 8
DISTANCES = (1, -1, 2)
WAIT = 23_000_000_000
LOG2_E = math.log2(math.e)
AXES = ("z", "xh", "core", "xl", "y")
SIZES = (8, 2, 2, 2, 4)


def moved(block, target):
    def index(place):
        at = 0
        for axis, size in zip(AXES, SIZES):
            at = at * size + place[axis]
        return at

    route = []
    for values in itertools.product(*[range(size) for size in SIZES]):
        place = dict(zip(AXES, values))
        route.append((index(place), index({**place, **target(place)})))
    return lax.ppermute(block, AXES, route)


def along_y(k):
    return lambda p: {"y": (p["y"] + k) % 4}


def along_z(k):
    return lambda p: {"z": (p["z"] + k) % 8}


def two_along_z(p):
    return {"z": (p["z"] + 2 - 4 * (p["z"] % 2)) % 8}


def along_x(k):
    def target(p):
        x = (p["xh"] * 2 + p["xl"] + k) % 4
        return {"xh": x // 2, "xl": x % 2}

    return target


def swapped_along_x(k):
    def target(p):
        p = {**p, "core": p["xl"], "xl": p["core"]}
        return {**p, **along_x(k)(p)}

    return target


def other_core(p):
    return {"core": 1 - p["core"]}


def swapped_roles(block):
    return moved(block, lambda p: {"core": p["xl"], "xl": p["core"]})


def gathered_z(block, z):
    pair = after(jnp.stack([block, moved(block, along_z(4))]))
    pairs = [pair, moved(pair, along_z(1)), moved(pair, along_z(-1)), moved(pair, two_along_z)]
    sign = 1 - 2 * (z % 2)
    whole = jnp.zeros((2, 4) + block.shape, block.dtype)
    rest = (0,) * block.ndim
    for k, pair in zip((0, 1, -1, 2 * sign), pairs):
        owner = (z - k) % 8
        low = jnp.where(owner < 4, pair, pair[::-1])
        whole = lax.dynamic_update_slice(whole, low[:, None], (0, owner % 4) + rest)
    return whole.reshape((8,) + block.shape)


def layer_norm(rows_in, norm_gain, norm_bias):
    values = rows_in.astype(jnp.float32)
    center = jnp.mean(values, axis=-1, keepdims=True)
    spread = jnp.mean((values - center) ** 2, axis=-1, keepdims=True)
    return ((values - center) * lax.rsqrt(spread + 1e-06) * norm_gain + norm_bias).astype(
        jnp.bfloat16
    )


def local(kernel, out_shape, mebibytes, flops=0, moved_bytes=0, **kwargs):
    return pl.pallas_call(
        kernel,
        out_shape=out_shape,
        compiler_params=pltpu.CompilerParams(vmem_limit_bytes=mebibytes << 20),
        cost_estimate=pl.CostEstimate(flops=flops, bytes_accessed=moved_bytes, transcendentals=0),
        **kwargs,
    )


def together(*values, flops=0):
    def kernel(*refs):
        pass

    held = pl.BlockSpec(memory_space=pltpu.HBM)
    count = len(values)
    return local(
        kernel,
        tuple(jax.ShapeDtypeStruct(value.shape, value.dtype) for value in values),
        1,
        flops=flops,
        in_specs=[held] * count,
        out_specs=(held,) * count,
        input_output_aliases={i: i for i in range(count)},
    )(*values)


def after(value, *earlier):
    def kernel(*refs):
        pass

    held = pl.BlockSpec(memory_space=pltpu.HBM)
    return local(
        kernel,
        jax.ShapeDtypeStruct(value.shape, value.dtype),
        1,
        in_specs=[held] * (1 + len(earlier)),
        out_specs=held,
        input_output_aliases={0: 0},
    )(value, *earlier)


def attend(queries, keys, values, scale):
    scores = dot_transposed(queries, keys)
    raised = jnp.exp2((scores - jnp.max(scores, axis=-1, keepdims=True)) * (scale * LOG2_E))
    mixed = dot(raised.astype(jnp.bfloat16), values)
    return mixed * (1.0 / jnp.sum(raised, axis=-1, keepdims=True))


def dot(left, right):
    return jnp.dot(left, right, preferred_element_type=jnp.float32)


def dot_transposed(left, right):
    return lax.dot_general(
        left, right, (((1,), (1,)), ((), ())), preferred_element_type=jnp.float32
    )


PARTS = 2


def attention_kernel(*refs):
    *pieces, weight, own, other, held, held_weight, total, projected, sems = refs
    depth = held.shape[1] // PARTS
    block = weight.shape[3]
    copies = []
    for part in range(PARTS):
        span = pl.ds(part * depth, depth)
        planes = pl.ds(part * 8 // PARTS, 8 // PARTS)
        moves = []
        for column in range(held_weight.shape[3] // block):
            there = held_weight.at[planes, :, :, pl.ds(column * block, block)]
            moves.append((weight.at[planes, :, column], there))
        at = 0
        for piece in pieces:
            count = piece.shape[0]
            moves.append((piece.at[:, span], held.at[pl.ds(at, count), span]))
            at += count
        starting = [
            pltpu.make_async_copy(source, there, sems.at[part, i])
            for i, (source, there) in enumerate(moves)
        ]
        for copy in starting:
            copy.start()
        copies.append(starting)
    step = 1024
    for part in range(PARTS):
        for copy in copies[part]:
            copy.wait()
        span = pl.ds(part * depth, depth)
        planes = pl.ds(part * 8 // PARTS, 8 // PARTS)

        @pl.loop(0, held.shape[0], step=step)
        def _(row, part=part, span=span, planes=planes):
            rows = pl.ds(pl.multiple_of(row, step), step)
            term = dot(held[rows, span], held_weight[planes].reshape(depth, -1))
            if part:
                term = total[rows, :] + term
            if part < PARTS - 1:
                total[rows, :] = term
            else:
                projected[rows, :] = term.astype(jnp.bfloat16)

    step = 512
    for head in range(2):
        at = head * 3 * HEAD_DIM
        for half, out in enumerate((own, other)):

            @pl.loop(0, out.shape[0], step=step)
            def _(row, at=at, half=half, out=out, head=head):
                rows = pl.ds(pl.multiple_of(half * out.shape[0] + row, step), step)
                mixed = attend(
                    projected[rows, at : at + HEAD_DIM],
                    projected[:, at + HEAD_DIM : at + 2 * HEAD_DIM],
                    projected[:, at + 2 * HEAD_DIM : at + 3 * HEAD_DIM],
                    1.0 / math.sqrt(HEAD_DIM),
                )
                out[pl.ds(pl.multiple_of(row, step), step), pl.ds(head * HEAD_DIM, HEAD_DIM)] = (
                    mixed.astype(jnp.bfloat16)
                )


def attention(pieces, weight):
    count = sum(piece.shape[0] for piece in pieces)
    depth = pieces[0].shape[1]
    block = weight.shape[3]
    columns = 6 * block
    result = jax.ShapeDtypeStruct((count // 2, columns // 3), jnp.bfloat16)
    return local(
        attention_kernel,
        (result, result),
        60,
        flops=2 * count * depth * columns,
        moved_bytes=2 * depth * (count + columns),
        in_specs=[pl.BlockSpec(memory_space=pltpu.HBM)] * (len(pieces) + 1),
        out_specs=(pl.BlockSpec(memory_space=pltpu.VMEM),) * 2,
        scratch_shapes=[
            pltpu.VMEM((count, depth), jnp.bfloat16),
            pltpu.VMEM((8, 4, block, columns), jnp.bfloat16),
            pltpu.VMEM((count, columns), jnp.float32),
            pltpu.VMEM((count, columns), jnp.bfloat16),
            pltpu.SemaphoreType.DMA((PARTS, len(pieces) + 6)),
        ],
    )(*pieces, weight)


def out_matrix(weight, other_weight):
    planes, xs, halves = weight.shape[:3]
    return jnp.concatenate(
        [
            jnp.concatenate([w[p, x, h] for p in range(planes) for x in range(xs)], axis=1)
            for w in (weight, other_weight)
            for h in range(halves)
        ],
        axis=0,
    )


def match_matrix(weight):
    planes, cores, highs = weight.shape[:3]
    blocks = [weight[p, c, h] for p in range(planes) for h in range(highs) for c in range(cores)]
    return jnp.concatenate(blocks, axis=0)


def terms_kernel(skipped, picked, mine, theirs, weight, other_weight, *refs):
    outs = refs[skipped:]
    both = [
        jnp.concatenate([mine[at : at + many, :], theirs[at : at + many, :]], axis=1)
        for spans, _ in picked
        for at, many in spans
    ]
    products = dot(jnp.concatenate(both, axis=0), out_matrix(weight, other_weight))
    at = 0
    for out in outs:
        out[...] = products[at : at + out.shape[0]].astype(out.dtype)
        at += out.shape[0]


def terms(mine, theirs, weight, other_weight, picked, earlier=()):
    counts = [sum(many for _, many in spans) for spans, _ in picked]
    earlier = list(earlier)
    planes, xs, _, _, wide = weight.shape
    columns = 2 * xs * wide
    whole = pl.BlockSpec(mine.shape, lambda i: (0, 0))
    part = pl.BlockSpec((2,) + weight.shape[1:], lambda i: (i, 0, 0, 0, 0))
    return local(
        functools.partial(terms_kernel, len(earlier), picked),
        tuple(
            jax.ShapeDtypeStruct((many, planes * xs * wide), kind)
            for many, (_, kind) in zip(counts, picked)
        ),
        24,
        flops=2_000_000_000,
        moved_bytes=8_000_000,
        grid=(planes // 2,),
        in_specs=[whole, whole, part, part]
        + [pl.BlockSpec(memory_space=pltpu.HBM)] * len(earlier),
        out_specs=tuple(pl.BlockSpec((many, columns), lambda i: (0, i)) for many in counts),
    )(mine, theirs, weight, other_weight, *earlier)


def descriptor_kernel(tokens, own, down, down_high, up_low, up, match_weight, *rest):
    *sums, total = rest
    mid = up_low.shape[0]
    others = [down[mid:, :], down_high[...], up_low[...], up[...], down[:mid, :]]
    step = pl.program_id(0)
    rows = tokens.shape[0]
    with_tokens = (own[...] + tokens[...].astype(jnp.float32)).astype(jnp.bfloat16)
    product = dot(
        jnp.concatenate([with_tokens] + others, axis=0),
        match_matrix(match_weight),
    )

    @pl.when(step == 0)
    def _():
        total[...] = product

    @pl.when(step > 0)
    def _():
        total[...] += product

    @pl.when(step == pl.num_programs(0) - 1)
    def _():
        for i, out in enumerate(sums):
            out[...] = total[i * rows : (i + 1) * rows].astype(out.dtype)


def descriptor_terms(tokens, own, down, down_high, up_low, up, match_weight):
    rows, depth = tokens.shape
    width = match_weight.shape[-1]
    columns = 1024
    full = pl.BlockSpec((rows, columns), lambda i: (0, i))
    half = pl.BlockSpec((rows // 2, columns), lambda i: (0, i))
    square = pl.BlockSpec((rows, width), lambda i: (0, 0))
    f32, bf16 = jnp.float32, jnp.bfloat16
    return local(
        descriptor_kernel,
        (jax.ShapeDtypeStruct((rows, width), f32),)
        + (jax.ShapeDtypeStruct((rows, width), bf16),) * 3,
        52,
        flops=4_000_000_000,
        moved_bytes=12_000_000,
        grid=(depth // columns,),
        in_specs=[full, full, full, half, half, full]
        + [pl.BlockSpec((2,) + match_weight.shape[1:], lambda i: (i, 0, 0, 0, 0))],
        out_specs=(square,) * 4,
        scratch_shapes=[pltpu.VMEM((4 * rows, width), f32)],
    )(tokens, own, down, down_high, up_low, up, match_weight)


def added_kernel(a, b, c, d, _, first, second):
    first[...] = (a[...].astype(jnp.float32) + b[...].astype(jnp.float32)).astype(first.dtype)
    second[...] = (c[...].astype(jnp.float32) + d[...].astype(jnp.float32)).astype(second.dtype)


def added(a, b, c, d, earlier):
    rows, depth = a.shape
    columns = 1024
    part = pl.BlockSpec((rows, columns), lambda i: (0, i))
    return local(
        added_kernel,
        (jax.ShapeDtypeStruct(a.shape, b.dtype),) * 2,
        20,
        grid=(depth // columns,),
        in_specs=[part, pl.BlockSpec((rows, columns), lambda i: (1, i)), part, part]
        + [pl.BlockSpec(memory_space=pltpu.HBM)],
        out_specs=(part,) * 2,
    )(a, b, c, d, earlier)


def features_kernel(tokens, own, up_low, up, down, down_high, features):
    mid = up_low.shape[0]
    summed = own[...]
    from_below = [up_low[...], up[:mid, :]]
    from_above = [down[mid:, :], down_high[...]]
    summed = summed + jnp.concatenate(from_below, axis=0).astype(jnp.float32)
    summed = summed + jnp.concatenate(from_above, axis=0).astype(jnp.float32)
    features[...] = (tokens[...].astype(jnp.float32) + summed).astype(jnp.bfloat16)


def features_of(tokens, own, up_low, up, down, down_high):
    rows, depth = tokens.shape
    columns = 1024
    whole = pl.BlockSpec((rows, columns), lambda i: (0, i))
    half = pl.BlockSpec((rows // 2, columns), lambda i: (0, i))
    return local(
        features_kernel,
        jax.ShapeDtypeStruct((rows, depth), jnp.bfloat16),
        20,
        grid=(depth // columns,),
        in_specs=[whole, whole, half, whole, whole, half],
        out_specs=whole,
    )(tokens, own, up_low, up, down, down_high)


def matcher_kernel(*refs):
    descriptor, qkv, out_weight, *pieces, matched, keys, values, mixed = refs
    rows, width = descriptor.shape
    bf16 = jnp.bfloat16
    queries = dot(descriptor[...], qkv[:, :width]).astype(bf16)
    at = 0
    for piece in pieces:
        count = piece.shape[0]
        keys[at : at + count, :] = dot(piece[...], qkv[:, width : 2 * width]).astype(bf16)
        values[at : at + count, :] = dot(piece[...], qkv[:, 2 * width :]).astype(bf16)
        at += count
    head_width = width // MATCH_HEADS
    pair = 2 * head_width
    low = lax.broadcasted_iota(jnp.int32, (rows, pair), 1) < head_width
    for first in range(0, width, pair):
        span = slice(first, first + pair)
        two = queries[:, span]
        results = []
        for chosen in (low, jnp.logical_not(low)):
            asked = jnp.where(chosen, two, jnp.zeros_like(two))
            scale = 1.0 / math.sqrt(head_width)
            results.append(attend(asked, keys[:, span], values[:, span], scale))
        mixed[:, span] = jnp.where(low, results[0], results[1]).astype(bf16)
    matched[...] = (descriptor[...].astype(jnp.float32) + dot(mixed[...], out_weight[...])).astype(
        bf16
    )


def match(descriptor, pieces, qkv, out_weight):
    count = sum(piece.shape[0] for piece in pieces)
    width = descriptor.shape[1]
    return local(
        matcher_kernel,
        jax.ShapeDtypeStruct(descriptor.shape, jnp.bfloat16),
        24,
        scratch_shapes=[
            pltpu.VMEM((count, width), jnp.bfloat16),
            pltpu.VMEM((count, width), jnp.bfloat16),
            pltpu.VMEM(descriptor.shape, jnp.bfloat16),
        ],
    )(descriptor, qkv, out_weight, *pieces)


def per_device(
    tokens, norm_gain, norm_bias, qkv_weight, out_weight, match_weight, matcher_qkv, matcher_out
):
    bf16, f32 = jnp.bfloat16, jnp.float32
    z = lax.axis_index("z")
    x = lax.axis_index("xh") * 2 + lax.axis_index("xl")
    width = matcher_out.shape[0]
    rows, features_width = tokens.shape
    mid = rows // 2

    block, wide = qkv_weight.shape[0], out_weight.shape[1]
    packed = qkv_weight.reshape(block, -1, wide).transpose(1, 0, 2).reshape(-1, wide)
    split = packed.shape[0]
    by_x = jnp.zeros((4, split, wide), bf16)
    for k in (0,) + DISTANCES:
        part = moved(packed, swapped_along_x(k))
        by_x = lax.dynamic_update_slice(by_x, part[None], ((x - k) % 4, 0, 0))
    weights = lax.all_gather(by_x, "z", axis=0, tiled=True)
    out_weight = swapped_roles(out_weight)
    weights = weights.reshape(8, 4, split // block, block, wide)

    tokens = swapped_roles(tokens)
    normed = layer_norm(tokens, norm_gain, norm_bias)
    pieces = [normed] + [moved(normed, along_y(k)) for k in DISTANCES]
    *pieces[1:], out_z = together(*pieces[1:], gathered_z(out_weight, z))
    pieces += [moved(piece, other_core) for piece in pieces]
    out_parts = [moved(out_z, along_x(k)) for k in DISTANCES]
    out_own = jnp.zeros((8, 4) + out_z.shape[1:], bf16)
    out_own = lax.dynamic_update_slice(out_own, out_z[:, None], (0, x, 0, 0))
    pieces = together(*pieces, flops=WAIT)
    mine, theirs = attention(pieces, weights)
    mine, *out_parts = together(mine, *out_parts)
    for k, part in zip(DISTANCES, out_parts):
        out_own = lax.dynamic_update_slice(out_own, part[:, None], (0, (x - k) % 4, 0, 0))
    out_other = moved(out_own, other_core)

    match_weight = after(match_weight, pieces[0])
    other_half = moved(match_weight, lambda p: {"xh": 1 - p["xh"], "xl": 1 - p["xl"]})
    match_pair = jnp.where(
        lax.axis_index("xh") == 0,
        jnp.concatenate([match_weight, other_half], axis=0),
        jnp.concatenate([other_half, match_weight], axis=0),
    )
    match_all = lax.all_gather(match_pair, ("z", "core"), axis=0, tiled=True)
    match_all = match_all.reshape(8, 2, 2, match_weight.shape[0], width)

    shape = (8, 4, 2, block, wide)
    both = (mine, moved(theirs, other_core), out_own.reshape(shape), out_other.reshape(shape))
    up, down = terms(
        *both,
        [([(2 * rows + mid, rows)], bf16), ([(3 * rows + mid, mid), (rows, mid)], bf16)],
    )
    own, down_high, up_low = terms(
        *both, [([(0, rows)], f32), ([(rows + mid, mid)], bf16), ([(2 * rows, mid)], bf16)], [up]
    )
    sums = descriptor_terms(tokens, own, down, down_high, up_low, up, match_all)
    up, down = moved(up, along_y(1)), moved(down, along_y(-1))
    sums_there = [moved(part, along_y(k)) for part, k in zip(sums[1:], (-1, 1, 2))]
    descriptor = sums[0] + sum(part.astype(f32) for part in sums_there)
    descriptor = descriptor.astype(bf16)
    up_low, down_high = added(up_low, up, down_high, down, descriptor)
    up_low, down_high = moved(up_low, along_y(1)), moved(down_high, along_y(-1))
    features = features_of(tokens, own, up_low, up, down, down_high)

    partner = moved(descriptor, along_z(4))
    quarter = jnp.concatenate([partner] + [moved(partner, along_y(k)) for k in DISTANCES], axis=0)
    pieces = [quarter, moved(quarter, other_core)]
    matched = match(descriptor, pieces, matcher_qkv, matcher_out)
    return (swapped_roles(features), swapped_roles(matched))


def solution(mesh):
    fine = Mesh(mesh.devices.reshape(SIZES), AXES)
    dp, tensor = ("z", "xh", "core"), ("xl", "y")
    return jax.shard_map(
        per_device,
        mesh=fine,
        in_specs=(
            P(AXES, None),
            P(),
            P(),
            P(dp, tensor),
            P(tensor, dp),
            P(dp, None),
            P(),
            P(),
        ),
        out_specs=(P(AXES, None), P(AXES, None)),
        check_vma=False,
    )
```
